32 devices in a mesh: task: 4 (over x, core), dp: 8 (over z, y).
Axes of the slice: x: 2, y: 2, z: 4, core: 2. Of those that a mesh axis runs over, the one named last changes fastest.
Arguments:
- features: bfloat16 [16, 36, 48, 512], P('dp'), may hold values from -6 to 6
- labels: int32 [16, 36, 48], P('dp'), may hold values from 0 to 12
- depth_mask: int32 [16, 36, 48], P('dp'), may hold values 0 or 1
- depth_target: float32 [16, 36, 48], P('dp'), may hold values from 0.5 to 3
- normal_target: float32 [16, 3, 36, 48], P('dp'), may hold values from -1 to 1
- scene_ids: int32 [16], P('dp'), may hold values from 0 to 26
- task_weights: float32 [27, 4], replicated, may hold values from 0.5 to 2
- conflict: int32 [4, 4], replicated, may hold values 0 or 1
- trunk_copy: bfloat16 [2, 9, 512, 512], P(None, None, 'dp'), may hold values from -0.09375 to 0.09375
- trunk_master: float32 [2, 9, 512, 512], P(None, None, 'dp'), may hold values from -0.09375 to 0.09375
- trunk_left: float32 [2, 9, 512, 512], P(None, None, 'dp')
- trunk_right: float32 [2, 9, 512, 512], P(None, None, 'dp')
- left_root: float32 [2, 9, 512, 512], P(None, None, 'dp')
- right_root: float32 [2, 9, 512, 512], replicated
- head_copy: bfloat16 [4, 2, 512, 256], P('task', None, 'dp'), may hold values from -0.25 to 0.25
- head_master: float32 [4, 2, 512, 256], P('task', None, 'dp'), may hold values from -0.25 to 0.25
- head_first: float32 [4, 2, 512, 256], P('task', None, 'dp'), may hold values from -0.09375 to 0.09375
- head_second: float32 [4, 2, 512, 256], P('task', None, 'dp'), may hold values from 3.616898e-05 to 0.00014467593
- out_copy: bfloat16 [256, 18], replicated, may hold values from -0.375 to 0.375
- out_master: float32 [256, 18], replicated, may hold values from -0.375 to 0.375
- out_first: float32 [256, 18], replicated, may hold values from -0.09375 to 0.09375
- out_second: float32 [256, 18], replicated, may hold values from 3.616898e-05 to 0.00014467593
- trunk_gains: float32 [4, 512], replicated, may hold values from 0.5 to 1.5
- gains_first: float32 [4, 512], replicated, may hold values from -0.09375 to 0.09375
- gains_second: float32 [4, 512], replicated, may hold values from 3.616898e-05 to 0.00014467593
- head_bias: float32 [4, 256], replicated, may hold values from -3 to 3
- bias_first: float32 [4, 256], replicated, may hold values from -0.09375 to 0.09375
- bias_second: float32 [4, 256], replicated, may hold values from 3.616898e-05 to 0.00014467593
Outputs:
- trunk_grad: float32 [2, 9, 512, 512], P(None, None, 'dp')
- left_new: float32 [2, 9, 512, 512], P(None, None, 'dp')
- right_new: float32 [2, 9, 512, 512], P(None, None, 'dp')
- trunk_master_new: float32 [2, 9, 512, 512], P(None, None, 'dp')
- trunk_copy_new: bfloat16 [2, 9, 512, 512], P(None, None, 'dp')
- head_first_new: float32 [4, 2, 512, 256], P('task', None, 'dp')
- head_second_new: float32 [4, 2, 512, 256], P('task', None, 'dp')
- head_master_new: float32 [4, 2, 512, 256], P('task', None, 'dp')
- head_copy_new: bfloat16 [4, 2, 512, 256], P('task', None, 'dp')
- out_first_new: float32 [256, 18], replicated
- out_second_new: float32 [256, 18], replicated
- out_master_new: float32 [256, 18], replicated
- out_copy_new: bfloat16 [256, 18], replicated
- gains_first_new: float32 [4, 512], replicated
- gains_second_new: float32 [4, 512], replicated
- trunk_gains_new: float32 [4, 512], replicated
- bias_first_new: float32 [4, 256], replicated
- bias_second_new: float32 [4, 256], replicated
- head_bias_new: float32 [4, 256], replicated
- loss_terms: float32 [5], replicated
- pair_products: float32 [4, 4], replicated
The draws below stay inside these ranges and needn't reach their ends.
All inputs are finite; a program needn't handle non-finite values. No bound on the sum of `depth_mask` on one device may be relied on, other than what follows from the above.
Results may differ from the reference program's by a relative error of at most 0.0055.
Values may be sent and summed in bfloat16 or wider, within the bound.
A program may use at most 320 MiB of HBM per device.

```python
import math
import jax
import jax.numpy as jnp
from jax import lax

CHANNELS = 512
BRANCH_WIDTH = 256
CLASSES = 13
TASKS = 4
SCENES = 27
MAP_HEIGHT = 36
MAP_WIDTH = 48
DILATION_STEP = 2
STEP = 5
BATCH = 16


def symmetric(key, diagonal, off_level):
    full_shape = (2, 9, CHANNELS, CHANNELS)
    noise = jax.random.uniform(key, full_shape, jnp.float32, -1.0, 1.0) * (1.7320508 * off_level)
    mirrored = 0.5 * (noise + jnp.swapaxes(noise, 2, 3))
    identity = jnp.arange(CHANNELS)[:, None] == jnp.arange(CHANNELS)[None, :]
    return jnp.where(identity, diagonal[..., None], mirrored)


def statistic(key):
    level = CHANNELS / (BATCH * MAP_HEIGHT * MAP_WIDTH)
    key_diag, key_off = jax.random.split(key)
    diagonal = level * jnp.exp(jax.random.uniform(key_diag, (2, 9, CHANNELS), jnp.float32, 0.0, 1.3862944))
    return symmetric(key_off, diagonal, level / CHANNELS ** 0.5)


def inverse_root(key):
    level = (CHANNELS / (BATCH * MAP_HEIGHT * MAP_WIDTH)) ** (-0.25)
    key_diag, key_off = jax.random.split(key)
    diagonal = level * jax.random.uniform(key_diag, (2, 9, CHANNELS), jnp.float32, 0.7, 1.4)
    return symmetric(key_off, diagonal, 0.3 * level / CHANNELS ** 0.5)


def draw_trunk_left(key, part):
    key = jax.random.fold_in(key, 11)
    return statistic(key)


def draw_trunk_right(key, part):
    key = jax.random.fold_in(key, 12)
    return statistic(key)


def draw_left_root(key, part):
    key = jax.random.fold_in(key, 13)
    return inverse_root(key)


def draw_right_root(key, part):
    key = jax.random.fold_in(key, 14)
    return inverse_root(key)


def draw_labels(key, part):
    key = jax.random.fold_in(key, 15)
    coarse = jax.random.randint(key, (BATCH, MAP_HEIGHT // 4, MAP_WIDTH // 4), 0, CLASSES)
    return jnp.repeat(jnp.repeat(coarse, 4, axis=1), 4, axis=2).astype(jnp.int32)


def plant(drawn, rng, smallest, top_value):
    extent = drawn.shape
    place = [jax.random.randint(jax.random.fold_in(rng, axis), (), 0, extent[axis]) for axis in range(len(extent))]
    drawn = drawn.at[tuple(place)].set(smallest)
    longest = extent.index(max(extent))
    place[longest] = (place[longest] + 1) % extent[longest]
    return drawn.at[tuple(place)].set(top_value)


def block_levels(key, shape, cuts, smallest, high):
    def one(axis_at, shards_of):
        draws = jax.random.uniform(jax.random.fold_in(jax.random.fold_in(key, 6), axis_at), (shards_of,), jnp.float32, smallest / len(cuts), high / len(cuts))
        return jnp.repeat(jnp.exp(draws), shape[axis_at] // shards_of).reshape((-1,) + (1,) * (len(shape) - axis_at - 1))

    level = one(*cuts[0])
    for cut in cuts[1:]:
        level = level * one(*cut)
    return level


def normal_values(key, extent, deviation, most, pieces=(), kind=jnp.bfloat16):
    level = block_levels(key, extent, pieces, -0.22, 0.18) if pieces else 1.0
    values = jax.random.normal(key, extent, jnp.float32) * deviation * level
    return jnp.minimum(jnp.maximum(values, -most), most).astype(kind)


def setup_inputs(seed: int = 0) -> dict:
    seeds = jax.random.split(jax.random.key(seed), 29)
    return {
        "features": normal_values(seeds[0], (BATCH, MAP_HEIGHT, MAP_WIDTH, CHANNELS), 1.0, 6.0, ((0, 8),)),
        "labels": draw_labels(jax.random.fold_in(seeds[28], 71), 0),
        "depth_mask": plant((jax.random.randint(seeds[2], (BATCH, MAP_HEIGHT, MAP_WIDTH), 0, 10) < 7).astype(jnp.int32), jax.random.fold_in(seeds[2], 1), 0, 1),
        "depth_target": jnp.clip(0.5 + 2.5 * jax.random.uniform(seeds[3], (BATCH, MAP_HEIGHT, MAP_WIDTH), jnp.float32) ** block_levels(seeds[3], (BATCH, MAP_HEIGHT, MAP_WIDTH), ((0, 8),), -0.2, 0.2), 0.5, 3.0),
        "normal_target": jnp.clip(jax.random.uniform(seeds[4], (BATCH, 3, MAP_HEIGHT, MAP_WIDTH), jnp.float32, -1.0, 1.0) * block_levels(seeds[4], (BATCH, 3, MAP_HEIGHT, MAP_WIDTH), ((0, 8),), -0.4, 0.0), -1.0, 1.0),
        "scene_ids": plant(jax.random.randint(seeds[5], (BATCH,), 0, SCENES), jax.random.fold_in(seeds[5], 1), 0, SCENES - 1).astype(jnp.int32),
        "task_weights": jnp.clip(jnp.exp(jax.random.uniform(seeds[6], (SCENES, TASKS), jnp.float32, math.log(0.5), math.log(2.0))), 0.5, 2.0),
        "conflict": plant((jax.random.randint(seeds[7], (TASKS, TASKS), 0, 2) < 1).astype(jnp.int32), jax.random.fold_in(seeds[7], 1), 0, 1),
        "trunk_copy": normal_values(seeds[8], (2, 9, CHANNELS, CHANNELS), (9 * CHANNELS) ** -0.5, 0.09375, ((2, 8),)),
        "trunk_master": normal_values(seeds[9], (2, 9, CHANNELS, CHANNELS), (9 * CHANNELS) ** -0.5, 0.09375, ((2, 8),), jnp.float32),
        "trunk_left": draw_trunk_left(jax.random.fold_in(seeds[28], 71), 0),
        "trunk_right": draw_trunk_right(jax.random.fold_in(seeds[28], 71), 0),
        "left_root": draw_left_root(jax.random.fold_in(seeds[28], 71), 0),
        "right_root": draw_right_root(jax.random.fold_in(seeds[28], 71), 0),
        "head_copy": normal_values(seeds[14], (TASKS, 2, CHANNELS, BRANCH_WIDTH), CHANNELS ** -0.5, 0.25, ((0, 4), (2, 8))),
        "head_master": normal_values(seeds[15], (TASKS, 2, CHANNELS, BRANCH_WIDTH), CHANNELS ** -0.5, 0.25, ((0, 4), (2, 8)), jnp.float32),
        "head_first": normal_values(seeds[16], (TASKS, 2, CHANNELS, BRANCH_WIDTH), ((BATCH * MAP_HEIGHT * MAP_WIDTH) ** -0.5), 0.09375, ((0, 4), (2, 8)), jnp.float32),
        "head_second": jnp.clip(jnp.exp(math.log(0.00014467593) - 1.3862944 * jax.random.uniform(seeds[17], (TASKS, 2, CHANNELS, BRANCH_WIDTH), jnp.float32) ** block_levels(seeds[17], (TASKS, 2, CHANNELS, BRANCH_WIDTH), ((0, 4), (2, 8)), -0.2, 0.2)), 3.616898175096139e-05, 0.00014467593),
        "out_copy": normal_values(seeds[18], (BRANCH_WIDTH, CLASSES + 5), BRANCH_WIDTH ** -0.5, 0.375),
        "out_master": normal_values(seeds[19], (BRANCH_WIDTH, CLASSES + 5), BRANCH_WIDTH ** -0.5, 0.375, (), jnp.float32),
        "out_first": normal_values(seeds[20], (BRANCH_WIDTH, CLASSES + 5), ((BATCH * MAP_HEIGHT * MAP_WIDTH) ** -0.5), 0.09375, (), jnp.float32),
        "out_second": jnp.clip(jnp.exp(jax.random.uniform(seeds[21], (BRANCH_WIDTH, CLASSES + 5), jnp.float32, math.log(3.616898175096139e-05), math.log(0.00014467593))), 3.616898175096139e-05, 0.00014467593),
        "trunk_gains": jnp.clip(jax.random.uniform(seeds[22], (4, CHANNELS), jnp.float32, 0.5, 1.5), 0.5, 1.5),
        "gains_first": normal_values(seeds[23], (4, CHANNELS), ((BATCH * MAP_HEIGHT * MAP_WIDTH) ** -0.5), 0.09375, (), jnp.float32),
        "gains_second": jnp.clip(jnp.exp(jax.random.uniform(seeds[24], (4, CHANNELS), jnp.float32, math.log(3.616898175096139e-05), math.log(0.00014467593))), 3.616898175096139e-05, 0.00014467593),
        "head_bias": normal_values(seeds[25], (TASKS, BRANCH_WIDTH), 0.5, 3.0, (), jnp.float32),
        "bias_first": normal_values(seeds[26], (TASKS, BRANCH_WIDTH), ((BATCH * MAP_HEIGHT * MAP_WIDTH) ** -0.5), 0.09375, (), jnp.float32),
        "bias_second": jnp.clip(jnp.exp(jax.random.uniform(seeds[27], (TASKS, BRANCH_WIDTH), jnp.float32, math.log(3.616898175096139e-05), math.log(0.00014467593))), 3.616898175096139e-05, 0.00014467593),
    }


@jax.custom_vjp
def low(v):
    return lax.optimization_barrier(v.astype(jnp.bfloat16)).astype(jnp.float32)

@jax.custom_vjp
def low_back(v):
    return v

def low_keep(v):
    return (low(v), None)

def low_pass(kept, grad):
    return (grad,)

def back_keep(v):
    return (v, None)

def back_low(kept, grad):
    return (low(grad),)
low.defvjp(low_keep, low_pass)
low_back.defvjp(back_keep, back_low)
PRECISE = lax.Precision.HIGHEST
NORM_EPS = 1e-05
RATE_TRUNK = 0.3
RATE_MATRIX = 0.05
RATE_VECTOR = 0.3
WEIGHT_DECAY = 0.01
ADAM_EPS = 1e-08
GRAM_EPS = 1e-12

def conv_taps(tap_values, weights):
    padded_input = jnp.pad(tap_values, ((0, 0), (DILATION_STEP, DILATION_STEP), (DILATION_STEP, DILATION_STEP), (0, 0)))
    result = jnp.zeros(tap_values.shape[:3] + (weights.shape[2],), jnp.float32)
    for tap_index in range(9):
        kernel_row, kernel_column = divmod(tap_index, 3)
        shifted_window = padded_input[:, DILATION_STEP * kernel_row:DILATION_STEP * kernel_row + MAP_HEIGHT, DILATION_STEP * kernel_column:DILATION_STEP * kernel_column + MAP_WIDTH, :]
        result = result + jnp.einsum('bhwi,io->bhwo', shifted_window, weights[tap_index], precision=PRECISE)
    return result

def batch_norm(conv_out, gain, shift):
    center = lax.optimization_barrier(jnp.mean(conv_out, axis=(0, 1, 2)))
    spread = lax.optimization_barrier(jnp.mean(conv_out * conv_out, axis=(0, 1, 2))) - center * center
    return gain * ((conv_out - center) * lax.rsqrt(spread + NORM_EPS)) + shift

def boundary(labels):
    across = jnp.pad((labels[:, :, 1:] != labels[:, :, :-1]).astype(jnp.float32), ((0, 0), (0, 0), (0, 1)))
    downward = jnp.pad((labels[:, 1:, :] != labels[:, :-1, :]).astype(jnp.float32), ((0, 0), (0, 1), (0, 0)))
    return jnp.maximum(across, downward)

def pixel_data(labels, depth_mask, depth_target, normal_target, scene_ids, task_weights):
    images, feature_rows, feature_columns = labels.shape
    choose = (scene_ids[:, None] == jnp.arange(task_weights.shape[0])[None, :]).astype(jnp.float32)
    per_image = jnp.dot(choose, task_weights, precision=PRECISE)
    return (labels.reshape(-1), depth_mask.reshape(-1).astype(jnp.float32), boundary(labels).reshape(-1), depth_target.reshape(-1), jnp.transpose(normal_target, (0, 2, 3, 1)).reshape(-1, 3), jnp.repeat(per_image, feature_rows * feature_columns, axis=0))

def task_sums(logits, pixel_info):
    labels, valid_mask, edge_target, depth_values, normals, weights = pixel_info
    classes = logits[:, :CLASSES]
    largest = lax.optimization_barrier(jnp.max(classes, axis=1, keepdims=True))
    spread = jnp.log(lax.optimization_barrier(jnp.sum(jnp.exp(classes - largest), axis=1))) + largest[:, 0]
    picked = lax.optimization_barrier(jnp.sum(jnp.where(labels[:, None] == jnp.arange(CLASSES)[None, :], classes, 0.0), axis=1))
    segment = jnp.sum(weights[:, 0] * (spread - picked))
    offset = logits[:, CLASSES] - depth_values
    distance = jnp.sum(weights[:, 1] * valid_mask * (jnp.sqrt(offset * offset + 1.0) - 1.0))
    predicted = logits[:, CLASSES + 1:CLASSES + 4]
    cosine = lax.optimization_barrier(jnp.sum(predicted * normals, axis=1)) * lax.rsqrt((lax.optimization_barrier(jnp.sum(predicted * predicted, axis=1)) + 1.0) * (lax.optimization_barrier(jnp.sum(normals * normals, axis=1)) + 1.0))
    surface = jnp.sum(weights[:, 2] * (1.0 - cosine))
    edge_logit = logits[:, CLASSES + 4]
    contour = jnp.sum(weights[:, 3] * (jax.nn.softplus(edge_logit) - edge_target * edge_logit))
    return jnp.stack([segment, distance, surface, contour])

def combine_weights(pair_products, conflict):
    offdiagonal = (1.0 - jnp.eye(TASKS, dtype=jnp.float32)) * conflict.astype(jnp.float32)
    ratios = offdiagonal * pair_products / (jnp.diagonal(pair_products)[None, :] + GRAM_EPS)
    return 1.0 - lax.optimization_barrier(jnp.sum(ratios, axis=0))

def adamw_update(gradient, moment_one, moment_two, weight, rate):
    moment_one = 0.5 * moment_one + 0.5 * gradient
    moment_two = 0.5 * moment_two + 0.5 * gradient * gradient
    correction = 1.0 - 0.5 ** STEP
    weight = weight - rate * (moment_one / correction / (jnp.sqrt(moment_two / correction) + ADAM_EPS) + WEIGHT_DECAY * weight)
    return (moment_one, moment_two, weight)

def forward(params, inputs, pixel_info):
    trunk_mats, vectors, head_mats, head_bias, out_weight = params
    first_conv = low_back(conv_taps(inputs, trunk_mats[0]))
    first_act = low(jax.nn.silu(batch_norm(first_conv, vectors[0], vectors[1])))
    second_conv = low_back(conv_taps(first_act, trunk_mats[1]))
    second_norm = batch_norm(second_conv, vectors[2], vectors[3])
    trunk_out = low(jax.nn.silu(second_norm + inputs))
    pooled = low(lax.optimization_barrier(jnp.mean(trunk_out, axis=(1, 2))))
    totals = []
    for task_index in range(TASKS):
        head_pre = jnp.einsum('bhwc,cd->bhwd', trunk_out, head_mats[task_index, 0], precision=PRECISE)
        head_pre = head_pre + jnp.dot(pooled, head_mats[task_index, 1], precision=PRECISE)[:, None, None, :] + head_bias[task_index]
        hidden = low(jax.nn.silu(low_back(head_pre)))
        logits = low_back(jnp.dot(hidden.reshape(-1, BRANCH_WIDTH), out_weight, precision=PRECISE))
        totals.append(task_sums(logits, pixel_info)[task_index])
    return jnp.stack(totals)

def reference(features, labels, depth_mask, depth_target, normal_target, scene_ids, task_weights, conflict, trunk_copy, trunk_master, trunk_left, trunk_right, left_root, right_root, head_copy, head_master, head_first, head_second, out_copy, out_master, out_first, out_second, trunk_gains, gains_first, gains_second, head_bias, bias_first, bias_second):
    inputs = features.astype(jnp.float32)
    pixel_info = pixel_data(labels, depth_mask, depth_target, normal_target, scene_ids, task_weights)
    valid_count = jnp.sum(pixel_info[1])
    pixels = jnp.array(BATCH * MAP_HEIGHT * MAP_WIDTH, jnp.float32)
    divisor = jnp.stack([pixels, valid_count, pixels, pixels])
    params = (trunk_copy.astype(jnp.float32), trunk_gains, head_copy.astype(jnp.float32), head_bias, out_copy.astype(jnp.float32))
    totals, pullback = jax.vjp(lambda *weights: forward(weights, inputs, pixel_info), *params)
    selectors = jnp.eye(TASKS, dtype=jnp.float32)
    gradients = [pullback(selectors[task_index]) for task_index in range(TASKS)]
    scaled = jnp.stack([gradients[task_index][0] / divisor[task_index] for task_index in range(TASKS)])
    flattened = scaled.reshape(TASKS, -1)
    pair_products = jnp.dot(flattened, flattened.T, precision=PRECISE)
    mixing = combine_weights(pair_products, conflict)
    combined = lax.optimization_barrier(jnp.sum(mixing[:, None, None, None, None] * scaled, axis=0))

    def summed(position):
        return sum((gradients[task_index][position] / divisor[task_index] for task_index in range(TASKS)))
    left_new = 0.5 * trunk_left + 0.5 * jnp.einsum('lkio,lkjo->lkij', combined, combined, precision=PRECISE)
    right_new = 0.5 * trunk_right + 0.5 * jnp.einsum('lkio,lkip->lkop', combined, combined, precision=PRECISE)
    turned = jnp.einsum('lkia,lkaj->lkij', left_root, combined, precision=PRECISE)
    step_full = jnp.einsum('lkij,lkjo->lkio', turned, right_root, precision=PRECISE)
    master_new = trunk_master - RATE_TRUNK * (step_full + WEIGHT_DECAY * trunk_master)
    head_one, head_two, head_new = adamw_update(summed(2), head_first, head_second, head_master, RATE_MATRIX)
    out_one, out_two, out_new = adamw_update(summed(4), out_first, out_second, out_master, RATE_MATRIX)
    gain_one, gain_two, gain_new = adamw_update(summed(1), gains_first, gains_second, trunk_gains, RATE_VECTOR)
    bias_one, bias_two, bias_new = adamw_update(summed(3), bias_first, bias_second, head_bias, RATE_VECTOR)
    loss_terms = jnp.concatenate([totals, valid_count[None]])
    return (combined, left_new, right_new, master_new, master_new.astype(jnp.bfloat16), head_one, head_two, head_new, head_new.astype(jnp.bfloat16), out_one, out_two, out_new, out_new.astype(jnp.bfloat16), gain_one, gain_two, gain_new, bias_one, bias_two, bias_new, loss_terms, pair_products)
```

```python
import functools

import jax
import jax.numpy as jnp
from jax import lax
from jax.experimental import pallas as pl
from jax.experimental.pallas import tpu as pltpu
from jax.sharding import PartitionSpec as P

BRANCH_WIDTH = 256
CLASSES = 13
TASKS = 4
DILATION_STEP = 2
STEP = 5


PRECISE = lax.Precision.HIGHEST
NORM_EPS = 1e-05
RATE_TRUNK = 0.3
RATE_MATRIX = 0.05
RATE_VECTOR = 0.3
WEIGHT_DECAY = 0.01
ADAM_EPS = 1e-08
GRAM_EPS = 1e-12
PLAIN = (((1,), (0,)), ((), ()))
CONTRACT_ROWS = (((0,), (0,)), ((), ()))
CONTRACT_COLS = (((1,), (1,)), ((), ()))
CHUNK = 9
TILE = 12
PARAMS = pltpu.CompilerParams(vmem_limit_bytes=58 * 1024 * 1024)


def silu_slope(tap_values):
    sigmoid = jax.nn.sigmoid(tap_values)
    return sigmoid * (1.0 + tap_values * (1.0 - sigmoid))


def dot(a, b, contract=PLAIN):
    return lax.dot_general(a, b, contract, preferred_element_type=jnp.float32)


def clear_edges(wide):
    rows = wide.shape[1]
    edge = jnp.zeros((wide.shape[0], DILATION_STEP) + wide.shape[2:], wide.dtype)
    wide[:, 0:DILATION_STEP] = edge
    wide[:, rows - DILATION_STEP : rows] = edge


def spread_columns(wide, image, row, values):
    width, channels = values.shape[1:]
    column = lax.broadcasted_iota(jnp.int32, (1, width, channels), 1)
    left = jnp.where(column >= DILATION_STEP, pltpu.roll(values, DILATION_STEP, 1), 0.0)
    right = jnp.where(
        column < width - DILATION_STEP, pltpu.roll(values, width - DILATION_STEP, 1), 0.0
    )
    place = pl.ds(DILATION_STEP + row, values.shape[0])
    for part, piece in enumerate((left, values, right)):
        wide[image, place, :, part * channels : (part + 1) * channels] = piece.astype(wide.dtype)


def window(wide, image, row, rows, kernel_row, part=None):
    channels = wide.shape[3] // 3
    place = pl.ds(row + DILATION_STEP * kernel_row, rows)
    if part is None:
        return wide[image, place].reshape(rows * wide.shape[2], 3 * channels)
    return wide[image, place, :, part * channels : (part + 1) * channels].reshape(
        rows * wide.shape[2], channels
    )


def conv_tile(wide, weights, image, row, rows):
    channels = weights.shape[1]
    taps = jnp.concatenate([window(wide, image, row, rows, k) for k in range(3)], axis=1)
    return dot(taps, weights[...].reshape(9 * channels, channels))


def conv_tile_back(wide, weights, image, row, rows):
    total = None
    for tap in range(9):
        kernel_row, kernel_column = divmod(tap, 3)
        part = dot(
            window(wide, image, row, rows, 2 - kernel_row, 2 - kernel_column),
            weights[tap],
            CONTRACT_COLS,
        )
        total = part if total is None else total + part
    return total


def add_sums(sums, first, second):
    sums[0:1] += jnp.sum(first, axis=0, keepdims=True)
    sums[1:2] += jnp.sum(second, axis=0, keepdims=True)


def first_kernel(steps, tiles, x_ref, w_ref, conv_ref, sums, wide):
    g = pl.program_id(0)

    @pl.when(g == 0)
    def _():
        clear_edges(wide)
        sums[...] = jnp.zeros_like(sums)

    @pl.when(g < steps)
    def _():
        per = steps // wide.shape[0]

        def one(i, carry):
            spread_columns(
                wide,
                g // per,
                lax.rem(g, per) * CHUNK + 3 * i,
                x_ref[0, pl.ds(3 * i, 3)].astype(jnp.float32),
            )
            return carry

        lax.fori_loop(0, CHUNK // 3, one, 0)
        sums[2:3] += jnp.sum(x_ref[0].astype(jnp.float32), axis=(0, 1))[None]

    @pl.when(g >= steps)
    def _():
        per = tiles // wide.shape[0]
        t = g - steps
        conv = conv_tile(wide, w_ref, t // per, lax.rem(t, per) * TILE, TILE)
        conv_ref[...] = conv
        add_sums(sums, conv, conv * conv)


def second_kernel(steps, tiles, y_ref, v_ref, w_ref, conv_ref, act_ref, sums, wide):
    g = pl.program_id(0)

    @pl.when(g == 0)
    def _():
        clear_edges(wide)
        sums[...] = jnp.zeros_like(sums)

    @pl.when(g < steps)
    def _():
        per = steps // wide.shape[0]

        def one(i, carry):
            values = y_ref[0, pl.ds(3 * i, 3)]
            normed = v_ref[2:3] * ((values - v_ref[0:1]) * v_ref[1:2]) + v_ref[3:4]
            act = jax.nn.silu(normed).astype(jnp.bfloat16)
            act_ref[0, pl.ds(3 * i, 3)] = act
            act = act.astype(jnp.float32)
            spread_columns(wide, g // per, lax.rem(g, per) * CHUNK + 3 * i, act)
            sums[2:3] += jnp.sum(act, axis=(0, 1))[None]
            return carry

        lax.fori_loop(0, CHUNK // 3, one, 0)

    @pl.when(g >= steps)
    def _():
        per = tiles // wide.shape[0]
        t = g - steps
        conv = conv_tile(wide, w_ref, t // per, lax.rem(t, per) * TILE, TILE)
        conv_ref[...] = conv
        add_sums(sums, conv, conv * conv)


def map_specs(images, height, width, channels):
    per = height // CHUNK
    steps = images * per
    stream = pl.BlockSpec(
        (1, CHUNK, width, channels),
        lambda g: (jnp.minimum(g, steps - 1) // per, lax.rem(jnp.minimum(g, steps - 1), per), 0, 0),
    )
    rows = pl.BlockSpec((TILE * width, channels), lambda g: (jnp.maximum(g - steps, 0), 0))
    return steps, images * (height // TILE), stream, rows


def fixed(*shape):
    return pl.BlockSpec(shape, lambda g: (0,) * len(shape))


def first_conv_call(x, weights):
    images, height, width, channels = x.shape
    steps, tiles, stream, rows = map_specs(*x.shape)
    pixels = images * height * width
    return pl.pallas_call(
        functools.partial(first_kernel, steps, tiles),
        grid=(steps + tiles,),
        in_specs=[stream, fixed(*weights.shape)],
        out_specs=(rows, fixed(8, channels)),
        out_shape=(
            jax.ShapeDtypeStruct((pixels, channels), jnp.float32),
            jax.ShapeDtypeStruct((8, channels), jnp.float32),
        ),
        scratch_shapes=[
            pltpu.VMEM((images, height + 2 * DILATION_STEP, width, 3 * channels), jnp.bfloat16)
        ],
        compiler_params=PARAMS,
        name="first_conv",
    )(x, weights)


def second_conv_call(y, vectors, weights, shape):
    images, height, width, channels = shape
    steps, tiles, stream, rows = map_specs(*shape)
    pixels = images * height * width
    return pl.pallas_call(
        functools.partial(second_kernel, steps, tiles),
        grid=(steps + tiles,),
        in_specs=[stream, fixed(8, channels), fixed(*weights.shape)],
        out_specs=(rows, stream, fixed(8, channels)),
        out_shape=(
            jax.ShapeDtypeStruct((pixels, channels), jnp.float32),
            jax.ShapeDtypeStruct(shape, jnp.bfloat16),
            jax.ShapeDtypeStruct((8, channels), jnp.float32),
        ),
        scratch_shapes=[
            pltpu.VMEM((images, height + 2 * DILATION_STEP, width, 3 * channels), jnp.bfloat16)
        ],
        compiler_params=PARAMS,
        name="second_conv",
    )(y.reshape(shape), vectors, weights)


def weight_kernel(steps, keep_back, x_ref, up_ref, y_ref, v_ref, mean_ref, grad_ref, edge_ref, *rest):
    wide, back = rest[-2:]
    g = pl.program_id(0)
    images, padded, width, channels = wide.shape
    channels = channels // 3
    height = padded - 2 * DILATION_STEP

    @pl.when(g == 0)
    def _():
        clear_edges(wide)
        edge_ref[...] = jnp.zeros_like(edge_ref)

    @pl.when(g < steps)
    def _():
        per = steps // images
        column = lax.broadcasted_iota(jnp.int32, (1, width, channels), 1)

        def one(i, carry):
            place = pl.ds(3 * i, 3)
            row = lax.rem(g, per) * CHUNK + 3 * i
            spread_columns(wide, g // per, row, x_ref[0, place].astype(jnp.float32))
            centered = (y_ref[0, place] - v_ref[0:1]) * v_ref[1:2]
            values = v_ref[2:3] * v_ref[1:2] * (
                up_ref[0, place] - v_ref[4:5] - centered * v_ref[5:6]
            )
            values = values.astype(jnp.bfloat16)
            if keep_back:
                rest[0][0, place] = values
            back[g // per, pl.ds(row, 3)] = values
            values = values.astype(jnp.float32)
            for kernel_column in range(3):
                shift = DILATION_STEP * (kernel_column - 1)
                inside = (column + shift >= 0) & (column + shift < width)
                line = jnp.sum(jnp.where(inside, values, 0.0), axis=1)
                for kernel_row in range(3):
                    at = row + DILATION_STEP * (kernel_row - 1)
                    part = [
                        jnp.where((at + r >= 0) & (at + r < height), line[r : r + 1], 0.0)
                        for r in range(3)
                    ]
                    tap = 3 * kernel_row + kernel_column
                    edge_ref[tap : tap + 1] += part[0] + part[1] + part[2]
            return carry

        lax.fori_loop(0, CHUNK // 3, one, 0)

    for column in range(3):

        @pl.when((g >= steps) & (lax.rem(g - steps, 3) == column))
        def _():
            total = None
            for image in range(images):
                part = dot(
                    window(wide, image, 0, height, (g - steps) // 3, column),
                    back[image].reshape(height * width, channels),
                    CONTRACT_ROWS,
                )
                total = part if total is None else total + part
            line = edge_ref[pl.ds(g - steps, 1)]
            grad_ref[0] = (total - mean_ref[...] * line).astype(grad_ref.dtype)


def weight_grad_call(x, upstream, y, vectors, mean, keep_back):
    images, height, width, channels = x.shape
    steps, tiles, stream, rows = map_specs(*x.shape)
    out_specs = [
        pl.BlockSpec((1, channels, channels), lambda g: (jnp.maximum(g - steps, 0), 0, 0)),
        fixed(16, channels),
    ]
    out_shape = [
        jax.ShapeDtypeStruct((9, channels, channels), jnp.bfloat16),
        jax.ShapeDtypeStruct((16, channels), jnp.float32),
    ]
    if keep_back:
        out_specs.append(stream)
        out_shape.append(jax.ShapeDtypeStruct(x.shape, jnp.bfloat16))
    return pl.pallas_call(
        functools.partial(weight_kernel, steps, keep_back),
        grid=(steps + 9,),
        in_specs=[stream, stream, stream, fixed(8, channels), fixed(channels, 1)],
        out_specs=tuple(out_specs),
        out_shape=tuple(out_shape),
        scratch_shapes=[
            pltpu.VMEM((images, height + 2 * DILATION_STEP, width, 3 * channels), jnp.bfloat16),
            pltpu.VMEM((images, height, width, channels), jnp.bfloat16),
        ],
        compiler_params=PARAMS,
        name="weight_grad",
    )(x, upstream.reshape(x.shape), y.reshape(x.shape), vectors, mean.reshape(channels, 1))


def act_grad_kernel(steps, tiles, back_ref, y_ref, v_ref, w_ref, up_ref, sums, wide):
    g = pl.program_id(0)

    @pl.when(g == 0)
    def _():
        clear_edges(wide)
        sums[...] = jnp.zeros_like(sums)

    @pl.when(g < steps)
    def _():
        per = steps // wide.shape[0]

        def one(i, carry):
            spread_columns(
                wide,
                g // per,
                lax.rem(g, per) * CHUNK + 3 * i,
                back_ref[0, pl.ds(3 * i, 3)].astype(jnp.float32),
            )
            return carry

        lax.fori_loop(0, CHUNK // 3, one, 0)

    @pl.when(g >= steps)
    def _():
        per = tiles // wide.shape[0]
        t = g - steps
        grad = conv_tile_back(wide, w_ref, t // per, lax.rem(t, per) * TILE, TILE)
        centered = (y_ref[...] - v_ref[0:1]) * v_ref[1:2]
        upstream = grad * silu_slope(v_ref[2:3] * centered + v_ref[3:4])
        up_ref[...] = upstream
        add_sums(sums, upstream, upstream * centered)


def act_grad_call(back, y, vectors, weights):
    images, height, width, channels = back.shape
    steps, tiles, stream, rows = map_specs(*back.shape)
    pixels = images * height * width
    return pl.pallas_call(
        functools.partial(act_grad_kernel, steps, tiles),
        grid=(steps + tiles,),
        in_specs=[stream, rows, fixed(8, channels), fixed(*weights.shape)],
        out_specs=(rows, fixed(8, channels)),
        out_shape=(
            jax.ShapeDtypeStruct((pixels, channels), jnp.float32),
            jax.ShapeDtypeStruct((8, channels), jnp.float32),
        ),
        scratch_shapes=[
            pltpu.VMEM((images, height + 2 * DILATION_STEP, width, 3 * channels), jnp.bfloat16)
        ],
        compiler_params=PARAMS,
        name="act_grad",
    )(back, y, vectors, weights)


def update_kernel(
    g_ref, rows_ref, cols_ref, left_ref, right_ref, master_ref, lroot_ref,
    rroot_ref, grad_out, left_out, right_out, master_out, copy_out,
):
    full = g_ref[0]
    rows = rows_ref[0]
    grad_out[0] = rows.astype(jnp.float32)
    left_out[0] = 0.5 * left_ref[0] + 0.5 * dot(rows, full, CONTRACT_COLS)
    right_out[0] = 0.5 * right_ref[0] + 0.5 * dot(cols_ref[0], full)
    turned = dot(lroot_ref[0].astype(jnp.bfloat16), full).astype(jnp.bfloat16)
    step = dot(turned, rroot_ref[0].astype(jnp.bfloat16))
    master = master_ref[0]
    master = master - RATE_TRUNK * (step + WEIGHT_DECAY * master)
    master_out[0] = master
    copy_out[0] = master.astype(jnp.bfloat16)


def update_call(owner, combined, left, right, master, lroot, rroot):
    layers, taps, shard_rows, channels = left.shape
    count = layers * taps
    one = pl.BlockSpec((1, shard_rows, channels), lambda g: (g, 0, 0))
    whole = pl.BlockSpec((1, channels, channels), lambda g: (g, 0, 0))
    flat = (count, shard_rows, channels)
    start = owner * shard_rows
    rows = lax.dynamic_slice_in_dim(combined, start, shard_rows, 1)
    cols = jnp.swapaxes(lax.dynamic_slice_in_dim(combined, start, shard_rows, 2), 1, 2)
    outs = pl.pallas_call(
        update_kernel,
        grid=(count,),
        in_specs=[whole, one, one, one, one, one, one, whole],
        out_specs=(one,) * 5,
        out_shape=tuple(
            jax.ShapeDtypeStruct(flat, kind)
            for kind in (jnp.float32, jnp.float32, jnp.float32, jnp.float32, jnp.bfloat16)
        ),
        compiler_params=PARAMS,
        name="update",
    )(
        combined,
        rows,
        cols,
        left.reshape(flat),
        right.reshape(flat),
        master.reshape(flat),
        lroot.reshape(flat),
        rroot.reshape(count, channels, channels),
    )
    return [out.reshape(left.shape) for out in outs]


def small_sum_kernel(members, x_ref, out_ref, slots, send_sem, recv_sem):
    me = lax.axis_index("dp")
    barrier = pltpu.get_barrier_semaphore()
    for k in range(1, members):
        pl.semaphore_signal(
            barrier,
            inc=1,
            device_id={"dp": lax.rem(me + k, members)},
            device_id_type=pl.DeviceIdType.MESH,
        )
    pl.semaphore_wait(barrier, members - 1)
    copies = []
    for k in range(1, members):
        copy = pltpu.make_async_remote_copy(
            src_ref=x_ref,
            dst_ref=slots.at[me],
            send_sem=send_sem.at[k],
            recv_sem=recv_sem.at[me],
            device_id={"dp": lax.rem(me + k, members)},
            device_id_type=pl.DeviceIdType.MESH,
        )
        copy.start()
        copies.append(copy)
    slots[me] = x_ref[...]
    for k in range(1, members):
        source = lax.rem(me + k, members)
        pltpu.make_async_remote_copy(
            src_ref=x_ref,
            dst_ref=slots.at[source],
            send_sem=send_sem.at[k],
            recv_sem=recv_sem.at[source],
            device_id={"dp": source},
            device_id_type=pl.DeviceIdType.MESH,
        ).wait_recv()
    total = slots[0]
    for k in range(1, members):
        total = total + slots[k]
    out_ref[...] = total
    for copy in copies:
        copy.wait_send()


def small_sum(x, identity):
    members = lax.axis_size("dp")
    return pl.pallas_call(
        functools.partial(small_sum_kernel, members),
        out_shape=jax.ShapeDtypeStruct(x.shape, jnp.float32),
        in_specs=[pl.BlockSpec(memory_space=pltpu.VMEM)],
        out_specs=pl.BlockSpec(memory_space=pltpu.VMEM),
        scratch_shapes=[
            pltpu.VMEM((members,) + x.shape, jnp.float32),
            pltpu.SemaphoreType.DMA((members,)),
            pltpu.SemaphoreType.DMA((members,)),
        ],
        compiler_params=pltpu.CompilerParams(collective_id=identity, has_side_effects=True),
        name="small_sum",
    )(x)


def scatter_sum(parts):
    members = lax.axis_size("dp")
    me = lax.axis_index("dp")
    taps, channels, width = parts.shape
    held = parts.reshape(taps, members, channels // members, width)
    bit = 1
    while bit < members:
        held = held.reshape(taps, -1, 2, channels // members, width)
        mine = lax.rem(me // bit, 2)
        other = lax.dynamic_index_in_dim(held, 1 - mine, 2, keepdims=False)
        keep = lax.dynamic_index_in_dim(held, mine, 2, keepdims=False)
        other = lax.ppermute(
            other.astype(jnp.bfloat16), "dp", [(i, i ^ bit) for i in range(members)]
        )
        held = keep.astype(jnp.float32) + other.astype(jnp.float32)
        bit *= 2
    return held.reshape(taps, channels // members, width)


def pad_rows(parts, rows):
    used = sum(part.shape[0] for part in parts)
    if used < rows:
        parts = list(parts) + [jnp.zeros((rows - used, parts[0].shape[1]), jnp.float32)]
    return jnp.concatenate(parts)


def norm_vectors(totals, gain, shift, pixels):
    center = totals[0] / pixels
    inverse = lax.rsqrt(totals[1] / pixels - center * center + NORM_EPS)
    return center, inverse, gain, shift


def stack_vectors(parts):
    zero = jnp.zeros_like(parts[0])
    return jnp.stack(list(parts) + [zero] * (8 - len(parts)))


def boundary(labels):
    across = jnp.pad(
        (labels[:, :, 1:] != labels[:, :, :-1]).astype(jnp.float32), ((0, 0), (0, 0), (0, 1))
    )
    downward = jnp.pad(
        (labels[:, 1:, :] != labels[:, :-1, :]).astype(jnp.float32), ((0, 0), (0, 1), (0, 0))
    )
    return jnp.maximum(across, downward)


def pixel_data(labels, depth_mask, depth_target, normal_target, scene_ids, task_weights):
    images, feature_rows, feature_columns = labels.shape
    choose = (scene_ids[:, None] == jnp.arange(task_weights.shape[0])[None, :]).astype(jnp.float32)
    per_image = jnp.dot(choose, task_weights, precision=PRECISE)
    return (
        labels.reshape(-1),
        depth_mask.reshape(-1).astype(jnp.float32),
        boundary(labels).reshape(-1),
        depth_target.reshape(-1),
        jnp.transpose(normal_target, (0, 2, 3, 1)).reshape(-1, 3),
        jnp.repeat(per_image, feature_rows * feature_columns, axis=0),
    )


def task_sums(logits, pixel_info):
    labels, valid_mask, edge_target, depth_values, normals, weights = pixel_info
    classes = logits[:, :CLASSES]
    largest = jnp.max(classes, axis=1, keepdims=True)
    spread = jnp.log(jnp.sum(jnp.exp(classes - largest), axis=1)) + largest[:, 0]
    picked = jnp.sum(
        jnp.where(labels[:, None] == jnp.arange(CLASSES)[None, :], classes, 0.0), axis=1
    )
    segment = jnp.sum(weights[:, 0] * (spread - picked))
    offset = logits[:, CLASSES] - depth_values
    distance = jnp.sum(weights[:, 1] * valid_mask * (jnp.sqrt(offset * offset + 1.0) - 1.0))
    predicted = logits[:, CLASSES + 1 : CLASSES + 4]
    cosine = jnp.sum(predicted * normals, axis=1) * lax.rsqrt(
        (jnp.sum(predicted * predicted, axis=1) + 1.0) * (jnp.sum(normals * normals, axis=1) + 1.0)
    )
    surface = jnp.sum(weights[:, 2] * (1.0 - cosine))
    edge_logit = logits[:, CLASSES + 4]
    contour = jnp.sum(weights[:, 3] * (jax.nn.softplus(edge_logit) - edge_target * edge_logit))
    return jnp.stack([segment, distance, surface, contour])


def combine_weights(pair_products, conflict):
    offdiagonal = (1.0 - jnp.eye(TASKS, dtype=jnp.float32)) * conflict.astype(jnp.float32)
    ratios = offdiagonal * pair_products / (jnp.diagonal(pair_products)[None, :] + GRAM_EPS)
    return 1.0 - jnp.sum(ratios, axis=0)


def adamw_update(gradient, moment_one, moment_two, weight, rate):
    moment_one = 0.5 * moment_one + 0.5 * gradient
    moment_two = 0.5 * moment_two + 0.5 * gradient * gradient
    correction = 1.0 - 0.5**STEP
    weight = weight - rate * (
        moment_one / correction / (jnp.sqrt(moment_two / correction) + ADAM_EPS)
        + WEIGHT_DECAY * weight
    )
    return (moment_one, moment_two, weight)


def body(
    features,
    labels,
    depth_mask,
    depth_target,
    normal_target,
    scene_ids,
    task_weights,
    conflict,
    trunk_copy,
    trunk_master,
    trunk_left,
    trunk_right,
    left_root,
    right_root,
    head_copy,
    head_master,
    head_first,
    head_second,
    out_copy,
    out_master,
    out_first,
    out_second,
    trunk_gains,
    gains_first,
    gains_second,
    head_bias,
    bias_first,
    bias_second,
):
    images, feature_rows, feature_columns, channels = features.shape
    pixels = jnp.array(images * feature_rows * feature_columns * lax.axis_size("dp"), jnp.float32)
    task_index = lax.axis_index("task")
    owner_index = lax.axis_index("dp")
    trunk_first = lax.all_gather(trunk_copy[0], "dp", axis=1, tiled=True)
    trunk_second = lax.all_gather(trunk_copy[1], "dp", axis=1, tiled=True)
    head_full = lax.all_gather(head_copy, "dp", axis=2, tiled=True)
    pixel_info = pixel_data(
        labels, depth_mask, depth_target, normal_target, scene_ids, task_weights
    )
    local_valid = jnp.sum(pixel_info[1])
    first_conv, first_sums = first_conv_call(features, trunk_first)
    first_totals = small_sum(
        pad_rows([first_sums[:3], jnp.full((1, channels), local_valid)], 8), 0
    )
    valid_count = first_totals[3, 0]
    first_norm = norm_vectors(first_totals, trunk_gains[0], trunk_gains[1], pixels)
    second_conv, first_act, second_sums = second_conv_call(
        first_conv, stack_vectors(first_norm), trunk_second, features.shape
    )
    second_totals = small_sum(second_sums, 1)
    second_norm = norm_vectors(second_totals, trunk_gains[2], trunk_gains[3], pixels)
    second_center = (second_conv - second_norm[0]) * second_norm[1]
    residual_in = (
        trunk_gains[2] * second_center + trunk_gains[3] + features.reshape(-1, channels)
    )
    trunk_out = jax.nn.silu(residual_in).astype(jnp.bfloat16)
    pooled = jnp.mean(trunk_out.reshape(images, -1, channels), axis=1, dtype=jnp.float32).astype(
        jnp.bfloat16
    )
    selector = (jnp.arange(TASKS) == task_index).astype(jnp.float32)
    own_bias = jnp.dot(selector, head_bias, precision=PRECISE)
    head_pre = jnp.dot(trunk_out, head_full[0, 0], preferred_element_type=jnp.float32).reshape(
        images, -1, BRANCH_WIDTH
    )
    head_pre = (
        head_pre
        + jnp.dot(pooled, head_full[0, 1], preferred_element_type=jnp.float32)[:, None, :]
        + own_bias
    )
    head_pre = head_pre.reshape(-1, BRANCH_WIDTH)
    hidden_act = jax.nn.silu(head_pre).astype(jnp.bfloat16)
    logits = jnp.dot(hidden_act, out_copy, preferred_element_type=jnp.float32)
    totals, pullback = jax.vjp(lambda tap_values: task_sums(tap_values, pixel_info), logits)
    logit_grad = pullback(selector)[0].astype(jnp.bfloat16)
    out_grad = dot(hidden_act, logit_grad, CONTRACT_ROWS)
    hidden_grad = dot(logit_grad, out_copy, CONTRACT_COLS)
    pre_grad = (hidden_grad * silu_slope(head_pre)).astype(jnp.bfloat16)
    bias_grad = jnp.sum(pre_grad, axis=0, dtype=jnp.float32)
    per_image = jnp.sum(pre_grad.reshape(images, -1, BRANCH_WIDTH), axis=1, dtype=jnp.float32)
    input_grad = dot(trunk_out, pre_grad, CONTRACT_ROWS)
    pool_grad = jnp.dot(pooled.astype(jnp.float32).T, per_image, precision=PRECISE)
    pooled_back = jnp.dot(per_image, head_full[0, 1].astype(jnp.float32).T, precision=PRECISE)
    out_back = dot(pre_grad, head_full[0, 0], CONTRACT_COLS)
    out_back = (
        out_back.reshape(images, -1, channels)
        + pooled_back[:, None, :] / (feature_rows * feature_columns)
    ).reshape(-1, channels)
    second_up = out_back * silu_slope(residual_in)
    second_back_sums = small_sum(
        pad_rows(
            [
                jnp.sum(second_up, axis=0, keepdims=True),
                jnp.sum(second_up * second_center, axis=0, keepdims=True),
            ],
            8,
        ),
        2,
    )[:2]
    second_mean = second_totals[2] / pixels
    second_weight, second_edges, second_back = weight_grad_call(
        first_act,
        second_up,
        second_conv,
        stack_vectors(second_norm + tuple(second_back_sums / pixels)),
        second_mean,
        True,
    )
    second_sum = scatter_sum(second_weight)
    first_up, first_up_sums = act_grad_call(
        second_back, first_conv, stack_vectors(first_norm), trunk_second
    )
    first_back_sums = small_sum(first_up_sums, 3)[:2]
    first_mean = first_totals[2] / pixels
    first_weight, first_edges = weight_grad_call(
        features,
        first_up,
        first_conv,
        stack_vectors(first_norm + tuple(first_back_sums / pixels)),
        first_mean,
        False,
    )
    first_sum = scatter_sum(first_weight)
    edges = small_sum(jnp.concatenate([first_edges, second_edges]), 4).reshape(2, 16, 1, channels)
    means = jnp.stack([first_mean, second_mean])
    shard_rows = trunk_copy.shape[2]
    own_means = lax.dynamic_slice_in_dim(means, owner_index * shard_rows, shard_rows, 1)
    removed = (own_means[:, None, :, None] * edges[:, :9]).reshape(18, shard_rows, channels)
    head_grad = jnp.stack([input_grad, pool_grad])[None]
    leading = (owner_index == 0).astype(jnp.float32)
    gains_part = (
        selector[:, None, None]
        * (
            leading
            * jnp.stack(
                [first_back_sums[1], first_back_sums[0], second_back_sums[1], second_back_sums[0]]
            )
        )[None]
    )
    bias_part = selector[:, None] * bias_grad[None]
    loss_part = totals * selector
    gains_sum, bias_sum, out_sum, loss_sum = lax.psum(
        (gains_part, bias_part, out_grad, loss_part), ("task", "dp")
    )
    divisor = jnp.stack([pixels, valid_count, pixels, pixels])
    own_divisor = jnp.sum(divisor * selector)
    gains_total = jnp.sum(gains_sum / divisor[:, None, None], axis=0)
    bias_total = bias_sum / divisor[:, None]
    column_divisor = jnp.concatenate(
        [jnp.full((CLASSES,), divisor[0]), divisor[1:2], jnp.full((3,), divisor[2]), divisor[3:4]]
    )
    out_total = out_sum / column_divisor[None, :]
    head_rows = lax.psum_scatter(head_grad, "dp", scatter_dimension=2, tiled=True)
    own_scaled = (
        (jnp.concatenate([first_sum, second_sum]) + removed) / own_divisor
    ).astype(jnp.bfloat16)
    taps, shard_rows = own_scaled.shape[:2]
    pieces = own_scaled.reshape(taps, shard_rows, TASKS, channels // TASKS)
    scaled = lax.all_to_all(pieces, "task", split_axis=2, concat_axis=0, tiled=False)
    scaled = scaled.reshape(TASKS, taps * shard_rows, channels // TASKS).astype(jnp.float32)
    products = {
        (i, j): jnp.sum(scaled[i] * scaled[j]) for i in range(TASKS) for j in range(i, TASKS)
    }
    pair_products = lax.psum(
        jnp.stack(
            [products[min(i, j), max(i, j)] for i in range(TASKS) for j in range(TASKS)]
        ).reshape(TASKS, TASKS),
        ("task", "dp"),
    )
    mixing = combine_weights(pair_products, conflict)
    quarter = jnp.sum(mixing[:, None, None] * scaled, axis=0).astype(jnp.bfloat16)
    quarter = quarter.reshape(taps, shard_rows, channels // TASKS)
    combined = lax.all_gather(
        lax.all_gather(quarter, "task", axis=2, tiled=True), "dp", axis=1, tiled=True
    )
    grad_rows, left_new, right_new, master_new, copy_new = update_call(
        owner_index, combined, trunk_left, trunk_right, trunk_master, left_root, right_root
    )
    head_one, head_two, head_new = adamw_update(
        head_rows / own_divisor, head_first, head_second, head_master, RATE_MATRIX
    )
    out_one, out_two, out_new = adamw_update(
        out_total, out_first, out_second, out_master, RATE_MATRIX
    )
    gain_one, gain_two, gain_new = adamw_update(
        gains_total, gains_first, gains_second, trunk_gains, RATE_VECTOR
    )
    bias_one, bias_two, bias_new = adamw_update(
        bias_total, bias_first, bias_second, head_bias, RATE_VECTOR
    )
    loss_terms = jnp.concatenate([loss_sum, valid_count[None]])
    return (
        grad_rows,
        left_new,
        right_new,
        master_new,
        copy_new,
        head_one,
        head_two,
        head_new,
        head_new.astype(jnp.bfloat16),
        out_one,
        out_two,
        out_new,
        out_new.astype(jnp.bfloat16),
        gain_one,
        gain_two,
        gain_new,
        bias_one,
        bias_two,
        bias_new,
        loss_terms,
        pair_products,
    )


def solution(mesh):
    rows = P(None, None, "dp", None)
    heads = P("task", None, "dp", None)
    images = P("dp")
    placed = (
        (images,) * 6
        + (P(), P())
        + (rows,) * 5
        + (P(),)
        + (heads,) * 4
        + (P(),) * 10
    )
    return jax.shard_map(
        body,
        mesh=mesh,
        in_specs=placed,
        out_specs=(rows,) * 5 + (heads,) * 4 + (P(),) * 12,
        check_vma=False,
    )
```

```python
import functools

import jax
import jax.numpy as jnp
from jax import lax
from jax.experimental import pallas as pl
from jax.experimental.pallas import tpu as pltpu
from jax.sharding import PartitionSpec as P

BRANCH_WIDTH = 256
CLASSES = 13
TASKS = 4
DILATION_STEP = 2
STEP = 5


PRECISE = lax.Precision.HIGHEST
NORM_EPS = 1e-05
RATE_TRUNK = 0.3
RATE_MATRIX = 0.05
RATE_VECTOR = 0.3
WEIGHT_DECAY = 0.01
ADAM_EPS = 1e-08
GRAM_EPS = 1e-12
PLAIN = (((1,), (0,)), ((), ()))
CONTRACT_ROWS = (((0,), (0,)), ((), ()))
CONTRACT_COLS = (((1,), (1,)), ((), ()))
CHUNK = 9
TILE = 12
PARAMS = pltpu.CompilerParams(vmem_limit_bytes=58 * 1024 * 1024)


def silu_slope(tap_values):
    sigmoid = jax.nn.sigmoid(tap_values)
    return sigmoid * (1.0 + tap_values * (1.0 - sigmoid))


def dot(a, b, contract=PLAIN):
    return lax.dot_general(a, b, contract, preferred_element_type=jnp.float32)


def clear_edges(wide):
    rows = wide.shape[1]
    edge = jnp.zeros((wide.shape[0], DILATION_STEP) + wide.shape[2:], wide.dtype)
    wide[:, 0:DILATION_STEP] = edge
    wide[:, rows - DILATION_STEP : rows] = edge


def spread_columns(wide, image, row, values):
    width, channels = values.shape[1:]
    column = lax.broadcasted_iota(jnp.int32, (1, width, channels), 1)
    left = jnp.where(column >= DILATION_STEP, pltpu.roll(values, DILATION_STEP, 1), 0.0)
    right = jnp.where(
        column < width - DILATION_STEP, pltpu.roll(values, width - DILATION_STEP, 1), 0.0
    )
    place = pl.ds(DILATION_STEP + row, values.shape[0])
    for part, piece in enumerate((left, values, right)):
        wide[image, place, :, part * channels : (part + 1) * channels] = piece.astype(wide.dtype)


def window(wide, image, row, rows, kernel_row, part=None):
    channels = wide.shape[3] // 3
    place = pl.ds(row + DILATION_STEP * kernel_row, rows)
    if part is None:
        return wide[image, place].reshape(rows * wide.shape[2], 3 * channels)
    return wide[image, place, :, part * channels : (part + 1) * channels].reshape(
        rows * wide.shape[2], channels
    )


def conv_tile(wide, weights, image, row, rows):
    parts, channels, width = weights.shape[1:]
    taps = jnp.concatenate([window(wide, image, row, rows, k) for k in range(3)], axis=1)
    full = jnp.concatenate(
        [weights[:, part].reshape(9 * channels, width) for part in range(parts)], axis=1
    )
    return dot(taps, full)


def conv_tile_back(wide, weights, image, row, rows):
    total = None
    for tap in range(9):
        kernel_row, kernel_column = divmod(tap, 3)
        part = dot(
            window(wide, image, row, rows, 2 - kernel_row, 2 - kernel_column),
            jnp.concatenate([weights[tap, part] for part in range(weights.shape[1])], axis=1),
            CONTRACT_COLS,
        )
        total = part if total is None else total + part
    return total


def add_sums(sums, first, second):
    sums[0:1] += jnp.sum(first, axis=0, keepdims=True)
    sums[1:2] += jnp.sum(second, axis=0, keepdims=True)


def first_kernel(steps, tiles, x_ref, w_ref, conv_ref, sums, wide):
    g = pl.program_id(0)

    @pl.when(g == 0)
    def _():
        clear_edges(wide)
        sums[...] = jnp.zeros_like(sums)

    @pl.when(g < steps)
    def _():
        per = steps // wide.shape[0]

        def one(i, carry):
            spread_columns(
                wide,
                g // per,
                lax.rem(g, per) * CHUNK + 3 * i,
                x_ref[0, pl.ds(3 * i, 3)].astype(jnp.float32),
            )
            return carry

        lax.fori_loop(0, CHUNK // 3, one, 0)
        sums[2:3] += jnp.sum(x_ref[0].astype(jnp.float32), axis=(0, 1))[None]

    @pl.when(g >= steps)
    def _():
        per = tiles // wide.shape[0]
        t = g - steps
        conv = conv_tile(wide, w_ref, t // per, lax.rem(t, per) * TILE, TILE)
        conv_ref[...] = conv
        add_sums(sums, conv, conv * conv)


def second_kernel(steps, tiles, y_ref, v_ref, w_ref, conv_ref, act_ref, sums, wide):
    g = pl.program_id(0)

    @pl.when(g == 0)
    def _():
        clear_edges(wide)
        sums[...] = jnp.zeros_like(sums)

    @pl.when(g < steps)
    def _():
        per = steps // wide.shape[0]

        def one(i, carry):
            values = y_ref[0, pl.ds(3 * i, 3)]
            normed = v_ref[2:3] * ((values - v_ref[0:1]) * v_ref[1:2]) + v_ref[3:4]
            act = jax.nn.silu(normed).astype(jnp.bfloat16)
            act_ref[0, pl.ds(3 * i, 3)] = act
            act = act.astype(jnp.float32)
            spread_columns(wide, g // per, lax.rem(g, per) * CHUNK + 3 * i, act)
            sums[2:3] += jnp.sum(act, axis=(0, 1))[None]
            return carry

        lax.fori_loop(0, CHUNK // 3, one, 0)

    @pl.when(g >= steps)
    def _():
        per = tiles // wide.shape[0]
        t = g - steps
        conv = conv_tile(wide, w_ref, t // per, lax.rem(t, per) * TILE, TILE)
        conv_ref[...] = conv
        add_sums(sums, conv, conv * conv)


def map_specs(images, height, width, channels):
    per = height // CHUNK
    steps = images * per
    stream = pl.BlockSpec(
        (1, CHUNK, width, channels),
        lambda g: (jnp.minimum(g, steps - 1) // per, lax.rem(jnp.minimum(g, steps - 1), per), 0, 0),
    )
    rows = pl.BlockSpec((TILE * width, channels), lambda g: (jnp.maximum(g - steps, 0), 0))
    return steps, images * (height // TILE), stream, rows


def fixed(*shape):
    return pl.BlockSpec(shape, lambda g: (0,) * len(shape))


def layer_spec(weights, layer):
    shape = (9,) + weights.shape[1:]
    return pl.BlockSpec(shape, lambda g: (layer, 0, 0, 0))


def first_conv_call(x, weights):
    images, height, width, channels = x.shape
    steps, tiles, stream, rows = map_specs(*x.shape)
    pixels = images * height * width
    return pl.pallas_call(
        functools.partial(first_kernel, steps, tiles),
        grid=(steps + tiles,),
        in_specs=[stream, layer_spec(weights, 0)],
        out_specs=(rows, fixed(8, channels)),
        out_shape=(
            jax.ShapeDtypeStruct((pixels, channels), jnp.float32),
            jax.ShapeDtypeStruct((8, channels), jnp.float32),
        ),
        scratch_shapes=[
            pltpu.VMEM((images, height + 2 * DILATION_STEP, width, 3 * channels), jnp.bfloat16)
        ],
        compiler_params=PARAMS,
        name="first_conv",
    )(x, weights)


def second_conv_call(y, vectors, weights, shape):
    images, height, width, channels = shape
    steps, tiles, stream, rows = map_specs(*shape)
    pixels = images * height * width
    return pl.pallas_call(
        functools.partial(second_kernel, steps, tiles),
        grid=(steps + tiles,),
        in_specs=[stream, fixed(8, channels), layer_spec(weights, 1)],
        out_specs=(rows, stream, fixed(8, channels)),
        out_shape=(
            jax.ShapeDtypeStruct((pixels, channels), jnp.float32),
            jax.ShapeDtypeStruct(shape, jnp.bfloat16),
            jax.ShapeDtypeStruct((8, channels), jnp.float32),
        ),
        scratch_shapes=[
            pltpu.VMEM((images, height + 2 * DILATION_STEP, width, 3 * channels), jnp.bfloat16)
        ],
        compiler_params=PARAMS,
        name="second_conv",
    )(y.reshape(shape), vectors, weights)


def weight_kernel(steps, keep_back, x_ref, up_ref, y_ref, v_ref, mean_ref, grad_ref, edge_ref, *rest):
    wide, back = rest[-2:]
    g = pl.program_id(0)
    images, padded, width, channels = wide.shape
    channels = channels // 3
    height = padded - 2 * DILATION_STEP

    @pl.when(g == 0)
    def _():
        clear_edges(wide)
        edge_ref[...] = jnp.zeros_like(edge_ref)

    @pl.when(g < steps)
    def _():
        per = steps // images
        column = lax.broadcasted_iota(jnp.int32, (1, width, channels), 1)

        def one(i, carry):
            place = pl.ds(3 * i, 3)
            row = lax.rem(g, per) * CHUNK + 3 * i
            spread_columns(wide, g // per, row, x_ref[0, place].astype(jnp.float32))
            centered = (y_ref[0, place] - v_ref[0:1]) * v_ref[1:2]
            values = v_ref[2:3] * v_ref[1:2] * (
                up_ref[0, place] - v_ref[4:5] - centered * v_ref[5:6]
            )
            values = values.astype(jnp.bfloat16)
            if keep_back:
                rest[0][0, place] = values
            back[g // per, pl.ds(row, 3)] = values
            values = values.astype(jnp.float32)
            for kernel_column in range(3):
                shift = DILATION_STEP * (kernel_column - 1)
                inside = (column + shift >= 0) & (column + shift < width)
                line = jnp.sum(jnp.where(inside, values, 0.0), axis=1)
                for kernel_row in range(3):
                    at = row + DILATION_STEP * (kernel_row - 1)
                    part = [
                        jnp.where((at + r >= 0) & (at + r < height), line[r : r + 1], 0.0)
                        for r in range(3)
                    ]
                    tap = 3 * kernel_row + kernel_column
                    edge_ref[tap : tap + 1] += part[0] + part[1] + part[2]
            return carry

        lax.fori_loop(0, CHUNK // 3, one, 0)

    for column in range(3):

        @pl.when((g >= steps) & (lax.rem(g - steps, 3) == column))
        def _():
            total = None
            for image in range(images):
                part = dot(
                    window(wide, image, 0, height, (g - steps) // 3, column),
                    back[image].reshape(height * width, channels),
                    CONTRACT_ROWS,
                )
                total = part if total is None else total + part
            line = edge_ref[pl.ds(g - steps, 1)]
            grad_ref[0] = (total - mean_ref[...] * line).astype(grad_ref.dtype)


def weight_grad_call(x, upstream, y, vectors, mean, keep_back):
    images, height, width, channels = x.shape
    steps, tiles, stream, rows = map_specs(*x.shape)
    out_specs = [
        pl.BlockSpec((1, channels, channels), lambda g: (jnp.maximum(g - steps, 0), 0, 0)),
        fixed(16, channels),
    ]
    out_shape = [
        jax.ShapeDtypeStruct((9, channels, channels), jnp.bfloat16),
        jax.ShapeDtypeStruct((16, channels), jnp.float32),
    ]
    if keep_back:
        out_specs.append(stream)
        out_shape.append(jax.ShapeDtypeStruct(x.shape, jnp.bfloat16))
    return pl.pallas_call(
        functools.partial(weight_kernel, steps, keep_back),
        grid=(steps + 9,),
        in_specs=[stream, stream, stream, fixed(8, channels), fixed(channels, 1)],
        out_specs=tuple(out_specs),
        out_shape=tuple(out_shape),
        scratch_shapes=[
            pltpu.VMEM((images, height + 2 * DILATION_STEP, width, 3 * channels), jnp.bfloat16),
            pltpu.VMEM((images, height, width, channels), jnp.bfloat16),
        ],
        compiler_params=PARAMS,
        name="weight_grad",
    )(x, upstream.reshape(x.shape), y.reshape(x.shape), vectors, mean.reshape(channels, 1))


def act_grad_kernel(steps, tiles, back_ref, y_ref, v_ref, w_ref, up_ref, sums, wide):
    g = pl.program_id(0)

    @pl.when(g == 0)
    def _():
        clear_edges(wide)
        sums[...] = jnp.zeros_like(sums)

    @pl.when(g < steps)
    def _():
        per = steps // wide.shape[0]

        def one(i, carry):
            spread_columns(
                wide,
                g // per,
                lax.rem(g, per) * CHUNK + 3 * i,
                back_ref[0, pl.ds(3 * i, 3)].astype(jnp.float32),
            )
            return carry

        lax.fori_loop(0, CHUNK // 3, one, 0)

    @pl.when(g >= steps)
    def _():
        per = tiles // wide.shape[0]
        t = g - steps
        grad = conv_tile_back(wide, w_ref, t // per, lax.rem(t, per) * TILE, TILE)
        centered = (y_ref[...] - v_ref[0:1]) * v_ref[1:2]
        upstream = grad * silu_slope(v_ref[2:3] * centered + v_ref[3:4])
        up_ref[...] = upstream
        add_sums(sums, upstream, upstream * centered)


def act_grad_call(back, y, vectors, weights):
    images, height, width, channels = back.shape
    steps, tiles, stream, rows = map_specs(*back.shape)
    pixels = images * height * width
    return pl.pallas_call(
        functools.partial(act_grad_kernel, steps, tiles),
        grid=(steps + tiles,),
        in_specs=[stream, rows, fixed(8, channels), layer_spec(weights, 1)],
        out_specs=(rows, fixed(8, channels)),
        out_shape=(
            jax.ShapeDtypeStruct((pixels, channels), jnp.float32),
            jax.ShapeDtypeStruct((8, channels), jnp.float32),
        ),
        scratch_shapes=[
            pltpu.VMEM((images, height + 2 * DILATION_STEP, width, 3 * channels), jnp.bfloat16)
        ],
        compiler_params=PARAMS,
        name="act_grad",
    )(back, y, vectors, weights)


def update_kernel(
    place_ref, g_ref, rows_ref, cols_ref, left_ref, right_ref, master_ref, lroot_ref, rroot_ref,
    grad_out, left_out, right_out, master_out, copy_out, gram,
):
    parts = g_ref.shape[1]
    shard_rows = left_ref.shape[1]
    full = jnp.concatenate([g_ref[0, part] for part in range(parts)], axis=1)
    rows = jnp.concatenate([rows_ref[0, part] for part in range(parts)], axis=1)
    grad_out[0] = rows.astype(jnp.float32)
    left_out[0] = 0.5 * left_ref[0] + 0.5 * dot(rows, full, CONTRACT_COLS)
    gram[...] = dot(cols_ref[0, 0], full, CONTRACT_ROWS)
    right_out[0] = 0.5 * right_ref[0] + 0.5 * gram[
        pl.ds(pl.multiple_of(place_ref[2], 8), shard_rows)
    ]
    turned = dot(lroot_ref[0].astype(jnp.bfloat16), full).astype(jnp.bfloat16)
    step = dot(turned, rroot_ref[0].astype(jnp.bfloat16))
    master = master_ref[0]
    master = master - RATE_TRUNK * (step + WEIGHT_DECAY * master)
    master_out[0] = master
    copy_out[0] = master.astype(jnp.bfloat16)


def update_call(owner, combined, left, right, master, lroot, rroot):
    layers, taps, shard_rows, channels = left.shape
    count, parts, _, width = combined.shape
    one = pl.BlockSpec((1, shard_rows, channels), lambda g, place: (g, 0, 0))
    whole = pl.BlockSpec((1, channels, channels), lambda g, place: (g, 0, 0))
    flat = (count, shard_rows, channels)
    start = owner * shard_rows
    place = jnp.stack([owner, start // width, lax.rem(start, width)]).astype(jnp.int32)
    outs = pl.pallas_call(
        update_kernel,
        grid_spec=pltpu.PrefetchScalarGridSpec(
            num_scalar_prefetch=1,
            grid=(count,),
            in_specs=[
                pl.BlockSpec((1, parts, channels, width), lambda g, place: (g, 0, 0, 0)),
                pl.BlockSpec((1, parts, shard_rows, width), lambda g, place: (g, 0, place[0], 0)),
                pl.BlockSpec((1, 1, channels, width), lambda g, place: (g, place[1], 0, 0)),
                one,
                one,
                one,
                one,
                whole,
            ],
            out_specs=(one,) * 5,
            scratch_shapes=[pltpu.VMEM((width, channels), jnp.float32)],
        ),
        out_shape=tuple(
            jax.ShapeDtypeStruct(flat, kind)
            for kind in (jnp.float32, jnp.float32, jnp.float32, jnp.float32, jnp.bfloat16)
        ),
        compiler_params=PARAMS,
        name="update",
    )(
        place,
        combined,
        combined,
        combined,
        left.reshape(flat),
        right.reshape(flat),
        master.reshape(flat),
        lroot.reshape(flat),
        rroot.reshape(count, channels, channels),
    )
    return [out.reshape(left.shape) for out in outs]


FAR = ("task", 2)
CORE = ("task", 1)


def owner_bits(members):
    bits = []
    bit = members // 2
    while bit:
        bits.append(("dp", bit))
        bit //= 2
    return bits


def partner(dim):
    axis, bit = dim
    me = lax.axis_index(axis)
    mine = lax.rem(me // bit, 2)
    return mine, {axis: me + bit * (1 - 2 * mine)}


def greet(dims):
    barrier = pltpu.get_barrier_semaphore()
    for dim in dims:
        pl.semaphore_signal(
            barrier, inc=1, device_id=partner(dim)[1], device_id_type=pl.DeviceIdType.MESH
        )
    pl.semaphore_wait(barrier, len(dims))


def gather_kernel(plans, dims, split, *refs):
    count = len(plans)
    ins, outs = refs[:count], refs[count : 2 * count]
    local_sem, send_sem, recv_sem = refs[2 * count :]
    greet(dims[0])
    task = lax.axis_index("task")
    entries = [
        (array, start, rows, order)
        for array, (plan, _) in enumerate(plans)
        for start, rows, order in plan
    ]
    group_of, groups = [], 0
    for plan, width in plans:
        group_of += [groups + i // width for i in range(len(plan))]
        groups = group_of[-1] + 1

    def held(array, start, rows, free):
        return (pl.ds(start, rows),) + tuple(
            slice(None) if dim in free else partner(dim)[0] for dim in dims[array]
        )

    placed = []
    for index, (array, start, rows, order) in enumerate(entries):
        source = ins[array].at[pl.ds(start, rows)]
        target = held(array, start, rows, ())
        pairs = []
        if not split[array]:
            pairs.append((source, target))
        elif FAR in order:
            column = pl.multiple_of(task * 128, 128)
            pairs.append((ins[array].at[pl.ds(start, rows), :, pl.ds(column, 128)], target))
        else:
            for half in range(2):
                column = pl.multiple_of((lax.rem(task, 2) + 2 * half) * 128, 128)
                pairs.append(
                    (
                        ins[array].at[pl.ds(start, rows), :, pl.ds(column, 128)],
                        (target[0], half) + target[2:],
                    )
                )
        copies = [
            pltpu.make_async_copy(source, outs[array].at[target], local_sem.at[index, i])
            for i, (source, target) in enumerate(pairs)
        ]
        for copy in copies:
            copy.start()
        placed.append(copies)
    depth = max(len(entry[3]) for entry in entries)
    started = {}
    for step in range(groups + depth):
        for stage in range(depth, -1, -1):
            for index, (array, start, rows, order) in enumerate(entries):
                if group_of[index] != step - stage or stage > len(order):
                    continue
                if stage == 0:
                    for copy in placed[index]:
                        copy.wait()
                else:
                    started[index, stage - 1].wait_recv()
                if stage < len(order):
                    free = set(order[:stage]) | {d for d in dims[array] if d not in order}
                    where = held(array, start, rows, free)
                    copy = pltpu.make_async_remote_copy(
                        src_ref=outs[array].at[where],
                        dst_ref=outs[array].at[where],
                        send_sem=send_sem.at[index, stage],
                        recv_sem=recv_sem.at[index, stage],
                        device_id=partner(order[stage])[1],
                        device_id_type=pl.DeviceIdType.MESH,
                    )
                    copy.start()
                    started[index, stage] = copy
    for copy in started.values():
        copy.wait_send()


def gather(arrays, plans, dims, split, identity):
    shapes = [
        (x.shape[0],) + (2,) * len(d) + (x.shape[1], 128 if cut else x.shape[2])
        for x, d, cut in zip(arrays, dims, split)
    ]
    entries = sum(len(plan) for plan, _ in plans)
    depth = max(len(d) for d in dims)
    outs = pl.pallas_call(
        functools.partial(gather_kernel, plans, dims, split),
        out_shape=tuple(
            jax.ShapeDtypeStruct(shape, x.dtype) for shape, x in zip(shapes, arrays)
        ),
        in_specs=[pl.BlockSpec(memory_space=pl.ANY)] * len(arrays),
        out_specs=(pl.BlockSpec(memory_space=pl.ANY),) * len(arrays),
        scratch_shapes=[
            pltpu.SemaphoreType.DMA((entries, 2)),
            pltpu.SemaphoreType.DMA((entries, depth)),
            pltpu.SemaphoreType.DMA((entries, depth)),
        ],
        compiler_params=pltpu.CompilerParams(collective_id=identity, has_side_effects=True),
        name="gather",
    )(*arrays)
    return outs


def spread(orders, taps, width):
    rows = taps // len(orders)
    return [(i * rows, rows, order) for i, order in enumerate(orders)], width


def gather_weights(trunk, head, identity):
    members = lax.axis_size("dp")
    bits = owner_bits(members)
    quarters = tuple(bits) + (FAR, CORE)
    halves = tuple(bits) + (CORE,)
    layers, taps, shard_rows, channels = trunk.shape
    trunk_plan = spread([quarters, halves, quarters] * 6, layers * taps, 6)
    head_plan = spread([tuple(bits)], 2, 1)
    full, heads = gather(
        [trunk.reshape(layers * taps, shard_rows, channels), head[0]],
        [trunk_plan, head_plan],
        [[FAR, CORE] + bits, bits],
        [True, False],
        identity,
    )
    return (
        full.reshape(layers * taps, TASKS, channels, 128),
        heads.reshape(2, channels, head.shape[3]),
    )


def gather_combined(quarter, identity):
    members = lax.axis_size("dp")
    bits = owner_bits(members)
    last = bits[-1:]
    plain = tuple(bits) + (FAR, CORE)
    other = tuple(bits[:-1]) + (FAR,) + tuple(last) + (CORE,)
    early = tuple(last) + (FAR,) + tuple(bits[:-1]) + (CORE,)
    first = (FAR,) + tuple(last) + tuple(bits[:-1]) + (CORE,)
    taps, shard_rows, width = quarter.shape
    (full,) = gather(
        [quarter],
        [spread([plain, other, plain, other, early, first] * 3, taps, 6)],
        [[FAR, CORE] + bits],
        [False],
        identity,
    )
    return full.reshape(taps, TASKS, members * shard_rows, width)


def small_sum_kernel(members, x_ref, out_ref, slots, send_sem, recv_sem):
    me = lax.axis_index("dp")
    barrier = pltpu.get_barrier_semaphore()
    for k in range(1, members):
        pl.semaphore_signal(
            barrier,
            inc=1,
            device_id={"dp": lax.rem(me + k, members)},
            device_id_type=pl.DeviceIdType.MESH,
        )
    pl.semaphore_wait(barrier, members - 1)
    copies = []
    for k in range(1, members):
        copy = pltpu.make_async_remote_copy(
            src_ref=x_ref,
            dst_ref=slots.at[me],
            send_sem=send_sem.at[k],
            recv_sem=recv_sem.at[me],
            device_id={"dp": lax.rem(me + k, members)},
            device_id_type=pl.DeviceIdType.MESH,
        )
        copy.start()
        copies.append(copy)
    slots[me] = x_ref[...]
    for k in range(1, members):
        source = lax.rem(me + k, members)
        pltpu.make_async_remote_copy(
            src_ref=x_ref,
            dst_ref=slots.at[source],
            send_sem=send_sem.at[k],
            recv_sem=recv_sem.at[source],
            device_id={"dp": source},
            device_id_type=pl.DeviceIdType.MESH,
        ).wait_recv()
    total = slots[0]
    for k in range(1, members):
        total = total + slots[k]
    out_ref[...] = total
    for copy in copies:
        copy.wait_send()


def small_sum(x, identity):
    members = lax.axis_size("dp")
    return pl.pallas_call(
        functools.partial(small_sum_kernel, members),
        out_shape=jax.ShapeDtypeStruct(x.shape, jnp.float32),
        in_specs=[pl.BlockSpec(memory_space=pltpu.VMEM)],
        out_specs=pl.BlockSpec(memory_space=pltpu.VMEM),
        scratch_shapes=[
            pltpu.VMEM((members,) + x.shape, jnp.float32),
            pltpu.SemaphoreType.DMA((members,)),
            pltpu.SemaphoreType.DMA((members,)),
        ],
        compiler_params=pltpu.CompilerParams(collective_id=identity, has_side_effects=True),
        name="small_sum",
    )(x)


def scatter_sum(parts):
    members = lax.axis_size("dp")
    me = lax.axis_index("dp")
    taps, channels, width = parts.shape
    held = parts.reshape(taps, members, channels // members, width)
    bit = 1
    while bit < members:
        held = held.reshape(taps, -1, 2, channels // members, width)
        mine = lax.rem(me // bit, 2)
        other = lax.dynamic_index_in_dim(held, 1 - mine, 2, keepdims=False)
        keep = lax.dynamic_index_in_dim(held, mine, 2, keepdims=False)
        other = lax.ppermute(
            other.astype(jnp.bfloat16), "dp", [(i, i ^ bit) for i in range(members)]
        )
        held = keep.astype(jnp.float32) + other.astype(jnp.float32)
        bit *= 2
    return held.reshape(taps, channels // members, width)


def pad_rows(parts, rows):
    used = sum(part.shape[0] for part in parts)
    if used < rows:
        parts = list(parts) + [jnp.zeros((rows - used, parts[0].shape[1]), jnp.float32)]
    return jnp.concatenate(parts)


def norm_vectors(totals, gain, shift, pixels):
    center = totals[0] / pixels
    inverse = lax.rsqrt(totals[1] / pixels - center * center + NORM_EPS)
    return center, inverse, gain, shift


def stack_vectors(parts):
    zero = jnp.zeros_like(parts[0])
    return jnp.stack(list(parts) + [zero] * (8 - len(parts)))


def boundary(labels):
    across = jnp.pad(
        (labels[:, :, 1:] != labels[:, :, :-1]).astype(jnp.float32), ((0, 0), (0, 0), (0, 1))
    )
    downward = jnp.pad(
        (labels[:, 1:, :] != labels[:, :-1, :]).astype(jnp.float32), ((0, 0), (0, 1), (0, 0))
    )
    return jnp.maximum(across, downward)


def pixel_data(labels, depth_mask, depth_target, normal_target, scene_ids, task_weights):
    images, feature_rows, feature_columns = labels.shape
    choose = (scene_ids[:, None] == jnp.arange(task_weights.shape[0])[None, :]).astype(jnp.float32)
    per_image = jnp.dot(choose, task_weights, precision=PRECISE)
    return (
        labels.reshape(-1),
        depth_mask.reshape(-1).astype(jnp.float32),
        boundary(labels).reshape(-1),
        depth_target.reshape(-1),
        jnp.transpose(normal_target, (0, 2, 3, 1)).reshape(-1, 3),
        jnp.repeat(per_image, feature_rows * feature_columns, axis=0),
    )


def task_sums(logits, pixel_info):
    labels, valid_mask, edge_target, depth_values, normals, weights = pixel_info
    classes = logits[:, :CLASSES]
    largest = jnp.max(classes, axis=1, keepdims=True)
    spread = jnp.log(jnp.sum(jnp.exp(classes - largest), axis=1)) + largest[:, 0]
    picked = jnp.sum(
        jnp.where(labels[:, None] == jnp.arange(CLASSES)[None, :], classes, 0.0), axis=1
    )
    segment = jnp.sum(weights[:, 0] * (spread - picked))
    offset = logits[:, CLASSES] - depth_values
    distance = jnp.sum(weights[:, 1] * valid_mask * (jnp.sqrt(offset * offset + 1.0) - 1.0))
    predicted = logits[:, CLASSES + 1 : CLASSES + 4]
    cosine = jnp.sum(predicted * normals, axis=1) * lax.rsqrt(
        (jnp.sum(predicted * predicted, axis=1) + 1.0) * (jnp.sum(normals * normals, axis=1) + 1.0)
    )
    surface = jnp.sum(weights[:, 2] * (1.0 - cosine))
    edge_logit = logits[:, CLASSES + 4]
    contour = jnp.sum(weights[:, 3] * (jax.nn.softplus(edge_logit) - edge_target * edge_logit))
    return jnp.stack([segment, distance, surface, contour])


def combine_weights(pair_products, conflict):
    offdiagonal = (1.0 - jnp.eye(TASKS, dtype=jnp.float32)) * conflict.astype(jnp.float32)
    ratios = offdiagonal * pair_products / (jnp.diagonal(pair_products)[None, :] + GRAM_EPS)
    return 1.0 - jnp.sum(ratios, axis=0)


def adamw_update(gradient, moment_one, moment_two, weight, rate):
    moment_one = 0.5 * moment_one + 0.5 * gradient
    moment_two = 0.5 * moment_two + 0.5 * gradient * gradient
    correction = 1.0 - 0.5**STEP
    weight = weight - rate * (
        moment_one / correction / (jnp.sqrt(moment_two / correction) + ADAM_EPS)
        + WEIGHT_DECAY * weight
    )
    return (moment_one, moment_two, weight)


def body(
    features,
    labels,
    depth_mask,
    depth_target,
    normal_target,
    scene_ids,
    task_weights,
    conflict,
    trunk_copy,
    trunk_master,
    trunk_left,
    trunk_right,
    left_root,
    right_root,
    head_copy,
    head_master,
    head_first,
    head_second,
    out_copy,
    out_master,
    out_first,
    out_second,
    trunk_gains,
    gains_first,
    gains_second,
    head_bias,
    bias_first,
    bias_second,
):
    images, feature_rows, feature_columns, channels = features.shape
    pixels = jnp.array(images * feature_rows * feature_columns * lax.axis_size("dp"), jnp.float32)
    task_index = lax.axis_index("task")
    owner_index = lax.axis_index("dp")
    trunk_full, head_full = gather_weights(trunk_copy, head_copy, 5)
    pixel_info = pixel_data(
        labels, depth_mask, depth_target, normal_target, scene_ids, task_weights
    )
    local_valid = jnp.sum(pixel_info[1])
    first_conv, first_sums = first_conv_call(features, trunk_full)
    first_totals = small_sum(
        pad_rows([first_sums[:3], jnp.full((1, channels), local_valid)], 8), 0
    )
    valid_count = first_totals[3, 0]
    first_norm = norm_vectors(first_totals, trunk_gains[0], trunk_gains[1], pixels)
    second_conv, first_act, second_sums = second_conv_call(
        first_conv, stack_vectors(first_norm), trunk_full, features.shape
    )
    second_totals = small_sum(second_sums, 1)
    second_norm = norm_vectors(second_totals, trunk_gains[2], trunk_gains[3], pixels)
    second_center = (second_conv - second_norm[0]) * second_norm[1]
    residual_in = (
        trunk_gains[2] * second_center + trunk_gains[3] + features.reshape(-1, channels)
    )
    trunk_out = jax.nn.silu(residual_in).astype(jnp.bfloat16)
    pooled = jnp.mean(trunk_out.reshape(images, -1, channels), axis=1, dtype=jnp.float32).astype(
        jnp.bfloat16
    )
    selector = (jnp.arange(TASKS) == task_index).astype(jnp.float32)
    own_bias = jnp.dot(selector, head_bias, precision=PRECISE)
    head_pre = jnp.dot(trunk_out, head_full[0], preferred_element_type=jnp.float32).reshape(
        images, -1, BRANCH_WIDTH
    )
    head_pre = (
        head_pre
        + jnp.dot(pooled, head_full[1], preferred_element_type=jnp.float32)[:, None, :]
        + own_bias
    )
    head_pre = head_pre.reshape(-1, BRANCH_WIDTH)
    hidden_act = jax.nn.silu(head_pre).astype(jnp.bfloat16)
    logits = jnp.dot(hidden_act, out_copy, preferred_element_type=jnp.float32)
    totals, pullback = jax.vjp(lambda tap_values: task_sums(tap_values, pixel_info), logits)
    logit_grad = pullback(selector)[0].astype(jnp.bfloat16)
    out_grad = dot(hidden_act, logit_grad, CONTRACT_ROWS)
    hidden_grad = dot(logit_grad, out_copy, CONTRACT_COLS)
    pre_grad = (hidden_grad * silu_slope(head_pre)).astype(jnp.bfloat16)
    bias_grad = jnp.sum(pre_grad, axis=0, dtype=jnp.float32)
    per_image = jnp.sum(pre_grad.reshape(images, -1, BRANCH_WIDTH), axis=1, dtype=jnp.float32)
    input_grad = dot(trunk_out, pre_grad, CONTRACT_ROWS)
    pool_grad = jnp.dot(pooled.astype(jnp.float32).T, per_image, precision=PRECISE)
    pooled_back = jnp.dot(per_image, head_full[1].astype(jnp.float32).T, precision=PRECISE)
    out_back = dot(pre_grad, head_full[0], CONTRACT_COLS)
    out_back = (
        out_back.reshape(images, -1, channels)
        + pooled_back[:, None, :] / (feature_rows * feature_columns)
    ).reshape(-1, channels)
    head_sum = scatter_sum(jnp.concatenate([input_grad, pool_grad], axis=1)[None])
    second_up = out_back * silu_slope(residual_in)
    second_back_sums = small_sum(
        pad_rows(
            [
                jnp.sum(second_up, axis=0, keepdims=True),
                jnp.sum(second_up * second_center, axis=0, keepdims=True),
            ],
            8,
        ),
        2,
    )[:2]
    second_mean = second_totals[2] / pixels
    second_weight, second_edges, second_back = weight_grad_call(
        first_act,
        second_up,
        second_conv,
        stack_vectors(second_norm + tuple(second_back_sums / pixels)),
        second_mean,
        True,
    )
    second_sum = scatter_sum(second_weight)
    first_up, first_up_sums = act_grad_call(
        second_back, first_conv, stack_vectors(first_norm), trunk_full
    )
    first_back_sums = small_sum(first_up_sums, 3)[:2]
    first_mean = first_totals[2] / pixels
    first_weight, first_edges = weight_grad_call(
        features,
        first_up,
        first_conv,
        stack_vectors(first_norm + tuple(first_back_sums / pixels)),
        first_mean,
        False,
    )
    first_sum = scatter_sum(first_weight)
    edges = small_sum(jnp.concatenate([first_edges, second_edges]), 4).reshape(2, 16, 1, channels)
    means = jnp.stack([first_mean, second_mean])
    shard_rows = trunk_copy.shape[2]
    own_means = lax.dynamic_slice_in_dim(means, owner_index * shard_rows, shard_rows, 1)
    removed = (own_means[:, None, :, None] * edges[:, :9]).reshape(18, shard_rows, channels)
    leading = (owner_index == 0).astype(jnp.float32)
    gains_part = (
        selector[:, None, None]
        * (
            leading
            * jnp.stack(
                [first_back_sums[1], first_back_sums[0], second_back_sums[1], second_back_sums[0]]
            )
        )[None]
    )
    bias_part = selector[:, None] * bias_grad[None]
    loss_part = totals * selector
    gains_sum, bias_sum, out_sum, loss_sum = lax.psum(
        (gains_part, bias_part, out_grad, loss_part), ("task", "dp")
    )
    divisor = jnp.stack([pixels, valid_count, pixels, pixels])
    own_divisor = jnp.sum(divisor * selector)
    gains_total = jnp.sum(gains_sum / divisor[:, None, None], axis=0)
    bias_total = bias_sum / divisor[:, None]
    column_divisor = jnp.concatenate(
        [jnp.full((CLASSES,), divisor[0]), divisor[1:2], jnp.full((3,), divisor[2]), divisor[3:4]]
    )
    out_total = out_sum / column_divisor[None, :]
    head_rows = jnp.stack(jnp.split(head_sum[0], 2, axis=1))[None]
    own_scaled = (
        (jnp.concatenate([first_sum, second_sum]) + removed) / own_divisor
    ).astype(jnp.bfloat16)
    taps, shard_rows = own_scaled.shape[:2]
    pieces = own_scaled.reshape(taps, shard_rows, TASKS, channels // TASKS)
    scaled = lax.all_to_all(pieces, "task", split_axis=2, concat_axis=0, tiled=False)
    scaled = scaled.reshape(TASKS, taps * shard_rows, channels // TASKS).astype(jnp.float32)
    products = {
        (i, j): jnp.sum(scaled[i] * scaled[j]) for i in range(TASKS) for j in range(i, TASKS)
    }
    pair_products = lax.psum(
        jnp.stack(
            [products[min(i, j), max(i, j)] for i in range(TASKS) for j in range(TASKS)]
        ).reshape(TASKS, TASKS),
        ("task", "dp"),
    )
    mixing = combine_weights(pair_products, conflict)
    quarter = jnp.sum(mixing[:, None, None] * scaled, axis=0).astype(jnp.bfloat16)
    quarter = quarter.reshape(taps, shard_rows, channels // TASKS)
    combined = gather_combined(quarter, 6)
    grad_rows, left_new, right_new, master_new, copy_new = update_call(
        owner_index, combined, trunk_left, trunk_right, trunk_master, left_root, right_root
    )
    head_one, head_two, head_new = adamw_update(
        head_rows / own_divisor, head_first, head_second, head_master, RATE_MATRIX
    )
    out_one, out_two, out_new = adamw_update(
        out_total, out_first, out_second, out_master, RATE_MATRIX
    )
    gain_one, gain_two, gain_new = adamw_update(
        gains_total, gains_first, gains_second, trunk_gains, RATE_VECTOR
    )
    bias_one, bias_two, bias_new = adamw_update(
        bias_total, bias_first, bias_second, head_bias, RATE_VECTOR
    )
    loss_terms = jnp.concatenate([loss_sum, valid_count[None]])
    return (
        grad_rows,
        left_new,
        right_new,
        master_new,
        copy_new,
        head_one,
        head_two,
        head_new,
        head_new.astype(jnp.bfloat16),
        out_one,
        out_two,
        out_new,
        out_new.astype(jnp.bfloat16),
        gain_one,
        gain_two,
        gain_new,
        bias_one,
        bias_two,
        bias_new,
        loss_terms,
        pair_products,
    )


def solution(mesh):
    rows = P(None, None, "dp", None)
    heads = P("task", None, "dp", None)
    images = P("dp")
    placed = (
        (images,) * 6
        + (P(), P())
        + (rows,) * 5
        + (P(),)
        + (heads,) * 4
        + (P(),) * 10
    )
    return jax.shard_map(
        body,
        mesh=mesh,
        in_specs=placed,
        out_specs=(rows,) * 5 + (heads,) * 4 + (P(),) * 12,
        check_vma=False,
    )
```

```python
import functools

import jax
import jax.numpy as jnp
from jax import lax
from jax.experimental import pallas as pl
from jax.experimental.pallas import tpu as pltpu
from jax.sharding import PartitionSpec as P

BRANCH_WIDTH = 256
CLASSES = 13
TASKS = 4
DILATION_STEP = 2
STEP = 5


PRECISE = lax.Precision.HIGHEST
NORM_EPS = 1e-05
RATE_TRUNK = 0.3
RATE_MATRIX = 0.05
RATE_VECTOR = 0.3
WEIGHT_DECAY = 0.01
ADAM_EPS = 1e-08
GRAM_EPS = 1e-12
PLAIN = (((1,), (0,)), ((), ()))
CONTRACT_ROWS = (((0,), (0,)), ((), ()))
CONTRACT_COLS = (((1,), (1,)), ((), ()))
CHUNK = 9
TILE = 12
VMEM_LIMIT = 58 * 1024 * 1024
PARAMS = pltpu.CompilerParams(vmem_limit_bytes=VMEM_LIMIT)


def summing(identity):
    return pltpu.CompilerParams(
        collective_id=identity, has_side_effects=True, vmem_limit_bytes=VMEM_LIMIT
    )


def silu_slope(tap_values):
    sigmoid = jax.nn.sigmoid(tap_values)
    return sigmoid * (1.0 + tap_values * (1.0 - sigmoid))


def dot(a, b, contract=PLAIN):
    return lax.dot_general(a, b, contract, preferred_element_type=jnp.float32)


def clear_edges(wide):
    rows = wide.shape[1]
    edge = jnp.zeros((wide.shape[0], DILATION_STEP) + wide.shape[2:], wide.dtype)
    wide[:, 0:DILATION_STEP] = edge
    wide[:, rows - DILATION_STEP : rows] = edge


def spread_columns(wide, image, row, values):
    width, channels = values.shape[1:]
    column = lax.broadcasted_iota(jnp.int32, (1, width, channels), 1)
    left = jnp.where(column >= DILATION_STEP, pltpu.roll(values, DILATION_STEP, 1), 0.0)
    right = jnp.where(
        column < width - DILATION_STEP, pltpu.roll(values, width - DILATION_STEP, 1), 0.0
    )
    place = pl.ds(DILATION_STEP + row, values.shape[0])
    for part, piece in enumerate((left, values, right)):
        wide[image, place, :, part * channels : (part + 1) * channels] = piece.astype(wide.dtype)


def window(wide, image, row, rows, kernel_row, part=None):
    channels = wide.shape[3] // 3
    place = pl.ds(row + DILATION_STEP * kernel_row, rows)
    if part is None:
        return wide[image, place].reshape(rows * wide.shape[2], 3 * channels)
    return wide[image, place, :, part * channels : (part + 1) * channels].reshape(
        rows * wide.shape[2], channels
    )


def conv_tile(wide, parts, image, row, rows):
    taps = jnp.concatenate([window(wide, image, row, rows, k) for k in range(3)], axis=1)
    parts = [part.reshape(-1, part.shape[-1]) for part in parts]
    return dot(taps, jnp.concatenate(parts, axis=1))


def conv_tile_back(wide, weights, image, row, rows):
    total = None
    for tap in range(9):
        kernel_row, kernel_column = divmod(tap, 3)
        part = dot(
            window(wide, image, row, rows, 2 - kernel_row, 2 - kernel_column),
            jnp.concatenate([weights[tap, part] for part in range(weights.shape[1])], axis=1),
            CONTRACT_COLS,
        )
        total = part if total is None else total + part
    return total


def peers(axis, members):
    me = lax.axis_index(axis)
    return [lax.rem(me + k, members) for k in range(1, members)]


def greet_peers(groups):
    signal_peers(groups)
    wait_peers(groups)


def share(axis, members, source, slots, send_sem, recv_sem):
    me = lax.axis_index(axis)
    copies = []
    for k, peer in enumerate(peers(axis, members)):
        copy = pltpu.make_async_remote_copy(
            src_ref=source(peer),
            dst_ref=slots.at[me],
            send_sem=send_sem.at[k],
            recv_sem=recv_sem.at[me],
            device_id={axis: peer},
            device_id_type=pl.DeviceIdType.MESH,
        )
        copy.start()
        copies.append(copy)
    return copies


def await_shares(axis, members, source, slots, send_sem, recv_sem):
    for k, peer in enumerate(peers(axis, members)):
        pltpu.make_async_remote_copy(
            src_ref=source(peer),
            dst_ref=slots.at[peer],
            send_sem=send_sem.at[k],
            recv_sem=recv_sem.at[peer],
            device_id={axis: peer},
            device_id_type=pl.DeviceIdType.MESH,
        ).wait_recv()


def await_sends(axis, members, source, slots, send_sem, recv_sem):
    for k, peer in enumerate(peers(axis, members)):
        pltpu.make_async_remote_copy(
            src_ref=source(peer),
            dst_ref=slots.at[peer],
            send_sem=send_sem.at[k],
            recv_sem=recv_sem.at[peer],
            device_id={axis: peer},
            device_id_type=pl.DeviceIdType.MESH,
        ).wait_send()


def slot_total(slots):
    total = slots[0]
    for k in range(1, slots.shape[0]):
        total = total + slots[k]
    return total


def signal_peers(groups):
    barrier = pltpu.get_barrier_semaphore()
    for axis, members in groups:
        for peer in peers(axis, members):
            pl.semaphore_signal(
                barrier, inc=1, device_id={axis: peer}, device_id_type=pl.DeviceIdType.MESH
            )


def wait_peers(groups):
    pl.semaphore_wait(pltpu.get_barrier_semaphore(), sum(members - 1 for _, members in groups))


def sum_over_owners(members, local, total, slots, send_sem, recv_sem):
    copies = share("dp", members, lambda peer: local, slots, send_sem, recv_sem)
    slots[lax.axis_index("dp")] = local[...]
    await_shares("dp", members, lambda peer: local, slots, send_sem, recv_sem)
    total[...] = slot_total(slots)
    for copy in copies:
        copy.wait_send()


def sum_scratch(members, rows, channels):
    return [
        pltpu.VMEM((rows, channels), jnp.float32),
        pltpu.VMEM((members, rows, channels), jnp.float32),
        pltpu.SemaphoreType.DMA((members,)),
        pltpu.SemaphoreType.DMA((members,)),
    ]


def pixel_count(wide, members):
    images, padded, width, _ = wide.shape
    return float(images * (padded - 2 * DILATION_STEP) * width * members)


def norm_rows(sums_ref, gain_ref, layer, pixels):
    center = sums_ref[0:1] / pixels
    inverse = lax.rsqrt(sums_ref[1:2] / pixels - center * center + NORM_EPS)
    return center, inverse, gain_ref[2 * layer : 2 * layer + 1], gain_ref[2 * layer + 1 : 2 * layer + 2]


def add_sums(sums, first, second):
    sums[0:1] += jnp.sum(first, axis=0, keepdims=True)
    sums[1:2] += jnp.sum(second, axis=0, keepdims=True)


FAR = ("task", 2)
CORE = ("task", 1)


def owner_bits(members):
    bits = []
    bit = members // 2
    while bit:
        bits.append(("dp", bit))
        bit //= 2
    return bits


def partner(dim):
    axis, bit = dim
    me = lax.axis_index(axis)
    mine = lax.rem(me // bit, 2)
    return mine, {axis: me + bit * (1 - 2 * mine)}


class Gather:
    def __init__(self, plans, dims, split, ins, outs, local_sem, send_sem, recv_sem):
        self.dims, self.split, self.ins, self.outs = dims, split, ins, outs
        self.local_sem, self.send_sem, self.recv_sem = local_sem, send_sem, recv_sem
        self.entries = [
            (array, start, rows, order)
            for array, (plan, _) in enumerate(plans)
            for start, rows, order in plan
        ]
        self.group_of, groups = [], 0
        for array, (plan, width) in enumerate(plans):
            late = groups + (2 if array == 1 else 0)
            self.group_of += [late + i // width for i in range(len(plan))]
            groups = self.group_of[-1] + 1
        self.depth = max(len(entry[3]) for entry in self.entries)
        self.steps = groups + self.depth

    def held(self, array, start, rows, free):
        return (pl.ds(start, rows),) + tuple(
            slice(None) if dim in free else partner(dim)[0] for dim in self.dims[array]
        )

    def placements(self, index):
        array, start, rows, order = self.entries[index]
        target = self.held(array, start, rows, ())
        source = self.ins[array]
        task = lax.axis_index("task")
        if not self.split[array]:
            pairs = [(source.at[pl.ds(start, rows)], target)]
        else:
            halves_of = [None] if FAR in order else [0, 1]
            pairs = []
            for half in halves_of:
                column = task if half is None else lax.rem(task, 2) + 2 * half
                column = pl.multiple_of(column * 128, 128)
                place = target if half is None else (target[0], half) + target[2:]
                pairs.append((source.at[pl.ds(start, rows), :, pl.ds(column, 128)], place))
        return [
            pltpu.make_async_copy(source, self.outs[array].at[place], self.local_sem.at[index, i])
            for i, (source, place) in enumerate(pairs)
        ]

    def copy_of(self, index, stage):
        array, start, rows, order = self.entries[index]
        free = set(order[:stage]) | {d for d in self.dims[array] if d not in order}
        where = self.held(array, start, rows, free)
        return pltpu.make_async_remote_copy(
            src_ref=self.outs[array].at[where],
            dst_ref=self.outs[array].at[where],
            send_sem=self.send_sem.at[index, stage],
            recv_sem=self.recv_sem.at[index, stage],
            device_id=partner(order[stage])[1],
            device_id_type=pl.DeviceIdType.MESH,
        )

    def place(self):
        for index in range(len(self.entries)):
            for copy in self.placements(index):
                copy.start()

    def step(self, step):
        for stage in range(self.depth, -1, -1):
            for index, (array, start, rows, order) in enumerate(self.entries):
                if self.group_of[index] != step - stage or stage > len(order):
                    continue
                if stage == 0:
                    for copy in self.placements(index):
                        copy.wait()
                else:
                    self.copy_of(index, stage - 1).wait_recv()
                if stage < len(order):
                    self.copy_of(index, stage).start()

    def finish(self):
        for index, entry in enumerate(self.entries):
            for stage in range(len(entry[3])):
                self.copy_of(index, stage).wait_send()

    def run(self):
        self.place()
        for step in range(self.steps):
            self.step(step)
        self.finish()


def spread(orders, taps, width):
    rows = taps // len(orders)
    return [(i * rows, rows, order) for i, order in enumerate(orders)], width


def weight_plans(members, taps):
    bits = owner_bits(members)
    quarters = tuple(bits) + (FAR, CORE)
    halves_only = tuple(bits) + (CORE,)
    trunk_plan = spread([quarters, halves_only, quarters] * 3, taps, 3)
    head_plan = spread([tuple(bits)], 2, 1)
    digits = [FAR, CORE] + bits
    return [trunk_plan, trunk_plan, head_plan], [digits, digits, bits], [True, True, False]


def first_kernel(
    members, steps, tiles, layout, x_ref, trunk_ref, head_ref, note_ref, conv_ref, total, full_ref,
    heads_ref, wide, weights, local_sem, send_sem, recv_sem, *exchange,
):
    g = pl.program_id(0)
    sums = exchange[0]
    moving = Gather(
        *layout,
        [trunk_ref.at[0], trunk_ref.at[1], head_ref],
        [weights, full_ref, heads_ref],
        local_sem,
        send_sem,
        recv_sem,
    )

    @pl.when(g == 0)
    def _():
        greet_peers([("dp", members), ("task", TASKS)])
        moving.place()
        clear_edges(wide)
        sums[...] = note_ref[...]

    spread_over = steps + tiles - 1
    ready = 3 + moving.depth
    for step in range(moving.steps):
        if step < ready:
            at = step * steps // ready
        else:
            at = steps + min(step - ready, tiles - 1)

        @pl.when(g == at)
        def _():
            moving.step(step)

    @pl.when(g < steps)
    def _():
        per = steps // wide.shape[0]

        def one(i, carry):
            spread_columns(
                wide,
                g // per,
                lax.rem(g, per) * CHUNK + 3 * i,
                x_ref[0, pl.ds(3 * i, 3)].astype(jnp.float32),
            )
            return carry

        lax.fori_loop(0, CHUNK // 3, one, 0)
        sums[2:3] += jnp.sum(x_ref[0].astype(jnp.float32), axis=(0, 1))[None]

    @pl.when(g >= steps)
    def _():
        per = tiles // wide.shape[0]
        t = g - steps
        parts = [weights[:, i, j] for i in range(2) for j in range(2)]
        conv = conv_tile(wide, parts, t // per, lax.rem(t, per) * TILE, TILE)
        conv_ref[...] = conv
        add_sums(sums, conv, conv * conv)

    @pl.when(g == spread_over)
    def _():
        moving.finish()
        sum_over_owners(members, sums, total, *exchange[1:])


def second_kernel(
    members, steps, tiles, y_ref, t_ref, n_ref, w_ref, conv_ref, act_ref, total, wide, *exchange
):
    g = pl.program_id(0)
    sums = exchange[0]

    @pl.when(g == 0)
    def _():
        signal_peers([("dp", members)])
        clear_edges(wide)
        sums[...] = jnp.zeros_like(sums)

    @pl.when(g < steps)
    def _():
        per = steps // wide.shape[0]
        center, inverse, gain, shift = norm_rows(t_ref, n_ref, 0, pixel_count(wide, members))

        def one(i, carry):
            values = y_ref[0, pl.ds(3 * i, 3)]
            normed = gain * ((values - center) * inverse) + shift
            act = jax.nn.silu(normed).astype(jnp.bfloat16)
            act_ref[0, pl.ds(3 * i, 3)] = act
            act = act.astype(jnp.float32)
            spread_columns(wide, g // per, lax.rem(g, per) * CHUNK + 3 * i, act)
            sums[2:3] += jnp.sum(act, axis=(0, 1))[None]
            return carry

        lax.fori_loop(0, CHUNK // 3, one, 0)

    @pl.when(g >= steps)
    def _():
        per = tiles // wide.shape[0]
        t = g - steps
        parts = [w_ref[:, part] for part in range(w_ref.shape[1])]
        conv = conv_tile(wide, parts, t // per, lax.rem(t, per) * TILE, TILE)
        conv_ref[...] = conv
        add_sums(sums, conv, conv * conv)

    @pl.when(g == steps + tiles - 1)
    def _():
        wait_peers([("dp", members)])
        sum_over_owners(members, sums, total, *exchange[1:])


def map_specs(images, height, width, channels):
    per = height // CHUNK
    steps = images * per
    stream = pl.BlockSpec(
        (1, CHUNK, width, channels),
        lambda g: (jnp.minimum(g, steps - 1) // per, lax.rem(jnp.minimum(g, steps - 1), per), 0, 0),
    )
    rows = pl.BlockSpec((TILE * width, channels), lambda g: (jnp.maximum(g - steps, 0), 0))
    return steps, images * (height // TILE), stream, rows


def fixed(*shape):
    return pl.BlockSpec(shape, lambda g: (0,) * len(shape))


def first_conv_call(x, trunk, head, note, identity):
    images, height, width, channels = x.shape
    steps, tiles, stream, rows = map_specs(*x.shape)
    pixels = images * height * width
    members = lax.axis_size("dp")
    layers, taps, shard_rows, _ = trunk.shape
    layout = weight_plans(members, taps)
    plans, dims, _ = layout
    entries = sum(len(plan) for plan, _ in plans)
    depth = max(len(digits) for digits in dims)
    matrix = (taps,) + (2,) * len(dims[0]) + (shard_rows, 128)
    branch = head.shape[3]
    anywhere = pl.BlockSpec(memory_space=pl.ANY)
    conv, total, full, heads = pl.pallas_call(
        functools.partial(first_kernel, members, steps, tiles, layout),
        grid=(steps + tiles,),
        in_specs=[stream, anywhere, anywhere, fixed(*note.shape)],
        out_specs=(rows, fixed(*note.shape), anywhere, anywhere),
        out_shape=(
            jax.ShapeDtypeStruct((pixels, channels), jnp.float32),
            jax.ShapeDtypeStruct(note.shape, jnp.float32),
            jax.ShapeDtypeStruct(matrix, trunk.dtype),
            jax.ShapeDtypeStruct((2,) + (2,) * len(dims[2]) + (shard_rows, branch), head.dtype),
        ),
        scratch_shapes=[
            pltpu.VMEM((images, height + 2 * DILATION_STEP, width, 3 * channels), jnp.bfloat16),
            pltpu.VMEM(matrix, trunk.dtype),
            pltpu.SemaphoreType.DMA((entries, 2)),
            pltpu.SemaphoreType.DMA((entries, depth)),
            pltpu.SemaphoreType.DMA((entries, depth)),
        ]
        + sum_scratch(members, note.shape[0], channels),
        compiler_params=summing(identity),
        name="first_conv",
    )(x, trunk, head[0], note)
    full = full.reshape(taps, TASKS, channels, 128)
    return conv, total, full, heads.reshape(2, channels, branch)


def second_conv_call(y, totals, gains, weights, shape, identity):
    images, height, width, channels = shape
    steps, tiles, stream, rows = map_specs(*shape)
    pixels = images * height * width
    members = lax.axis_size("dp")
    return pl.pallas_call(
        functools.partial(second_kernel, members, steps, tiles),
        grid=(steps + tiles,),
        in_specs=[stream, fixed(8, channels), fixed(4, channels), fixed(*weights.shape)],
        out_specs=(rows, stream, fixed(8, channels)),
        out_shape=(
            jax.ShapeDtypeStruct((pixels, channels), jnp.float32),
            jax.ShapeDtypeStruct(shape, jnp.bfloat16),
            jax.ShapeDtypeStruct((8, channels), jnp.float32),
        ),
        scratch_shapes=[
            pltpu.VMEM((images, height + 2 * DILATION_STEP, width, 3 * channels), jnp.bfloat16)
        ]
        + sum_scratch(members, 8, channels),
        compiler_params=summing(identity),
        name="second_conv",
    )(y.reshape(shape), totals, gains, weights)


def deltas(
    g, steps, members, layer, x_ref, up_ref, y_ref, t_ref, n_ref, b_ref, edge_ref, back_ref, wide, back
):
    images, padded, width, channels = wide.shape
    channels = channels // 3
    height = padded - 2 * DILATION_STEP

    @pl.when(g == 0)
    def _():
        clear_edges(wide)
        edge_ref[...] = jnp.zeros_like(edge_ref)

    @pl.when(g < steps)
    def _():
        per = steps // images
        column = lax.broadcasted_iota(jnp.int32, (1, 8, channels), 1)
        pixels = pixel_count(wide, members)
        center, inverse, gain, _ = norm_rows(t_ref, n_ref, layer, pixels)
        lean, slant = b_ref[0:1] / pixels, b_ref[1:2] / pixels

        def one(i, carry):
            place = pl.ds(3 * i, 3)
            row = lax.rem(g, per) * CHUNK + 3 * i
            spread_columns(wide, g // per, row, x_ref[0, place].astype(jnp.float32))
            centered = (y_ref[0, place] - center) * inverse
            values = gain * inverse * (up_ref[0, place] - lean - centered * slant)
            values = values.astype(jnp.bfloat16)
            if back_ref is not None:
                back_ref[0, place] = values
            back[g // per, pl.ds(row, 3)] = values
            values = values.astype(jnp.float32)
            whole = jnp.sum(values, axis=1)
            first = jnp.sum(jnp.where(column < DILATION_STEP, values[:, :8], 0.0), axis=1)
            last = jnp.sum(
                jnp.where(column >= 8 - DILATION_STEP, values[:, width - 8 :], 0.0), axis=1
            )
            for kernel_column, line in enumerate((whole - first, whole, whole - last)):
                for kernel_row in range(3):
                    at = row + DILATION_STEP * (kernel_row - 1)
                    part = [
                        jnp.where((at + r >= 0) & (at + r < height), line[r : r + 1], 0.0)
                        for r in range(3)
                    ]
                    tap = 3 * kernel_row + kernel_column
                    edge_ref[tap : tap + 1] += part[0] + part[1] + part[2]
            return carry

        lax.fori_loop(0, CHUNK // 3, one, 0)


def tap_gradient(wide, back, members, tap_row, column, t_ref, line):
    images, height, width, channels = back.shape
    total = None
    for image in range(images):
        part = dot(
            window(wide, image, 0, height, tap_row, column),
            back[image].reshape(height * width, channels),
            CONTRACT_ROWS,
        )
        total = part if total is None else total + part
    mean = jnp.swapaxes(t_ref[...], 0, 1)[:, 2:3] / pixel_count(wide, members)
    return total - mean * line


def weight_kernel(
    steps, members, x_ref, up_ref, y_ref, t_ref, n_ref, b_ref, grad_ref, edge_ref, back_ref, wide, back
):
    g = pl.program_id(0)
    deltas(
        g, steps, members, 1, x_ref, up_ref, y_ref, t_ref, n_ref, b_ref, edge_ref, back_ref, wide, back
    )
    for column in range(3):

        @pl.when((g >= steps) & (lax.rem(g - steps, 3) == column))
        def _():
            line = edge_ref[pl.ds(g - steps, 1)]
            grad = tap_gradient(wide, back, members, (g - steps) // 3, column, t_ref, line)
            grad_ref[0] = grad.astype(grad_ref.dtype)


def weight_grad_call(x, upstream, y, totals, gains, backs):
    images, height, width, channels = x.shape
    steps, tiles, stream, rows = map_specs(*x.shape)
    return pl.pallas_call(
        functools.partial(weight_kernel, steps, lax.axis_size("dp")),
        grid=(steps + 9,),
        in_specs=[stream, stream, stream, fixed(8, channels), fixed(4, channels), fixed(16, channels)],
        out_specs=(
            pl.BlockSpec((1, channels, channels), lambda g: (jnp.maximum(g - steps, 0), 0, 0)),
            fixed(16, channels),
            stream,
        ),
        out_shape=(
            jax.ShapeDtypeStruct((9, channels, channels), jnp.bfloat16),
            jax.ShapeDtypeStruct((16, channels), jnp.float32),
            jax.ShapeDtypeStruct(x.shape, jnp.bfloat16),
        ),
        scratch_shapes=[
            pltpu.VMEM((images, height + 2 * DILATION_STEP, width, 3 * channels), jnp.bfloat16),
            pltpu.VMEM((images, height, width, channels), jnp.bfloat16),
        ],
        compiler_params=PARAMS,
        name="weight_grad",
    )(x, upstream.reshape(x.shape), y.reshape(x.shape), totals, gains, backs)


def act_grad_kernel(
    members, steps, tiles, back_ref, y_ref, t_ref, n_ref, w_ref, note_ref, up_ref, total, wide, *exchange
):
    g = pl.program_id(0)
    sums = exchange[0]

    @pl.when(g == 0)
    def _():
        signal_peers([("dp", members)])
        clear_edges(wide)
        sums[...] = note_ref[...]

    @pl.when(g < steps)
    def _():
        per = steps // wide.shape[0]

        def one(i, carry):
            spread_columns(
                wide,
                g // per,
                lax.rem(g, per) * CHUNK + 3 * i,
                back_ref[0, pl.ds(3 * i, 3)].astype(jnp.float32),
            )
            return carry

        lax.fori_loop(0, CHUNK // 3, one, 0)

    @pl.when(g >= steps)
    def _():
        per = tiles // wide.shape[0]
        t = g - steps
        grad = conv_tile_back(wide, w_ref, t // per, lax.rem(t, per) * TILE, TILE)
        center, inverse, gain, shift = norm_rows(t_ref, n_ref, 0, pixel_count(wide, members))
        centered = (y_ref[...] - center) * inverse
        upstream = grad * silu_slope(gain * centered + shift)
        up_ref[...] = upstream
        add_sums(sums, upstream, upstream * centered)

    @pl.when(g == steps + tiles - 1)
    def _():
        wait_peers([("dp", members)])
        sum_over_owners(members, sums, total, *exchange[1:])


def act_grad_call(back, y, totals, gains, weights, note, identity):
    images, height, width, channels = back.shape
    steps, tiles, stream, rows = map_specs(*back.shape)
    pixels = images * height * width
    members = lax.axis_size("dp")
    return pl.pallas_call(
        functools.partial(act_grad_kernel, members, steps, tiles),
        grid=(steps + tiles,),
        in_specs=[
            stream,
            rows,
            fixed(8, channels),
            fixed(4, channels),
            fixed(*weights.shape),
            fixed(*note.shape),
        ],
        out_specs=(rows, fixed(16, channels)),
        out_shape=(
            jax.ShapeDtypeStruct((pixels, channels), jnp.float32),
            jax.ShapeDtypeStruct((16, channels), jnp.float32),
        ),
        scratch_shapes=[
            pltpu.VMEM((images, height + 2 * DILATION_STEP, width, 3 * channels), jnp.bfloat16)
        ]
        + sum_scratch(members, 16, channels),
        compiler_params=summing(identity),
        name="act_grad",
    )(back, y, totals, gains, weights, note)


def update_kernel(
    place_ref, g_ref, rows_ref, cols_ref, left_ref, right_ref, master_ref, lroot_ref, rroot_ref,
    grad_out, left_out, right_out, master_out, copy_out, gram,
):
    parts = g_ref.shape[1]
    shard_rows = left_ref.shape[1]
    full = jnp.concatenate([g_ref[0, part] for part in range(parts)], axis=1)
    rows = jnp.concatenate([rows_ref[0, part] for part in range(parts)], axis=1)
    grad_out[0] = rows.astype(jnp.float32)
    left_out[0] = 0.5 * left_ref[0] + 0.5 * dot(rows, full, CONTRACT_COLS)
    gram[...] = dot(cols_ref[0, 0], full, CONTRACT_ROWS)
    right_out[0] = 0.5 * right_ref[0] + 0.5 * gram[
        pl.ds(pl.multiple_of(place_ref[2], 8), shard_rows)
    ]
    turned = dot(lroot_ref[0].astype(jnp.bfloat16), full).astype(jnp.bfloat16)
    step = dot(turned, rroot_ref[0].astype(jnp.bfloat16))
    master = master_ref[0]
    master = master - RATE_TRUNK * (step + WEIGHT_DECAY * master)
    master_out[0] = master
    copy_out[0] = master.astype(jnp.bfloat16)


def update_call(owner, combined, left, right, master, lroot, rroot):
    layers, taps, shard_rows, channels = left.shape
    count, parts, _, width = combined.shape
    one = pl.BlockSpec((1, shard_rows, channels), lambda g, place: (g, 0, 0))
    whole = pl.BlockSpec((1, channels, channels), lambda g, place: (g, 0, 0))
    flat = (count, shard_rows, channels)
    start = owner * shard_rows
    place = jnp.stack([owner, start // width, lax.rem(start, width)]).astype(jnp.int32)
    outs = pl.pallas_call(
        update_kernel,
        grid_spec=pltpu.PrefetchScalarGridSpec(
            num_scalar_prefetch=1,
            grid=(count,),
            in_specs=[
                pl.BlockSpec((1, parts, channels, width), lambda g, place: (g, 0, 0, 0)),
                pl.BlockSpec((1, parts, shard_rows, width), lambda g, place: (g, 0, place[0], 0)),
                pl.BlockSpec((1, 1, channels, width), lambda g, place: (g, place[1], 0, 0)),
                one,
                one,
                one,
                one,
                whole,
            ],
            out_specs=(one,) * 5,
            scratch_shapes=[pltpu.VMEM((width, channels), jnp.float32)],
        ),
        out_shape=tuple(
            jax.ShapeDtypeStruct(flat, kind)
            for kind in (jnp.float32, jnp.float32, jnp.float32, jnp.float32, jnp.bfloat16)
        ),
        compiler_params=PARAMS,
        name="update",
    )(
        place,
        combined,
        combined,
        combined,
        left.reshape(flat),
        right.reshape(flat),
        master.reshape(flat),
        lroot.reshape(flat),
        rroot.reshape(count, channels, channels),
    )
    return [out.reshape(left.shape) for out in outs]


def combined_plan(members, taps):
    bits = owner_bits(members)
    last = bits[-1:]
    plain = tuple(bits) + (FAR, CORE)
    other = tuple(bits[:-1]) + (FAR,) + tuple(last) + (CORE,)
    early = tuple(last) + (FAR,) + tuple(bits[:-1]) + (CORE,)
    first = (FAR,) + tuple(last) + tuple(bits[:-1]) + (CORE,)
    return [spread([plain, other, plain, other, early, first] * 3, taps, 6)], [[FAR, CORE] + bits]


PAIRS = [(i, j) for i in range(TASKS) for j in range(i, TASKS)]


def mix_kernel(
    members, plans, dims, sum_ref, mean_ref, edge_ref, scale_ref, conflict_ref,
    notes_ref, full_ref, pair_ref, notes_out, own, sent, held, products, dp_slots, partial,
    task_slots, mixed, block_send, block_recv, note_send, note_recv, dp_send, dp_recv, task_send,
    task_recv, local_sem, send_sem, recv_sem,
):
    task = lax.axis_index("task")
    owner = lax.axis_index("dp")
    taps = held.shape[1] // 2
    greet_peers([("dp", members), ("task", TASKS)])
    notes = share("task", TASKS, lambda peer: notes_ref, notes_out, note_send, note_recv)
    notes_out[task] = notes_ref[...]
    for layer in range(2):

        def one(tap, carry):
            grad = sum_ref[layer * taps + tap] + mean_ref[layer] * edge_ref[layer, pl.ds(tap, 1)]
            grad = (grad * scale_ref[0:1]).astype(jnp.bfloat16)
            for part in range(TASKS):
                sent[part, layer * taps + tap] = grad[:, part * 128 : (part + 1) * 128]
            return carry

        lax.fori_loop(0, taps, one, 0)
    blocks = share("task", TASKS, lambda peer: sent.at[peer], held, block_send, block_recv)
    local = pltpu.make_async_copy(sent.at[task], held.at[task], own.at[0])
    local.start()
    local.wait()
    await_shares("task", TASKS, lambda peer: sent.at[peer], held, block_send, block_recv)
    width = held.shape[3]

    def multiply(tap, sums):
        values = [held[t, tap].astype(jnp.float32) for t in range(TASKS)]
        return tuple(
            total
            + jnp.sum((values[i] * values[j]).reshape(-1, 8, width), axis=0)
            for total, (i, j) in zip(sums, PAIRS)
        )

    sums = lax.fori_loop(
        0, 2 * taps, multiply, tuple(jnp.zeros((8, width), jnp.float32) for _ in PAIRS)
    )
    for row, total in enumerate(sums):
        products[row : row + 1] = jnp.sum(total, axis=0, keepdims=True)
    products[len(PAIRS) : 16] = jnp.zeros((16 - len(PAIRS), width), jnp.float32)
    over_dp = share("dp", members, lambda peer: products, dp_slots, dp_send, dp_recv)
    dp_slots[owner] = products[...]
    await_shares("dp", members, lambda peer: products, dp_slots, dp_send, dp_recv)
    partial[...] = slot_total(dp_slots)
    over_task = share("task", TASKS, lambda peer: partial, task_slots, task_send, task_recv)
    task_slots[task] = partial[...]
    await_shares("task", TASKS, lambda peer: partial, task_slots, task_send, task_recv)
    total = jnp.broadcast_to(
        jnp.sum(slot_total(task_slots), axis=1, keepdims=True), products.shape
    )
    rows = {pair: total[row : row + 1] for row, pair in enumerate(PAIRS)}
    weights = []
    for j in range(TASKS):
        weight = jnp.ones((1, width), jnp.float32)
        for i in range(TASKS):
            pair = rows[min(i, j), max(i, j)]
            pair_ref[TASKS * i + j : TASKS * i + j + 1] = pair
            if i != j:
                at = TASKS * i + j
                weight = weight - conflict_ref[at : at + 1] * pair / (rows[j, j] + GRAM_EPS)
        weights.append(weight)

    def blend(tap, carry):
        value = weights[0] * held[0, tap].astype(jnp.float32)
        for t in range(1, TASKS):
            value = value + weights[t] * held[t, tap].astype(jnp.float32)
        mixed[tap] = value.astype(jnp.bfloat16)
        return carry

    lax.fori_loop(0, 2 * taps, blend, 0)
    Gather(plans, dims, [False], [mixed], [full_ref], local_sem, send_sem, recv_sem).run()
    await_shares("task", TASKS, lambda peer: notes_ref, notes_out, note_send, note_recv)
    for copy in notes + blocks + over_dp + over_task:
        copy.wait_send()


def mix_call(sums, taps, means, edges, scale, conflict, notes, identity):
    members = lax.axis_size("dp")
    _, shard_rows, channels = sums.shape
    plans, dims = combined_plan(members, 2 * taps)
    width = channels // TASKS
    vmem = pl.BlockSpec(memory_space=pltpu.VMEM)
    dma = pltpu.SemaphoreType.DMA
    entries = len(plans[0][0])
    full, pairs, notes = pl.pallas_call(
        functools.partial(mix_kernel, members, plans, dims),
        out_shape=(
            jax.ShapeDtypeStruct(
                (2 * taps,) + (2,) * len(dims[0]) + (shard_rows, width), jnp.bfloat16
            ),
            jax.ShapeDtypeStruct((16, width), jnp.float32),
            jax.ShapeDtypeStruct((TASKS,) + notes.shape, jnp.float32),
        ),
        in_specs=[vmem] * 6,
        out_specs=(pl.BlockSpec(memory_space=pl.ANY), vmem, vmem),
        scratch_shapes=[
            dma((1,)),
            pltpu.VMEM((TASKS, 2 * taps, shard_rows, width), jnp.bfloat16),
            pltpu.VMEM((TASKS, 2 * taps, shard_rows, width), jnp.bfloat16),
            pltpu.VMEM((16, width), jnp.float32),
            pltpu.VMEM((members, 16, width), jnp.float32),
            pltpu.VMEM((16, width), jnp.float32),
            pltpu.VMEM((TASKS, 16, width), jnp.float32),
            pltpu.VMEM((2 * taps, shard_rows, width), jnp.bfloat16),
            dma((TASKS,)),
            dma((TASKS,)),
            dma((TASKS,)),
            dma((TASKS,)),
            dma((members,)),
            dma((members,)),
            dma((TASKS,)),
            dma((TASKS,)),
            dma((entries, 2)),
            dma((entries, len(dims[0]))),
            dma((entries, len(dims[0]))),
        ],
        compiler_params=pltpu.CompilerParams(
            collective_id=identity, has_side_effects=True, vmem_limit_bytes=40 * 1024 * 1024
        ),
        name="mix",
    )(sums, means, edges, scale, conflict, notes)
    return full.reshape(2 * taps, TASKS, members * shard_rows, width), pairs, notes


def reduce_kernel(
    members, stages, late, steps, x_ref, up_ref, y_ref, t_ref, n_ref, b_ref, *refs
):
    count = 2 * len(late)
    keeps, others = refs[:count:2], refs[1:count:2]
    sum_ref, edge_out, wide, back, edge_ref, part_ref = refs[count : count + 6]
    buffers, (slots, send_sem, recv_sem, slot_send, slot_recv) = refs[count + 6 : -5], refs[-5:]
    g = pl.program_id(0)
    got = buffers[:stages]
    sent = (None,) + tuple(buffers[stages : 2 * stages - 1])
    kept = (None,) + tuple(buffers[2 * stages - 1 :])
    taps = part_ref.shape[0]
    dims = [("dp", 1 << stage) for stage in range(stages)]
    starts = [(0, None, tap) for tap in range(taps)]
    for index, stage in enumerate(late):
        starts += [(stage, index, tap) for tap in range(keeps[index].shape[0])]
    whole = [entry for entry, (first, _, _) in enumerate(starts) if first == 0]

    def landed(stage, entry):
        return got[stage].at[entry if stage else whole.index(entry)]

    def copy_of(stage, entry):
        first, index, tap = starts[entry]
        mine, device = partner(dims[stage])
        if stage > first:
            source = sent[stage].at[entry]
        elif index is None:
            source = part_ref.at[tap, :, 1 - mine]
        else:
            source = others[index].at[tap]
        return pltpu.make_async_remote_copy(
            src_ref=source,
            dst_ref=landed(stage, entry),
            send_sem=send_sem.at[stage, entry],
            recv_sem=recv_sem.at[stage, entry],
            device_id=device,
            device_id_type=pl.DeviceIdType.MESH,
        )

    def total_of(stage, entry, at):
        first, index, tap = starts[entry]
        if stage > first:
            value = kept[stage][entry, at]
        elif index is None:
            value = part_ref[tap, at, partner(dims[0])[0]]
        else:
            value = keeps[index][tap, at]
        return value.astype(jnp.float32) + landed(stage, entry)[at].astype(jnp.float32)

    def advance(stage, entry):
        copy_of(stage, entry).wait_recv()
        if stage == stages - 1:
            sum_ref[entry] = total_of(stage, entry, 0)
            return
        following = partner(dims[stage + 1])[0]
        for block in range((members >> (stage + 1)) // 2):
            for half in range(2):
                at = 2 * block + (following if half else 1 - following)
                value = total_of(stage, entry, at)
                if half:
                    kept[stage + 1][entry, block] = value
                else:
                    sent[stage + 1][entry, block] = value.astype(jnp.bfloat16)
        copy_of(stage + 1, entry).start()

    @pl.when(g == 0)
    def _():
        greet_peers([("dp", members)])
        for entry in range(taps, len(starts)):
            copy_of(starts[entry][0], entry).start()

    deltas(g, steps, members, 0, x_ref, up_ref, y_ref, t_ref, n_ref, b_ref, edge_ref, None, wide, back)

    @pl.when(g == steps)
    def _():
        share("dp", members, lambda peer: edge_ref, slots, slot_send, slot_recv)
        slots[lax.axis_index("dp")] = edge_ref[...]

    waiting = [
        [entry for entry in range(taps, len(starts)) if starts[entry][0] == stage]
        for stage in range(stages)
    ]

    def turn():
        moved = []
        for stage in range(stages - 1, -1, -1):
            if waiting[stage]:
                entry = waiting[stage].pop(0)
                advance(stage, entry)
                if stage + 1 < stages:
                    moved.append((stage + 1, entry))
        for stage, entry in moved:
            waiting[stage].append(entry)

    for tap in range(taps):

        @pl.when(g == steps + tap)
        def _():
            grad = tap_gradient(
                wide, back, members, tap // 3, tap % 3, t_ref, edge_ref[tap : tap + 1]
            )
            part_ref[tap] = grad.reshape(part_ref.shape[1:]).astype(part_ref.dtype)
            copy_of(0, tap).start()
            if tap >= 4:
                turn()

    @pl.when(g == steps + taps - 1)
    def _():
        waiting[0].extend(range(taps))
        while any(waiting):
            turn()
        await_shares("dp", members, lambda peer: edge_ref, slots, slot_send, slot_recv)
        edge_out[...] = slot_total(slots)
        for entry, (first, _, _) in enumerate(starts):
            for stage in range(first, stages):
                copy_of(stage, entry).wait_send()
        await_sends("dp", members, lambda peer: edge_ref, slots, slot_send, slot_recv)


def reduce_call(x, upstream, y, totals, gains, backs, late, identity):
    images, height, columns, channels = x.shape
    steps, _, stream, _ = map_specs(*x.shape)
    members = lax.axis_size("dp")
    stages = members.bit_length() - 1
    taps, width = 9, channels
    shard_rows = channels // members
    entries = taps + sum(keep.shape[0] for _, keep, _ in late)
    vmem = pl.BlockSpec(memory_space=pltpu.VMEM)
    dma = pltpu.SemaphoreType.DMA

    whole = taps + sum(keep.shape[0] for stage, keep, _ in late if stage == 0)

    def blocks(stage, kind):
        held = entries if stage else whole
        return pltpu.VMEM((held, members >> (stage + 1), shard_rows, width), kind)

    late_arrays = [array for _, keep, other in late for array in (keep, other)]

    return pl.pallas_call(
        functools.partial(reduce_kernel, members, stages, [stage for stage, _, _ in late], steps),
        grid=(steps + taps,),
        out_shape=(
            jax.ShapeDtypeStruct((entries, shard_rows, width), jnp.float32),
            jax.ShapeDtypeStruct((16, channels), jnp.float32),
        ),
        in_specs=[stream, stream, stream, fixed(8, channels), fixed(4, channels), fixed(16, channels)]
        + [vmem] * len(late_arrays),
        out_specs=(vmem, vmem),
        scratch_shapes=[
            pltpu.VMEM((images, height + 2 * DILATION_STEP, columns, 3 * channels), jnp.bfloat16),
            pltpu.VMEM((images, height, columns, channels), jnp.bfloat16),
            pltpu.VMEM((16, channels), jnp.float32),
            pltpu.VMEM((taps, members // 2, 2, shard_rows, width), jnp.bfloat16),
        ]
        + [blocks(stage, jnp.bfloat16) for stage in range(stages)]
        + [blocks(stage, jnp.bfloat16) for stage in range(1, stages)]
        + [blocks(stage, jnp.float32) for stage in range(1, stages)]
        + [
            pltpu.VMEM((members, 16, channels), jnp.float32),
            dma((stages, entries)),
            dma((stages, entries)),
            dma((members,)),
            dma((members,)),
        ],
        compiler_params=summing(identity),
        name="reduce",
    )(
        x,
        upstream.reshape(x.shape),
        y.reshape(x.shape),
        totals,
        gains,
        backs,
        *late_arrays,
    )


def halves(held, bit):
    taps, count, rows, width = held.shape
    held = held.reshape(taps, count // 2, 2, rows, width)
    mine = lax.rem(lax.axis_index("dp") // bit, 2)
    other = lax.dynamic_index_in_dim(held, 1 - mine, 2, keepdims=False)
    keep = lax.dynamic_index_in_dim(held, mine, 2, keepdims=False)
    return keep, other.astype(jnp.bfloat16)


def swap(other, bit):
    members = lax.axis_size("dp")
    return lax.ppermute(other, "dp", [(i, i ^ bit) for i in range(members)])


def added(keep, other):
    return keep.astype(jnp.float32) + other.astype(jnp.float32)


def by_owner(parts):
    taps, channels, width = parts.shape
    members = lax.axis_size("dp")
    return parts.reshape(taps, members, channels // members, width)


def tied(first, second):
    return lax.optimization_barrier((first, second))


def pad_rows(parts, rows):
    used = sum(part.shape[0] for part in parts)
    if used < rows:
        parts = list(parts) + [jnp.zeros((rows - used, parts[0].shape[1]), jnp.float32)]
    return jnp.concatenate(parts)


def boundary(labels):
    across = jnp.pad(
        (labels[:, :, 1:] != labels[:, :, :-1]).astype(jnp.float32), ((0, 0), (0, 0), (0, 1))
    )
    downward = jnp.pad(
        (labels[:, 1:, :] != labels[:, :-1, :]).astype(jnp.float32), ((0, 0), (0, 1), (0, 0))
    )
    return jnp.maximum(across, downward)


def pixel_rows(labels, depth_mask, depth_target, normal_target):
    images, height, width = labels.shape
    rows = jnp.stack(
        [
            labels.astype(jnp.float32),
            depth_mask.astype(jnp.float32),
            boundary(labels),
            depth_target,
        ],
        axis=1,
    )
    rows = jnp.concatenate([rows, normal_target, jnp.zeros_like(rows[:, :1])], axis=1)
    rows = rows.reshape(images, 8, height // CHUNK, CHUNK * width)
    return jnp.swapaxes(rows, 1, 2)


def head_kernel(
    members, chunks, images, y_ref, x_ref, t_ref, n_ref, head_ref, out_ref, bias_ref, info_ref, weight_ref,
    up_ref, grad_ref, total, trunk, hidden_pre, pre_grads, pooled, base, per_image, matrix, *exchange,
):
    image, step = pl.program_id(0), pl.program_id(1)
    last = images - 1
    sums = exchange[0]
    rows = CHUNK * y_ref.shape[2]
    channels = y_ref.shape[3]
    area = float(chunks * rows)
    pixels = area * images * members
    phase = step // chunks
    place = pl.ds(lax.rem(step, chunks) * rows, rows)

    @pl.when((image == 0) & (step == 0))
    def _():
        signal_peers([("dp", members)])
        sums[...] = jnp.zeros_like(sums)
        matrix[...] = jnp.zeros_like(matrix)

    @pl.when(step == 0)
    def _():
        pooled[...] = jnp.zeros_like(pooled)
        per_image[...] = jnp.zeros_like(per_image)

    def residual():
        center, inverse, gain, shift = norm_rows(t_ref, n_ref, 1, pixels)
        centered = (y_ref[0].reshape(rows, channels) - center) * inverse
        inputs = x_ref[0].reshape(rows, channels).astype(jnp.float32)
        return centered, gain * centered + shift + inputs

    @pl.when(phase == 0)
    def _():
        _, before = residual()
        act = jax.nn.silu(before).astype(jnp.bfloat16)
        trunk[place] = act
        pooled[0:1] += jnp.sum(act.astype(jnp.float32), axis=0, keepdims=True)

    @pl.when(step == chunks)
    def _():
        mean = jnp.broadcast_to((pooled[0:1] / area).astype(jnp.bfloat16), (16, channels))
        base[...] = dot(mean, head_ref[1])[0:8] + bias_ref[...]

    @pl.when(phase == 1)
    def _():
        act = trunk[place]
        before = dot(act, head_ref[0]) + base[0:1]
        sigmoid = jax.nn.sigmoid(before)
        hidden = (before * sigmoid).astype(jnp.bfloat16)
        logits = dot(out_ref[...], hidden, CONTRACT_COLS)
        info = info_ref[0, 0]
        weight = [weight_ref[0, t : t + 1, 0:1] for t in range(TASKS)]
        classes = logits[:CLASSES]
        largest = jnp.max(classes, axis=0, keepdims=True)
        powers = jnp.exp(classes - largest)
        power = jnp.sum(powers, axis=0, keepdims=True)
        index = lax.broadcasted_iota(jnp.int32, classes.shape, 0).astype(jnp.float32)
        chosen = index == info[0:1]
        picked = jnp.sum(jnp.where(chosen, classes, 0.0), axis=0, keepdims=True)
        segment = jnp.log(power) + largest - picked
        class_grad = weight[0] * (powers / power - jnp.where(chosen, 1.0, 0.0))
        offset = logits[CLASSES : CLASSES + 1] - info[3:4]
        length = jnp.sqrt(offset * offset + 1.0)
        depth_grad = weight[1] * info[1:2] * (offset / length)
        predicted = logits[CLASSES + 1 : CLASSES + 4]
        normal = info[4:7]
        product = jnp.sum(predicted * normal, axis=0, keepdims=True)
        square = jnp.sum(predicted * predicted, axis=0, keepdims=True) + 1.0
        scale = lax.rsqrt(square * (jnp.sum(normal * normal, axis=0, keepdims=True) + 1.0))
        cosine = product * scale
        normal_grad = -weight[2] * (normal * scale - cosine * predicted / square)
        edge = logits[CLASSES + 4 : CLASSES + 5]
        softplus = jnp.maximum(edge, 0.0) + jnp.log1p(jnp.exp(-jnp.abs(edge)))
        edge_grad = weight[3] * (jax.nn.sigmoid(edge) - info[2:3])
        losses = (
            weight[0] * segment,
            weight[1] * info[1:2] * (length - 1.0),
            weight[2] * (1.0 - cosine),
            weight[3] * (softplus - info[2:3] * edge),
        )
        lane = lax.broadcasted_iota(jnp.int32, (1, channels), 1)
        for t, loss in enumerate(losses):
            value = jnp.sum(loss, axis=1, keepdims=True)
            sums[2:3] += jnp.where(lane == BRANCH_WIDTH + t, value, 0.0)
        rest = jnp.zeros((out_ref.shape[0] - CLASSES - 5, rows), jnp.float32)
        grads = jnp.concatenate([class_grad, depth_grad, normal_grad, edge_grad, rest], axis=0)
        grads = grads.astype(jnp.bfloat16)
        out_grad = dot(grads, hidden)
        sums[3:12, :BRANCH_WIDTH] += out_grad[0:9]
        sums[3:12, BRANCH_WIDTH:] += out_grad[9:18]
        back = dot(grads, out_ref[...], CONTRACT_ROWS)
        back = (back * (sigmoid * (1.0 + before * (1.0 - sigmoid)))).astype(jnp.bfloat16)
        pre_grads[place] = back
        matrix[:, :BRANCH_WIDTH] += dot(act, back, CONTRACT_ROWS)
        per_image[0:1] += jnp.sum(back.astype(jnp.float32), axis=0, keepdims=True)

    @pl.when(step == 2 * chunks)
    def _():
        line = per_image[...]
        mean = pooled[...] / area
        mean = mean.astype(jnp.bfloat16).astype(jnp.float32)
        matrix[:, BRANCH_WIDTH:] += lax.dot_general(
            mean, line, CONTRACT_ROWS, precision=PRECISE, preferred_element_type=jnp.float32
        )
        sums[2:3, :BRANCH_WIDTH] += line[0:1]
        hidden_pre[...] = lax.dot_general(
            line,
            head_ref[1].astype(jnp.float32),
            CONTRACT_COLS,
            precision=PRECISE,
            preferred_element_type=jnp.float32,
        )

    @pl.when(phase == 2)
    def _():
        centered, before = residual()
        back = dot(pre_grads[place], head_ref[0], CONTRACT_COLS) + hidden_pre[0:1] / area
        upstream = back * silu_slope(before)
        up_ref[...] = upstream
        add_sums(sums, upstream, upstream * centered)

    @pl.when((image == last) & (step == 3 * chunks - 1))
    def _():
        grad_ref[...] = matrix[...].astype(grad_ref.dtype)
        wait_peers([("dp", members)])
        sum_over_owners(members, sums, total, *exchange[1:])


def head_call(y, x, totals, gains, head, out_rows, bias, info, weights, identity):
    images, height, width, channels = x.shape
    chunks = height // CHUNK
    rows = CHUNK * width
    members = lax.axis_size("dp")

    def again(b, c):
        return jnp.where(c // chunks == 1, chunks - 1, lax.rem(c, chunks))

    def constant(*shape):
        return pl.BlockSpec(shape, lambda b, c: (0,) * len(shape))

    stream = pl.BlockSpec((1, CHUNK, width, channels), lambda b, c: (b, again(b, c), 0, 0))
    return pl.pallas_call(
        functools.partial(head_kernel, members, chunks, images),
        grid=(images, 3 * chunks),
        in_specs=[
            stream,
            stream,
            constant(8, channels),
            constant(4, channels),
            constant(*head.shape),
            constant(*out_rows.shape),
            constant(1, BRANCH_WIDTH),
            pl.BlockSpec((1, 1, 8, rows), lambda b, c: (b, lax.rem(c, chunks), 0, 0)),
            pl.BlockSpec((1, 8, 128), lambda b, c: (b, 0, 0)),
        ],
        out_specs=(
            pl.BlockSpec(
                (rows, channels), lambda b, c: (b * chunks + jnp.maximum(c - 2 * chunks, 0), 0)
            ),
            constant(channels, 2 * BRANCH_WIDTH),
            constant(16, channels),
        ),
        out_shape=(
            jax.ShapeDtypeStruct((images * height * width, channels), jnp.float32),
            jax.ShapeDtypeStruct((channels, 2 * BRANCH_WIDTH), jnp.bfloat16),
            jax.ShapeDtypeStruct((16, channels), jnp.float32),
        ),
        scratch_shapes=[
            pltpu.VMEM((chunks * rows, channels), jnp.bfloat16),
            pltpu.VMEM((8, channels), jnp.float32),
            pltpu.VMEM((chunks * rows, BRANCH_WIDTH), jnp.bfloat16),
            pltpu.VMEM((8, channels), jnp.float32),
            pltpu.VMEM((8, BRANCH_WIDTH), jnp.float32),
            pltpu.VMEM((8, BRANCH_WIDTH), jnp.float32),
            pltpu.VMEM((channels, 2 * BRANCH_WIDTH), jnp.float32),
        ]
        + sum_scratch(members, 16, channels),
        compiler_params=summing(identity),
        name="heads",
    )(y.reshape(x.shape), x, totals, gains, head, out_rows, bias, info, weights)


def adamw_update(gradient, moment_one, moment_two, weight, rate):
    moment_one = 0.5 * moment_one + 0.5 * gradient
    moment_two = 0.5 * moment_two + 0.5 * gradient * gradient
    correction = 1.0 - 0.5**STEP
    weight = weight - rate * (
        moment_one / correction / (jnp.sqrt(moment_two / correction) + ADAM_EPS)
        + WEIGHT_DECAY * weight
    )
    return (moment_one, moment_two, weight)


def body(
    features,
    labels,
    depth_mask,
    depth_target,
    normal_target,
    scene_ids,
    task_weights,
    conflict,
    trunk_copy,
    trunk_master,
    trunk_left,
    trunk_right,
    left_root,
    right_root,
    head_copy,
    head_master,
    head_first,
    head_second,
    out_copy,
    out_master,
    out_first,
    out_second,
    trunk_gains,
    gains_first,
    gains_second,
    head_bias,
    bias_first,
    bias_second,
):
    images, feature_rows, feature_columns, channels = features.shape
    pixels = jnp.array(images * feature_rows * feature_columns * lax.axis_size("dp"), jnp.float32)
    task_index = lax.axis_index("task")
    owner_index = lax.axis_index("dp")
    local_valid = jnp.sum(depth_mask.astype(jnp.float32))
    first_note = jnp.where(jnp.arange(8)[:, None] == 3, local_valid, jnp.zeros((8, channels)))
    first_conv, first_totals, second_full, head_full = first_conv_call(
        features, trunk_copy, head_copy, first_note, 0
    )
    valid_count = first_totals[3, 0]
    second_conv, first_act, second_totals = second_conv_call(
        first_conv, first_totals, trunk_gains, second_full, features.shape, 1
    )
    selector = (jnp.arange(TASKS) == task_index).astype(jnp.float32)
    own_bias = jnp.sum(selector[:, None] * head_bias, axis=0, keepdims=True)
    choose = (scene_ids[:, None] == jnp.arange(task_weights.shape[0])[None, :]).astype(jnp.float32)
    image_weights = jnp.sum(choose[:, :, None] * task_weights[None], axis=1) * selector
    image_weights = jnp.broadcast_to(
        jnp.pad(image_weights, ((0, 0), (0, 8 - TASKS)))[:, :, None], (images, 8, 128)
    )
    out_rows = jnp.pad(out_copy.T, ((0, 32 - out_copy.shape[1]), (0, 0)))
    second_up, head_grad, second_back_sums = head_call(
        second_conv,
        features,
        second_totals,
        trunk_gains,
        head_full,
        out_rows,
        own_bias,
        pixel_rows(labels, depth_mask, depth_target, normal_target),
        image_weights,
        2,
    )
    head_grad = by_owner(head_grad[None])
    second_weight, second_edges, second_back = weight_grad_call(
        first_act,
        second_up,
        second_conv,
        second_totals,
        trunk_gains,
        second_back_sums,
    )
    second_weight = by_owner(second_weight)
    cut = 4
    ahead, other = halves(jnp.concatenate([second_weight[:cut], head_grad]), 1)
    second_back, other = tied(second_back, other)
    other = swap(other, 1)
    edge_note = pad_rows([jnp.zeros((2, channels)), second_edges[:9]], 16)
    first_up, first_back_sums = act_grad_call(
        second_back, first_conv, first_totals, trunk_gains, second_full, edge_note, 3
    )
    second_edges = pad_rows([first_back_sums[2:11]], 16)
    ahead, other = halves(added(ahead, other), 2)
    behind, tail = halves(second_weight[cut:], 1)
    late = [
        (1, ahead[:cut], other[:cut]),
        (0, behind, tail),
        (1, ahead[cut:], other[cut:]),
    ]
    sums, first_edges = reduce_call(
        features,
        first_up,
        first_conv,
        first_totals,
        trunk_gains,
        first_back_sums,
        late,
        7,
    )
    edges = jnp.stack([first_edges, second_edges])
    means = jnp.stack([first_totals[2], second_totals[2]]) / pixels
    shard_rows = trunk_copy.shape[2]
    own_means = lax.dynamic_slice_in_dim(means, owner_index * shard_rows, shard_rows, 1)
    divisor = jnp.stack([pixels, valid_count, pixels, pixels])
    own_divisor = jnp.sum(divisor * selector)
    notes = pad_rows(
        [
            first_back_sums[1:2],
            first_back_sums[0:1],
            second_back_sums[1:2],
            second_back_sums[0:1],
            second_back_sums[2:12],
        ],
        16,
    )
    combined, pairs, notes = mix_call(
        sums,
        9,
        own_means[:, :, None],
        edges,
        jnp.full((8, channels), 1.0 / own_divisor),
        jnp.broadcast_to(
            conflict.astype(jnp.float32).reshape(TASKS * TASKS, 1), (TASKS * TASKS, 128)
        ),
        notes,
        6,
    )
    pair_products = pairs[:, 0].reshape(TASKS, TASKS)
    gains_total = jnp.sum(notes[:, 0:4] / divisor[:, None, None], axis=0)
    bias_total = notes[:, 4, :BRANCH_WIDTH] / divisor[:, None]
    loss_sum = jnp.sum(notes[:, 4, BRANCH_WIDTH : BRANCH_WIDTH + TASKS], axis=0)
    column_divisor = jnp.concatenate(
        [jnp.full((CLASSES,), divisor[0]), divisor[1:2], jnp.full((3,), divisor[2]), divisor[3:4]]
    )
    out_total = (
        jnp.concatenate(jnp.split(jnp.sum(notes[:, 5:14], axis=0), 2, axis=1)).T
        / column_divisor[None, :]
    )
    head_rows = jnp.stack(jnp.split(sums[18], 2, axis=1))[None]
    grad_rows, left_new, right_new, master_new, copy_new = update_call(
        owner_index, combined, trunk_left, trunk_right, trunk_master, left_root, right_root
    )
    head_one, head_two, head_new = adamw_update(
        head_rows / own_divisor, head_first, head_second, head_master, RATE_MATRIX
    )
    out_one, out_two, out_new = adamw_update(
        out_total, out_first, out_second, out_master, RATE_MATRIX
    )
    gain_one, gain_two, gain_new = adamw_update(
        gains_total, gains_first, gains_second, trunk_gains, RATE_VECTOR
    )
    bias_one, bias_two, bias_new = adamw_update(
        bias_total, bias_first, bias_second, head_bias, RATE_VECTOR
    )
    loss_terms = jnp.concatenate([loss_sum, valid_count[None]])
    return (
        grad_rows,
        left_new,
        right_new,
        master_new,
        copy_new,
        head_one,
        head_two,
        head_new,
        head_new.astype(jnp.bfloat16),
        out_one,
        out_two,
        out_new,
        out_new.astype(jnp.bfloat16),
        gain_one,
        gain_two,
        gain_new,
        bias_one,
        bias_two,
        bias_new,
        loss_terms,
        pair_products,
    )


def solution(mesh):
    rows = P(None, None, "dp", None)
    heads = P("task", None, "dp", None)
    images = P("dp")
    placed = (
        (images,) * 6
        + (P(), P())
        + (rows,) * 5
        + (P(),)
        + (heads,) * 4
        + (P(),) * 10
    )
    return jax.shard_map(
        body,
        mesh=mesh,
        in_specs=placed,
        out_specs=(rows,) * 5 + (heads,) * 4 + (P(),) * 12,
        check_vma=False,
    )
```

```python
import functools

import jax
import jax.numpy as jnp
from jax import lax
from jax.experimental import pallas as pl
from jax.experimental.pallas import tpu as pltpu
from jax.sharding import PartitionSpec as P

BRANCH_WIDTH = 256
CLASSES = 13
TASKS = 4
DILATION_STEP = 2
STEP = 5


PRECISE = lax.Precision.HIGHEST
NORM_EPS = 1e-05
RATE_TRUNK = 0.3
RATE_MATRIX = 0.05
RATE_VECTOR = 0.3
WEIGHT_DECAY = 0.01
ADAM_EPS = 1e-08
GRAM_EPS = 1e-12
PLAIN = (((1,), (0,)), ((), ()))
CONTRACT_ROWS = (((0,), (0,)), ((), ()))
CONTRACT_COLS = (((1,), (1,)), ((), ()))
CHUNK = 9
TILE = 12
VMEM_LIMIT = 58 * 1024 * 1024
PARAMS = pltpu.CompilerParams(vmem_limit_bytes=VMEM_LIMIT)


def summing(identity):
    return pltpu.CompilerParams(
        collective_id=identity, has_side_effects=True, vmem_limit_bytes=VMEM_LIMIT
    )


def silu_slope(tap_values):
    sigmoid = jax.nn.sigmoid(tap_values)
    return sigmoid * (1.0 + tap_values * (1.0 - sigmoid))


def dot(a, b, contract=PLAIN):
    return lax.dot_general(a, b, contract, preferred_element_type=jnp.float32)


def clear_edges(wide):
    rows = wide.shape[1]
    edge = jnp.zeros((wide.shape[0], DILATION_STEP) + wide.shape[2:], wide.dtype)
    wide[:, 0:DILATION_STEP] = edge
    wide[:, rows - DILATION_STEP : rows] = edge


def spread_columns(wide, image, row, values):
    width, channels = values.shape[1:]
    column = lax.broadcasted_iota(jnp.int32, (1, width, channels), 1)
    left = jnp.where(column >= DILATION_STEP, pltpu.roll(values, DILATION_STEP, 1), 0.0)
    right = jnp.where(
        column < width - DILATION_STEP, pltpu.roll(values, width - DILATION_STEP, 1), 0.0
    )
    place = pl.ds(DILATION_STEP + row, values.shape[0])
    for part, piece in enumerate((left, values, right)):
        wide[image, place, :, part * channels : (part + 1) * channels] = piece.astype(wide.dtype)


def window(wide, image, row, rows, kernel_row, part=None):
    channels = wide.shape[3] // 3
    place = pl.ds(row + DILATION_STEP * kernel_row, rows)
    if part is None:
        return wide[image, place].reshape(rows * wide.shape[2], 3 * channels)
    return wide[image, place, :, part * channels : (part + 1) * channels].reshape(
        rows * wide.shape[2], channels
    )


def conv_tile(wide, parts, image, row, rows):
    taps = jnp.concatenate([window(wide, image, row, rows, k) for k in range(3)], axis=1)
    parts = [part.reshape(-1, part.shape[-1]) for part in parts]
    return dot(taps, jnp.concatenate(parts, axis=1))


def conv_tile_back(wide, weights, image, row, rows):
    total = None
    for tap in range(9):
        kernel_row, kernel_column = divmod(tap, 3)
        part = dot(
            window(wide, image, row, rows, 2 - kernel_row, 2 - kernel_column),
            jnp.concatenate([weights[tap, part] for part in range(weights.shape[1])], axis=1),
            CONTRACT_COLS,
        )
        total = part if total is None else total + part
    return total


def peers(axis, members):
    me = lax.axis_index(axis)
    return [lax.rem(me + k, members) for k in range(1, members)]


def greet_peers(groups):
    signal_peers(groups)
    wait_peers(groups)


def share(axis, members, source, slots, send_sem, recv_sem):
    me = lax.axis_index(axis)
    copies = []
    for k, peer in enumerate(peers(axis, members)):
        copy = pltpu.make_async_remote_copy(
            src_ref=source(peer),
            dst_ref=slots.at[me],
            send_sem=send_sem.at[k],
            recv_sem=recv_sem.at[me],
            device_id={axis: peer},
            device_id_type=pl.DeviceIdType.MESH,
        )
        copy.start()
        copies.append(copy)
    return copies


def await_shares(axis, members, source, slots, send_sem, recv_sem):
    for k, peer in enumerate(peers(axis, members)):
        pltpu.make_async_remote_copy(
            src_ref=source(peer),
            dst_ref=slots.at[peer],
            send_sem=send_sem.at[k],
            recv_sem=recv_sem.at[peer],
            device_id={axis: peer},
            device_id_type=pl.DeviceIdType.MESH,
        ).wait_recv()


def await_sends(axis, members, source, slots, send_sem, recv_sem):
    for k, peer in enumerate(peers(axis, members)):
        pltpu.make_async_remote_copy(
            src_ref=source(peer),
            dst_ref=slots.at[peer],
            send_sem=send_sem.at[k],
            recv_sem=recv_sem.at[peer],
            device_id={axis: peer},
            device_id_type=pl.DeviceIdType.MESH,
        ).wait_send()


def slot_total(slots):
    total = slots[0]
    for k in range(1, slots.shape[0]):
        total = total + slots[k]
    return total


def signal_peers(groups):
    barrier = pltpu.get_barrier_semaphore()
    for axis, members in groups:
        for peer in peers(axis, members):
            pl.semaphore_signal(
                barrier, inc=1, device_id={axis: peer}, device_id_type=pl.DeviceIdType.MESH
            )


def wait_peers(groups):
    pl.semaphore_wait(pltpu.get_barrier_semaphore(), sum(members - 1 for _, members in groups))


def sum_over_owners(members, local, total, slots, send_sem, recv_sem):
    copies = share("dp", members, lambda peer: local, slots, send_sem, recv_sem)
    slots[lax.axis_index("dp")] = local[...]
    await_shares("dp", members, lambda peer: local, slots, send_sem, recv_sem)
    total[...] = slot_total(slots)
    for copy in copies:
        copy.wait_send()


def sum_scratch(members, rows, channels):
    return [
        pltpu.VMEM((rows, channels), jnp.float32),
        pltpu.VMEM((members, rows, channels), jnp.float32),
        pltpu.SemaphoreType.DMA((members,)),
        pltpu.SemaphoreType.DMA((members,)),
    ]


def pixel_count(wide, members):
    images, padded, width, _ = wide.shape
    return float(images * (padded - 2 * DILATION_STEP) * width * members)


def norm_rows(sums_ref, gain_ref, layer, pixels):
    center = sums_ref[0:1] / pixels
    inverse = lax.rsqrt(sums_ref[1:2] / pixels - center * center + NORM_EPS)
    return center, inverse, gain_ref[2 * layer : 2 * layer + 1], gain_ref[2 * layer + 1 : 2 * layer + 2]


def add_sums(sums, first, second):
    sums[0:1] += jnp.sum(first, axis=0, keepdims=True)
    sums[1:2] += jnp.sum(second, axis=0, keepdims=True)


FAR = ("task", 2)
CORE = ("task", 1)


def owner_bits(members):
    bits = []
    bit = members // 2
    while bit:
        bits.append(("dp", bit))
        bit //= 2
    return bits


def partner(dim):
    axis, bit = dim
    me = lax.axis_index(axis)
    mine = lax.rem(me // bit, 2)
    return mine, {axis: me + bit * (1 - 2 * mine)}


class Gather:
    def __init__(self, plans, dims, split, ins, outs, local_sem, send_sem, recv_sem):
        self.dims, self.split, self.ins, self.outs = dims, split, ins, outs
        self.local_sem, self.send_sem, self.recv_sem = local_sem, send_sem, recv_sem
        self.entries = [
            (array, start, rows, order)
            for array, (plan, _) in enumerate(plans)
            for start, rows, order in plan
        ]
        self.group_of, groups = [], 0
        for array, (plan, width) in enumerate(plans):
            late = groups + (2 if array == 1 else 0)
            self.group_of += [late + i // width for i in range(len(plan))]
            groups = self.group_of[-1] + 1
        self.depth = max(len(entry[3]) for entry in self.entries)
        self.steps = groups + self.depth

    def held(self, array, start, rows, free):
        return (pl.ds(start, rows),) + tuple(
            slice(None) if dim in free else partner(dim)[0] for dim in self.dims[array]
        )

    def placements(self, index):
        array, start, rows, order = self.entries[index]
        target = self.held(array, start, rows, ())
        source = self.ins[array]
        task = lax.axis_index("task")
        if not self.split[array]:
            pairs = [(source.at[pl.ds(start, rows)], target)]
        else:
            halves_of = [None] if FAR in order else [0, 1]
            pairs = []
            for half in halves_of:
                column = task if half is None else lax.rem(task, 2) + 2 * half
                column = pl.multiple_of(column * 128, 128)
                place = target if half is None else (target[0], half) + target[2:]
                pairs.append((source.at[pl.ds(start, rows), :, pl.ds(column, 128)], place))
        return [
            pltpu.make_async_copy(source, self.outs[array].at[place], self.local_sem.at[index, i])
            for i, (source, place) in enumerate(pairs)
        ]

    def copy_of(self, index, stage):
        array, start, rows, order = self.entries[index]
        free = set(order[:stage]) | {d for d in self.dims[array] if d not in order}
        where = self.held(array, start, rows, free)
        return pltpu.make_async_remote_copy(
            src_ref=self.outs[array].at[where],
            dst_ref=self.outs[array].at[where],
            send_sem=self.send_sem.at[index, stage],
            recv_sem=self.recv_sem.at[index, stage],
            device_id=partner(order[stage])[1],
            device_id_type=pl.DeviceIdType.MESH,
        )

    def place(self):
        for index in range(len(self.entries)):
            for copy in self.placements(index):
                copy.start()

    def step(self, step):
        for stage in range(self.depth, -1, -1):
            for index, (array, start, rows, order) in enumerate(self.entries):
                if self.group_of[index] != step - stage or stage > len(order):
                    continue
                if stage == 0:
                    for copy in self.placements(index):
                        copy.wait()
                else:
                    self.copy_of(index, stage - 1).wait_recv()
                if stage < len(order):
                    self.copy_of(index, stage).start()

    def finish(self):
        for index, entry in enumerate(self.entries):
            for stage in range(len(entry[3])):
                self.copy_of(index, stage).wait_send()

    def run(self):
        self.place()
        for step in range(self.steps):
            self.step(step)
        self.finish()


def spread(orders, taps, width):
    rows = taps // len(orders)
    return [(i * rows, rows, order) for i, order in enumerate(orders)], width


def weight_plans(members, taps):
    bits = owner_bits(members)
    quarters = tuple(bits) + (FAR, CORE)
    halves_only = tuple(bits) + (CORE,)
    trunk_plan = spread([quarters, halves_only, quarters] * 3, taps, 3)
    head_plan = spread([tuple(bits)], 2, 1)
    digits = [FAR, CORE] + bits
    return [trunk_plan, trunk_plan, head_plan], [digits, digits, bits], [True, True, False]


def first_kernel(
    members, steps, tiles, layout, x_ref, trunk_ref, head_ref, note_ref, conv_ref, total, full_ref,
    heads_ref, wide, weights, local_sem, send_sem, recv_sem, *exchange,
):
    g = pl.program_id(0)
    sums = exchange[0]
    moving = Gather(
        *layout,
        [trunk_ref.at[0], trunk_ref.at[1], head_ref],
        [weights, full_ref, heads_ref],
        local_sem,
        send_sem,
        recv_sem,
    )

    @pl.when(g == 0)
    def _():
        greet_peers([("dp", members), ("task", TASKS)])
        moving.place()
        clear_edges(wide)
        sums[...] = note_ref[...]

    spread_over = steps + tiles - 1
    ready = 3 + moving.depth
    for step in range(moving.steps):
        if step < ready:
            at = step * steps // ready
        else:
            at = steps + min(step - ready, tiles - 1)

        @pl.when(g == at)
        def _():
            moving.step(step)

    @pl.when(g < steps)
    def _():
        per = steps // wide.shape[0]

        def one(i, carry):
            spread_columns(
                wide,
                g // per,
                lax.rem(g, per) * CHUNK + 3 * i,
                x_ref[0, pl.ds(3 * i, 3)].astype(jnp.float32),
            )
            return carry

        lax.fori_loop(0, CHUNK // 3, one, 0)
        sums[2:3] += jnp.sum(x_ref[0].astype(jnp.float32), axis=(0, 1))[None]

    @pl.when(g >= steps)
    def _():
        per = tiles // wide.shape[0]
        t = g - steps
        parts = [weights[:, i, j] for i in range(2) for j in range(2)]
        conv = conv_tile(wide, parts, t // per, lax.rem(t, per) * TILE, TILE)
        conv_ref[...] = conv
        add_sums(sums, conv, conv * conv)

    @pl.when(g == spread_over)
    def _():
        moving.finish()
        sum_over_owners(members, sums, total, *exchange[1:])


def second_kernel(
    members, steps, tiles, y_ref, t_ref, n_ref, w_ref, conv_ref, act_ref, total, wide, *exchange
):
    g = pl.program_id(0)
    sums = exchange[0]

    @pl.when(g == 0)
    def _():
        signal_peers([("dp", members)])
        clear_edges(wide)
        sums[...] = jnp.zeros_like(sums)

    @pl.when(g < steps)
    def _():
        per = steps // wide.shape[0]
        center, inverse, gain, shift = norm_rows(t_ref, n_ref, 0, pixel_count(wide, members))

        def one(i, carry):
            values = y_ref[0, pl.ds(3 * i, 3)]
            normed = gain * ((values - center) * inverse) + shift
            act = jax.nn.silu(normed).astype(jnp.bfloat16)
            act_ref[0, pl.ds(3 * i, 3)] = act
            act = act.astype(jnp.float32)
            spread_columns(wide, g // per, lax.rem(g, per) * CHUNK + 3 * i, act)
            sums[2:3] += jnp.sum(act, axis=(0, 1))[None]
            return carry

        lax.fori_loop(0, CHUNK // 3, one, 0)

    @pl.when(g >= steps)
    def _():
        per = tiles // wide.shape[0]
        t = g - steps
        parts = [w_ref[:, part] for part in range(w_ref.shape[1])]
        conv = conv_tile(wide, parts, t // per, lax.rem(t, per) * TILE, TILE)
        conv_ref[...] = conv
        add_sums(sums, conv, conv * conv)

    @pl.when(g == steps + tiles - 1)
    def _():
        wait_peers([("dp", members)])
        sum_over_owners(members, sums, total, *exchange[1:])


def map_specs(images, height, width, channels):
    per = height // CHUNK
    steps = images * per
    stream = pl.BlockSpec(
        (1, CHUNK, width, channels),
        lambda g: (jnp.minimum(g, steps - 1) // per, lax.rem(jnp.minimum(g, steps - 1), per), 0, 0),
    )
    rows = pl.BlockSpec((TILE * width, channels), lambda g: (jnp.maximum(g - steps, 0), 0))
    return steps, images * (height // TILE), stream, rows


def fixed(*shape):
    return pl.BlockSpec(shape, lambda g: (0,) * len(shape))


def first_conv_call(x, trunk, head, note, identity):
    images, height, width, channels = x.shape
    steps, tiles, stream, rows = map_specs(*x.shape)
    pixels = images * height * width
    members = lax.axis_size("dp")
    layers, taps, shard_rows, _ = trunk.shape
    layout = weight_plans(members, taps)
    plans, dims, _ = layout
    entries = sum(len(plan) for plan, _ in plans)
    depth = max(len(digits) for digits in dims)
    matrix = (taps,) + (2,) * len(dims[0]) + (shard_rows, 128)
    branch = head.shape[3]
    anywhere = pl.BlockSpec(memory_space=pl.ANY)
    conv, total, full, heads = pl.pallas_call(
        functools.partial(first_kernel, members, steps, tiles, layout),
        grid=(steps + tiles,),
        in_specs=[stream, anywhere, anywhere, fixed(*note.shape)],
        out_specs=(rows, fixed(*note.shape), anywhere, anywhere),
        out_shape=(
            jax.ShapeDtypeStruct((pixels, channels), jnp.float32),
            jax.ShapeDtypeStruct(note.shape, jnp.float32),
            jax.ShapeDtypeStruct(matrix, trunk.dtype),
            jax.ShapeDtypeStruct((2,) + (2,) * len(dims[2]) + (shard_rows, branch), head.dtype),
        ),
        scratch_shapes=[
            pltpu.VMEM((images, height + 2 * DILATION_STEP, width, 3 * channels), jnp.bfloat16),
            pltpu.VMEM(matrix, trunk.dtype),
            pltpu.SemaphoreType.DMA((entries, 2)),
            pltpu.SemaphoreType.DMA((entries, depth)),
            pltpu.SemaphoreType.DMA((entries, depth)),
        ]
        + sum_scratch(members, note.shape[0], channels),
        compiler_params=summing(identity),
        name="first_conv",
    )(x, trunk, head[0], note)
    full = full.reshape(taps, TASKS, channels, 128)
    return conv, total, full, heads.reshape(2, channels, branch)


def second_conv_call(y, totals, gains, weights, shape, identity):
    images, height, width, channels = shape
    steps, tiles, stream, rows = map_specs(*shape)
    pixels = images * height * width
    members = lax.axis_size("dp")
    return pl.pallas_call(
        functools.partial(second_kernel, members, steps, tiles),
        grid=(steps + tiles,),
        in_specs=[stream, fixed(8, channels), fixed(4, channels), fixed(*weights.shape)],
        out_specs=(rows, stream, fixed(8, channels)),
        out_shape=(
            jax.ShapeDtypeStruct((pixels, channels), jnp.float32),
            jax.ShapeDtypeStruct(shape, jnp.bfloat16),
            jax.ShapeDtypeStruct((8, channels), jnp.float32),
        ),
        scratch_shapes=[
            pltpu.VMEM((images, height + 2 * DILATION_STEP, width, 3 * channels), jnp.bfloat16)
        ]
        + sum_scratch(members, 8, channels),
        compiler_params=summing(identity),
        name="second_conv",
    )(y.reshape(shape), totals, gains, weights)


def deltas(
    g, steps, members, layer, x_ref, up_ref, y_ref, t_ref, n_ref, b_ref, edge_ref, back_ref, wide, back
):
    images, padded, width, channels = wide.shape
    channels = channels // 3
    height = padded - 2 * DILATION_STEP

    @pl.when(g == 0)
    def _():
        clear_edges(wide)
        edge_ref[...] = jnp.zeros_like(edge_ref)

    @pl.when(g < steps)
    def _():
        per = steps // images
        column = lax.broadcasted_iota(jnp.int32, (1, 8, channels), 1)
        pixels = pixel_count(wide, members)
        center, inverse, gain, _ = norm_rows(t_ref, n_ref, layer, pixels)
        lean, slant = b_ref[0:1] / pixels, b_ref[1:2] / pixels

        def one(i, carry):
            place = pl.ds(3 * i, 3)
            row = lax.rem(g, per) * CHUNK + 3 * i
            spread_columns(wide, g // per, row, x_ref[0, place].astype(jnp.float32))
            centered = (y_ref[0, place] - center) * inverse
            values = gain * inverse * (up_ref[0, place] - lean - centered * slant)
            values = values.astype(jnp.bfloat16)
            if back_ref is not None:
                back_ref[0, place] = values
            back[g // per, pl.ds(row, 3)] = values
            values = values.astype(jnp.float32)
            whole = jnp.sum(values, axis=1)
            first = jnp.sum(jnp.where(column < DILATION_STEP, values[:, :8], 0.0), axis=1)
            last = jnp.sum(
                jnp.where(column >= 8 - DILATION_STEP, values[:, width - 8 :], 0.0), axis=1
            )
            for kernel_column, line in enumerate((whole - first, whole, whole - last)):
                for kernel_row in range(3):
                    at = row + DILATION_STEP * (kernel_row - 1)
                    part = [
                        jnp.where((at + r >= 0) & (at + r < height), line[r : r + 1], 0.0)
                        for r in range(3)
                    ]
                    tap = 3 * kernel_row + kernel_column
                    edge_ref[tap + 2 : tap + 3] += part[0] + part[1] + part[2]
            return carry

        lax.fori_loop(0, CHUNK // 3, one, 0)


def tap_gradient(wide, back, members, tap_row, column, t_ref, line):
    images, height, width, channels = back.shape
    total = None
    for image in range(images):
        part = dot(
            window(wide, image, 0, height, tap_row, column),
            back[image].reshape(height * width, channels),
            CONTRACT_ROWS,
        )
        total = part if total is None else total + part
    mean = jnp.swapaxes(t_ref[...], 0, 1)[:, 2:3] / pixel_count(wide, members)
    return total - mean * line


def weight_kernel(
    steps, members, cut, x_ref, up_ref, y_ref, t_ref, n_ref, b_ref, extra_ref, keep_ref, send_ref,
    keep_rest, send_rest, edge_ref, back_ref, wide, back, whole,
):
    g = pl.program_id(0)
    mine = lax.rem(lax.axis_index("dp"), 2)
    deltas(
        g, steps, members, 1, x_ref, up_ref, y_ref, t_ref, n_ref, b_ref, edge_ref, back_ref, wide, back
    )
    for column in range(3):

        @pl.when((g >= steps) & (lax.rem(g - steps, 3) == column))
        def _():
            line = edge_ref[pl.ds(g - steps + 2, 1)]
            grad = tap_gradient(wide, back, members, (g - steps) // 3, column, t_ref, line)
            whole[...] = grad.reshape(whole.shape)

    @pl.when((g >= steps) & (g < steps + cut))
    def _():
        keep_ref[0] = whole[:, mine].astype(keep_ref.dtype)
        send_ref[0] = whole[:, 1 - mine].astype(send_ref.dtype)

    @pl.when(g == steps + cut)
    def _():
        keep_ref[0] = extra_ref[:, mine]
        send_ref[0] = extra_ref[:, 1 - mine]

    @pl.when(g >= steps + cut)
    def _():
        keep_rest[0] = whole[:, mine].astype(keep_rest.dtype)
        send_rest[0] = whole[:, 1 - mine].astype(send_rest.dtype)


def weight_grad_call(x, upstream, y, totals, gains, backs, extra, cut):
    images, height, width, channels = x.shape
    steps, tiles, stream, rows = map_specs(*x.shape)
    members = lax.axis_size("dp")
    shape = (members // 2, channels // members, channels)

    def part(first, count):
        return pl.BlockSpec(
            (1,) + shape, lambda g: (jnp.clip(g - steps - first, 0, count - 1), 0, 0, 0)
        )

    ahead, rest = part(0, cut + 1), part(cut, 9 - cut)
    ahead_shape = jax.ShapeDtypeStruct((cut + 1,) + shape, jnp.bfloat16)
    rest_shape = jax.ShapeDtypeStruct((9 - cut,) + shape, jnp.bfloat16)
    extra = extra.reshape(shape[:1] + (2,) + shape[1:])
    return pl.pallas_call(
        functools.partial(weight_kernel, steps, members, cut),
        grid=(steps + 9,),
        in_specs=[
            stream,
            stream,
            stream,
            fixed(8, channels),
            fixed(4, channels),
            fixed(16, channels),
            fixed(*extra.shape),
        ],
        out_specs=(ahead, ahead, rest, rest, fixed(16, channels), stream),
        out_shape=(
            ahead_shape,
            ahead_shape,
            rest_shape,
            rest_shape,
            jax.ShapeDtypeStruct((16, channels), jnp.float32),
            jax.ShapeDtypeStruct(x.shape, jnp.bfloat16),
        ),
        scratch_shapes=[
            pltpu.VMEM((images, height + 2 * DILATION_STEP, width, 3 * channels), jnp.bfloat16),
            pltpu.VMEM((images, height, width, channels), jnp.bfloat16),
            pltpu.VMEM(shape[:1] + (2,) + shape[1:], jnp.float32),
        ],
        compiler_params=PARAMS,
        name="weight_grad",
    )(x, upstream.reshape(x.shape), y.reshape(x.shape), totals, gains, backs, extra)


def act_grad_kernel(
    members, steps, tiles, back_ref, y_ref, t_ref, n_ref, w_ref, note_ref, up_ref, total, wide, *exchange
):
    g = pl.program_id(0)
    sums = exchange[0]

    @pl.when(g == 0)
    def _():
        signal_peers([("dp", members)])
        clear_edges(wide)
        sums[...] = note_ref[...]

    @pl.when(g < steps)
    def _():
        per = steps // wide.shape[0]

        def one(i, carry):
            spread_columns(
                wide,
                g // per,
                lax.rem(g, per) * CHUNK + 3 * i,
                back_ref[0, pl.ds(3 * i, 3)].astype(jnp.float32),
            )
            return carry

        lax.fori_loop(0, CHUNK // 3, one, 0)

    @pl.when(g >= steps)
    def _():
        per = tiles // wide.shape[0]
        t = g - steps
        grad = conv_tile_back(wide, w_ref, t // per, lax.rem(t, per) * TILE, TILE)
        center, inverse, gain, shift = norm_rows(t_ref, n_ref, 0, pixel_count(wide, members))
        centered = (y_ref[...] - center) * inverse
        upstream = grad * silu_slope(gain * centered + shift)
        up_ref[...] = upstream
        add_sums(sums, upstream, upstream * centered)

    @pl.when(g == steps + tiles - 1)
    def _():
        wait_peers([("dp", members)])
        sum_over_owners(members, sums, total, *exchange[1:])


def act_grad_call(back, y, totals, gains, weights, note, identity):
    images, height, width, channels = back.shape
    steps, tiles, stream, rows = map_specs(*back.shape)
    pixels = images * height * width
    members = lax.axis_size("dp")
    return pl.pallas_call(
        functools.partial(act_grad_kernel, members, steps, tiles),
        grid=(steps + tiles,),
        in_specs=[
            stream,
            rows,
            fixed(8, channels),
            fixed(4, channels),
            fixed(*weights.shape),
            fixed(*note.shape),
        ],
        out_specs=(rows, fixed(16, channels)),
        out_shape=(
            jax.ShapeDtypeStruct((pixels, channels), jnp.float32),
            jax.ShapeDtypeStruct((16, channels), jnp.float32),
        ),
        scratch_shapes=[
            pltpu.VMEM((images, height + 2 * DILATION_STEP, width, 3 * channels), jnp.bfloat16)
        ]
        + sum_scratch(members, 16, channels),
        compiler_params=summing(identity),
        name="act_grad",
    )(back, y, totals, gains, weights, note)


def update_kernel(
    place_ref, g_ref, rows_ref, cols_ref, left_ref, right_ref, master_ref, lroot_ref, rroot_ref,
    grad_out, left_out, right_out, master_out, copy_out, gram,
):
    parts = g_ref.shape[1]
    shard_rows = left_ref.shape[1]
    full = jnp.concatenate([g_ref[0, part] for part in range(parts)], axis=1)
    rows = jnp.concatenate([rows_ref[0, part] for part in range(parts)], axis=1)
    grad_out[0] = rows.astype(jnp.float32)
    left_out[0] = 0.5 * left_ref[0] + 0.5 * dot(rows, full, CONTRACT_COLS)
    gram[...] = dot(cols_ref[0, 0], full, CONTRACT_ROWS)
    right_out[0] = 0.5 * right_ref[0] + 0.5 * gram[
        pl.ds(pl.multiple_of(place_ref[2], 8), shard_rows)
    ]
    turned = dot(lroot_ref[0].astype(jnp.bfloat16), full).astype(jnp.bfloat16)
    step = dot(turned, rroot_ref[0].astype(jnp.bfloat16))
    master = master_ref[0]
    master = master - RATE_TRUNK * (step + WEIGHT_DECAY * master)
    master_out[0] = master
    copy_out[0] = master.astype(jnp.bfloat16)


def update_call(owner, combined, left, right, master, lroot, rroot):
    layers, taps, shard_rows, channels = left.shape
    count, parts, _, width = combined.shape
    one = pl.BlockSpec((1, shard_rows, channels), lambda g, place: (g, 0, 0))
    whole = pl.BlockSpec((1, channels, channels), lambda g, place: (g, 0, 0))
    flat = (count, shard_rows, channels)
    start = owner * shard_rows
    place = jnp.stack([owner, start // width, lax.rem(start, width)]).astype(jnp.int32)
    outs = pl.pallas_call(
        update_kernel,
        grid_spec=pltpu.PrefetchScalarGridSpec(
            num_scalar_prefetch=1,
            grid=(count,),
            in_specs=[
                pl.BlockSpec((1, parts, channels, width), lambda g, place: (g, 0, 0, 0)),
                pl.BlockSpec((1, parts, shard_rows, width), lambda g, place: (g, 0, place[0], 0)),
                pl.BlockSpec((1, 1, channels, width), lambda g, place: (g, place[1], 0, 0)),
                one,
                one,
                one,
                one,
                whole,
            ],
            out_specs=(one,) * 5,
            scratch_shapes=[pltpu.VMEM((width, channels), jnp.float32)],
        ),
        out_shape=tuple(
            jax.ShapeDtypeStruct(flat, kind)
            for kind in (jnp.float32, jnp.float32, jnp.float32, jnp.float32, jnp.bfloat16)
        ),
        compiler_params=PARAMS,
        name="update",
    )(
        place,
        combined,
        combined,
        combined,
        left.reshape(flat),
        right.reshape(flat),
        master.reshape(flat),
        lroot.reshape(flat),
        rroot.reshape(count, channels, channels),
    )
    return [out.reshape(left.shape) for out in outs]


def combined_plan(members, taps):
    bits = owner_bits(members)
    last = bits[-1:]
    plain = tuple(bits) + (FAR, CORE)
    other = tuple(bits[:-1]) + (FAR,) + tuple(last) + (CORE,)
    early = tuple(last) + (FAR,) + tuple(bits[:-1]) + (CORE,)
    first = (FAR,) + tuple(last) + tuple(bits[:-1]) + (CORE,)
    return [spread([plain, other, plain, other, early, first] * 3, taps, 6)], [[FAR, CORE] + bits]


PAIRS = [(i, j) for i in range(TASKS) for j in range(i, TASKS)]


def mix_kernel(
    members, plans, dims, sum_ref, mean_ref, edge_ref, scale_ref, conflict_ref,
    notes_ref, full_ref, pair_ref, notes_out, own, sent, held, products, dp_slots, partial,
    task_slots, mixed, block_send, block_recv, note_send, note_recv, dp_send, dp_recv, task_send,
    task_recv, local_sem, send_sem, recv_sem,
):
    task = lax.axis_index("task")
    owner = lax.axis_index("dp")
    taps = held.shape[1] // 2
    greet_peers([("dp", members), ("task", TASKS)])
    notes = share("task", TASKS, lambda peer: notes_ref, notes_out, note_send, note_recv)
    notes_out[task] = notes_ref[...]
    for layer in range(2):

        def one(tap, carry):
            grad = sum_ref[layer * taps + tap] + mean_ref[layer] * edge_ref[layer, pl.ds(tap + 2, 1)]
            grad = (grad * scale_ref[0:1]).astype(jnp.bfloat16)
            for part in range(TASKS):
                sent[part, layer * taps + tap] = grad[:, part * 128 : (part + 1) * 128]
            return carry

        lax.fori_loop(0, taps, one, 0)
    blocks = share("task", TASKS, lambda peer: sent.at[peer], held, block_send, block_recv)
    local = pltpu.make_async_copy(sent.at[task], held.at[task], own.at[0])
    local.start()
    local.wait()
    await_shares("task", TASKS, lambda peer: sent.at[peer], held, block_send, block_recv)
    width = held.shape[3]

    def multiply(tap, sums):
        values = [held[t, tap].astype(jnp.float32) for t in range(TASKS)]
        return tuple(
            total
            + jnp.sum((values[i] * values[j]).reshape(-1, 8, width), axis=0)
            for total, (i, j) in zip(sums, PAIRS)
        )

    sums = lax.fori_loop(
        0, 2 * taps, multiply, tuple(jnp.zeros((8, width), jnp.float32) for _ in PAIRS)
    )
    for row, total in enumerate(sums):
        products[row : row + 1] = jnp.sum(total, axis=0, keepdims=True)
    products[len(PAIRS) : 16] = jnp.zeros((16 - len(PAIRS), width), jnp.float32)
    over_dp = share("dp", members, lambda peer: products, dp_slots, dp_send, dp_recv)
    dp_slots[owner] = products[...]
    await_shares("dp", members, lambda peer: products, dp_slots, dp_send, dp_recv)
    partial[...] = slot_total(dp_slots)
    over_task = share("task", TASKS, lambda peer: partial, task_slots, task_send, task_recv)
    task_slots[task] = partial[...]
    await_shares("task", TASKS, lambda peer: partial, task_slots, task_send, task_recv)
    total = jnp.broadcast_to(
        jnp.sum(slot_total(task_slots), axis=1, keepdims=True), products.shape
    )
    rows = {pair: total[row : row + 1] for row, pair in enumerate(PAIRS)}
    weights = []
    for j in range(TASKS):
        weight = jnp.ones((1, width), jnp.float32)
        for i in range(TASKS):
            pair = rows[min(i, j), max(i, j)]
            pair_ref[TASKS * i + j : TASKS * i + j + 1] = pair
            if i != j:
                at = TASKS * i + j
                weight = weight - conflict_ref[at : at + 1] * pair / (rows[j, j] + GRAM_EPS)
        weights.append(weight)

    def blend(tap, carry):
        value = weights[0] * held[0, tap].astype(jnp.float32)
        for t in range(1, TASKS):
            value = value + weights[t] * held[t, tap].astype(jnp.float32)
        mixed[tap] = value.astype(jnp.bfloat16)
        return carry

    lax.fori_loop(0, 2 * taps, blend, 0)
    Gather(plans, dims, [False], [mixed], [full_ref], local_sem, send_sem, recv_sem).run()
    await_shares("task", TASKS, lambda peer: notes_ref, notes_out, note_send, note_recv)
    for copy in notes + blocks + over_dp + over_task:
        copy.wait_send()


def mix_call(sums, taps, means, edges, scale, conflict, notes, identity):
    members = lax.axis_size("dp")
    _, shard_rows, channels = sums.shape
    plans, dims = combined_plan(members, 2 * taps)
    width = channels // TASKS
    vmem = pl.BlockSpec(memory_space=pltpu.VMEM)
    dma = pltpu.SemaphoreType.DMA
    entries = len(plans[0][0])
    full, pairs, notes = pl.pallas_call(
        functools.partial(mix_kernel, members, plans, dims),
        out_shape=(
            jax.ShapeDtypeStruct(
                (2 * taps,) + (2,) * len(dims[0]) + (shard_rows, width), jnp.bfloat16
            ),
            jax.ShapeDtypeStruct((16, width), jnp.float32),
            jax.ShapeDtypeStruct((TASKS,) + notes.shape, jnp.float32),
        ),
        in_specs=[vmem] * 6,
        out_specs=(pl.BlockSpec(memory_space=pl.ANY), vmem, vmem),
        scratch_shapes=[
            dma((1,)),
            pltpu.VMEM((TASKS, 2 * taps, shard_rows, width), jnp.bfloat16),
            pltpu.VMEM((TASKS, 2 * taps, shard_rows, width), jnp.bfloat16),
            pltpu.VMEM((16, width), jnp.float32),
            pltpu.VMEM((members, 16, width), jnp.float32),
            pltpu.VMEM((16, width), jnp.float32),
            pltpu.VMEM((TASKS, 16, width), jnp.float32),
            pltpu.VMEM((2 * taps, shard_rows, width), jnp.bfloat16),
            dma((TASKS,)),
            dma((TASKS,)),
            dma((TASKS,)),
            dma((TASKS,)),
            dma((members,)),
            dma((members,)),
            dma((TASKS,)),
            dma((TASKS,)),
            dma((entries, 2)),
            dma((entries, len(dims[0]))),
            dma((entries, len(dims[0]))),
        ],
        compiler_params=pltpu.CompilerParams(
            collective_id=identity, has_side_effects=True, vmem_limit_bytes=40 * 1024 * 1024
        ),
        name="mix",
    )(sums, means, edges, scale, conflict, notes)
    return full.reshape(2 * taps, TASKS, members * shard_rows, width), pairs, notes


def reduce_kernel(
    members, stages, cut, steps, x_ref, up_ref, y_ref, t_ref, n_ref, b_ref, keep_ahead, got_ahead,
    keep_rest, send_rest, *refs
):
    sum_ref, edge_out, wide, back, edge_ref, part_ref = refs[:6]
    buffers, (slots, send_sem, recv_sem, slot_send, slot_recv) = refs[6:-5], refs[-5:]
    g = pl.program_id(0)
    got = buffers[:stages]
    sent = (None,) + tuple(buffers[stages : 2 * stages - 1])
    kept = (None,) + tuple(buffers[2 * stages - 1 :])
    taps = part_ref.shape[0]
    dims = [("dp", 1 << stage) for stage in range(stages)]
    own, ahead, rest = "own", "ahead", "rest"
    starts = [(own, tap) for tap in range(taps)]
    starts += [(ahead, tap) for tap in range(cut)]
    starts += [(rest, tap) for tap in range(taps - cut)]
    starts += [(ahead, cut)]
    whole = [entry for entry, (kind, _) in enumerate(starts) if kind != ahead]

    def landed(stage, entry):
        return got[stage].at[entry if stage else whole.index(entry)]

    def copy_of(stage, entry):
        kind, tap = starts[entry]
        mine, device = partner(dims[stage])
        if stage:
            source = sent[stage].at[entry]
        elif kind == own:
            source = part_ref.at[tap, :, 1 - mine]
        else:
            source = send_rest.at[tap]
        return pltpu.make_async_remote_copy(
            src_ref=source,
            dst_ref=landed(stage, entry),
            send_sem=send_sem.at[stage, entry],
            recv_sem=recv_sem.at[stage, entry],
            device_id=device,
            device_id_type=pl.DeviceIdType.MESH,
        )

    def total_of(stage, entry, at):
        kind, tap = starts[entry]
        if stage:
            value = kept[stage][entry, at]
        elif kind == own:
            value = part_ref[tap, at, partner(dims[0])[0]]
        elif kind == rest:
            value = keep_rest[tap, at]
        else:
            value = keep_ahead[tap, at]
        if stage == 0 and kind == ahead:
            other = got_ahead[tap, at]
        else:
            other = landed(stage, entry)[at]
        return value.astype(jnp.float32) + other.astype(jnp.float32)

    def advance(stage, entry):
        if stage or entry in whole:
            copy_of(stage, entry).wait_recv()
        if stage == stages - 1:
            sum_ref[entry] = total_of(stage, entry, 0)
            return
        following = partner(dims[stage + 1])[0]
        for block in range((members >> (stage + 1)) // 2):
            for half in range(2):
                at = 2 * block + (following if half else 1 - following)
                value = total_of(stage, entry, at)
                if half:
                    kept[stage + 1][entry, block] = value
                else:
                    sent[stage + 1][entry, block] = value.astype(jnp.bfloat16)
        copy_of(stage + 1, entry).start()

    @pl.when(g == 0)
    def _():
        greet_peers([("dp", members)])
        for entry, (kind, _) in enumerate(starts):
            if kind == rest:
                copy_of(0, entry).start()
        for entry, (kind, _) in enumerate(starts):
            if kind == ahead:
                advance(0, entry)

    deltas(g, steps, members, 0, x_ref, up_ref, y_ref, t_ref, n_ref, b_ref, edge_ref, None, wide, back)

    @pl.when(g == steps)
    def _():
        share("dp", members, lambda peer: edge_ref, slots, slot_send, slot_recv)
        slots[lax.axis_index("dp")] = edge_ref[...]

    waiting = [[] for _ in range(stages)]
    waiting[0] += [entry for entry, (kind, _) in enumerate(starts) if kind == rest]
    waiting[1] += [entry for entry, (kind, _) in enumerate(starts) if kind == ahead]

    def turn():
        moved = []
        for stage in range(stages - 1, -1, -1):
            if waiting[stage]:
                entry = waiting[stage].pop(0)
                advance(stage, entry)
                if stage + 1 < stages:
                    moved.append((stage + 1, entry))
        for stage, entry in moved:
            waiting[stage].append(entry)

    for tap in range(taps):

        @pl.when(g == steps + tap)
        def _():
            grad = tap_gradient(
                wide, back, members, tap // 3, tap % 3, t_ref, edge_ref[tap + 2 : tap + 3]
            )
            part_ref[tap] = grad.reshape(part_ref.shape[1:]).astype(part_ref.dtype)
            copy_of(0, tap).start()
            if tap >= 4:
                turn()

    @pl.when(g == steps + taps - 1)
    def _():
        waiting[0].extend(range(taps))
        while any(waiting):
            turn()
        await_shares("dp", members, lambda peer: edge_ref, slots, slot_send, slot_recv)
        edge_out[...] = slot_total(slots)
        for entry in range(len(starts)):
            for stage in range(0 if entry in whole else 1, stages):
                copy_of(stage, entry).wait_send()
        await_sends("dp", members, lambda peer: edge_ref, slots, slot_send, slot_recv)


def reduce_call(x, upstream, y, totals, gains, backs, ahead, rest, identity):
    images, height, columns, channels = x.shape
    steps, _, stream, _ = map_specs(*x.shape)
    members = lax.axis_size("dp")
    stages = members.bit_length() - 1
    taps, width = 9, channels
    shard_rows = channels // members
    cut = ahead[0].shape[0] - 1
    entries, whole = 2 * taps + 1, 2 * taps - cut
    vmem = pl.BlockSpec(memory_space=pltpu.VMEM)
    dma = pltpu.SemaphoreType.DMA

    def blocks(stage, kind):
        held = entries if stage else whole
        return pltpu.VMEM((held, members >> (stage + 1), shard_rows, width), kind)

    late_arrays = ahead + rest

    return pl.pallas_call(
        functools.partial(reduce_kernel, members, stages, cut, steps),
        grid=(steps + taps,),
        out_shape=(
            jax.ShapeDtypeStruct((entries, shard_rows, width), jnp.float32),
            jax.ShapeDtypeStruct((16, channels), jnp.float32),
        ),
        in_specs=[stream, stream, stream, fixed(8, channels), fixed(4, channels), fixed(16, channels)]
        + [vmem] * len(late_arrays),
        out_specs=(vmem, vmem),
        scratch_shapes=[
            pltpu.VMEM((images, height + 2 * DILATION_STEP, columns, 3 * channels), jnp.bfloat16),
            pltpu.VMEM((images, height, columns, channels), jnp.bfloat16),
            pltpu.VMEM((16, channels), jnp.float32),
            pltpu.VMEM((taps, members // 2, 2, shard_rows, width), jnp.bfloat16),
        ]
        + [blocks(stage, jnp.bfloat16) for stage in range(stages)]
        + [blocks(stage, jnp.bfloat16) for stage in range(1, stages)]
        + [blocks(stage, jnp.float32) for stage in range(1, stages)]
        + [
            pltpu.VMEM((members, 16, channels), jnp.float32),
            dma((stages, entries)),
            dma((stages, entries)),
            dma((members,)),
            dma((members,)),
        ],
        compiler_params=summing(identity),
        name="reduce",
    )(
        x,
        upstream.reshape(x.shape),
        y.reshape(x.shape),
        totals,
        gains,
        backs,
        *late_arrays,
    )


def pad_rows(parts, rows):
    used = sum(part.shape[0] for part in parts)
    if used < rows:
        parts = list(parts) + [jnp.zeros((rows - used, parts[0].shape[1]), jnp.float32)]
    return jnp.concatenate(parts)


def boundary(labels):
    across = jnp.pad(
        (labels[:, :, 1:] != labels[:, :, :-1]).astype(jnp.float32), ((0, 0), (0, 0), (0, 1))
    )
    downward = jnp.pad(
        (labels[:, 1:, :] != labels[:, :-1, :]).astype(jnp.float32), ((0, 0), (0, 1), (0, 0))
    )
    return jnp.maximum(across, downward)


def pixel_rows(labels, depth_mask, depth_target, normal_target):
    images, height, width = labels.shape
    rows = jnp.stack(
        [
            labels.astype(jnp.float32),
            depth_mask.astype(jnp.float32),
            boundary(labels),
            depth_target,
        ],
        axis=1,
    )
    rows = jnp.concatenate([rows, normal_target, jnp.zeros_like(rows[:, :1])], axis=1)
    rows = rows.reshape(images, 8, height // CHUNK, CHUNK * width)
    return jnp.swapaxes(rows, 1, 2)


def head_kernel(
    members, chunks, images, y_ref, x_ref, t_ref, n_ref, head_ref, out_ref, bias_ref, info_ref, weight_ref,
    up_ref, grad_ref, total, trunk, hidden_pre, pre_grads, pooled, base, per_image, matrix, *exchange,
):
    image, step = pl.program_id(0), pl.program_id(1)
    last = images - 1
    sums = exchange[0]
    rows = CHUNK * y_ref.shape[2]
    channels = y_ref.shape[3]
    area = float(chunks * rows)
    pixels = area * images * members
    phase = step // chunks
    place = pl.ds(lax.rem(step, chunks) * rows, rows)

    @pl.when((image == 0) & (step == 0))
    def _():
        signal_peers([("dp", members)])
        sums[...] = jnp.zeros_like(sums)
        matrix[...] = jnp.zeros_like(matrix)

    @pl.when(step == 0)
    def _():
        pooled[...] = jnp.zeros_like(pooled)
        per_image[...] = jnp.zeros_like(per_image)

    def residual():
        center, inverse, gain, shift = norm_rows(t_ref, n_ref, 1, pixels)
        centered = (y_ref[0].reshape(rows, channels) - center) * inverse
        inputs = x_ref[0].reshape(rows, channels).astype(jnp.float32)
        return centered, gain * centered + shift + inputs

    @pl.when(phase == 0)
    def _():
        _, before = residual()
        act = jax.nn.silu(before).astype(jnp.bfloat16)
        trunk[place] = act
        pooled[0:1] += jnp.sum(act.astype(jnp.float32), axis=0, keepdims=True)

    @pl.when(step == chunks)
    def _():
        mean = jnp.broadcast_to((pooled[0:1] / area).astype(jnp.bfloat16), (16, channels))
        base[...] = dot(mean, head_ref[1])[0:8] + bias_ref[...]

    @pl.when(phase == 1)
    def _():
        act = trunk[place]
        before = dot(act, head_ref[0]) + base[0:1]
        sigmoid = jax.nn.sigmoid(before)
        hidden = (before * sigmoid).astype(jnp.bfloat16)
        logits = dot(out_ref[...], hidden, CONTRACT_COLS)
        info = info_ref[0, 0]
        weight = [weight_ref[0, t : t + 1, 0:1] for t in range(TASKS)]
        classes = logits[:CLASSES]
        largest = jnp.max(classes, axis=0, keepdims=True)
        powers = jnp.exp(classes - largest)
        power = jnp.sum(powers, axis=0, keepdims=True)
        index = lax.broadcasted_iota(jnp.int32, classes.shape, 0).astype(jnp.float32)
        chosen = index == info[0:1]
        picked = jnp.sum(jnp.where(chosen, classes, 0.0), axis=0, keepdims=True)
        segment = jnp.log(power) + largest - picked
        class_grad = weight[0] * (powers / power - jnp.where(chosen, 1.0, 0.0))
        offset = logits[CLASSES : CLASSES + 1] - info[3:4]
        length = jnp.sqrt(offset * offset + 1.0)
        depth_grad = weight[1] * info[1:2] * (offset / length)
        predicted = logits[CLASSES + 1 : CLASSES + 4]
        normal = info[4:7]
        product = jnp.sum(predicted * normal, axis=0, keepdims=True)
        square = jnp.sum(predicted * predicted, axis=0, keepdims=True) + 1.0
        scale = lax.rsqrt(square * (jnp.sum(normal * normal, axis=0, keepdims=True) + 1.0))
        cosine = product * scale
        normal_grad = -weight[2] * (normal * scale - cosine * predicted / square)
        edge = logits[CLASSES + 4 : CLASSES + 5]
        softplus = jnp.maximum(edge, 0.0) + jnp.log1p(jnp.exp(-jnp.abs(edge)))
        edge_grad = weight[3] * (jax.nn.sigmoid(edge) - info[2:3])
        losses = (
            weight[0] * segment,
            weight[1] * info[1:2] * (length - 1.0),
            weight[2] * (1.0 - cosine),
            weight[3] * (softplus - info[2:3] * edge),
        )
        lane = lax.broadcasted_iota(jnp.int32, (1, channels), 1)
        for t, loss in enumerate(losses):
            value = jnp.sum(loss, axis=1, keepdims=True)
            sums[2:3] += jnp.where(lane == BRANCH_WIDTH + t, value, 0.0)
        rest = jnp.zeros((out_ref.shape[0] - CLASSES - 5, rows), jnp.float32)
        grads = jnp.concatenate([class_grad, depth_grad, normal_grad, edge_grad, rest], axis=0)
        grads = grads.astype(jnp.bfloat16)
        out_grad = dot(grads, hidden)
        sums[3:12, :BRANCH_WIDTH] += out_grad[0:9]
        sums[3:12, BRANCH_WIDTH:] += out_grad[9:18]
        back = dot(grads, out_ref[...], CONTRACT_ROWS)
        back = (back * (sigmoid * (1.0 + before * (1.0 - sigmoid)))).astype(jnp.bfloat16)
        pre_grads[place] = back
        matrix[:, :BRANCH_WIDTH] += dot(act, back, CONTRACT_ROWS)
        per_image[0:1] += jnp.sum(back.astype(jnp.float32), axis=0, keepdims=True)

    @pl.when(step == 2 * chunks)
    def _():
        line = per_image[...]
        mean = pooled[...] / area
        mean = mean.astype(jnp.bfloat16).astype(jnp.float32)
        matrix[:, BRANCH_WIDTH:] += lax.dot_general(
            mean, line, CONTRACT_ROWS, precision=PRECISE, preferred_element_type=jnp.float32
        )
        sums[2:3, :BRANCH_WIDTH] += line[0:1]
        hidden_pre[...] = lax.dot_general(
            line,
            head_ref[1].astype(jnp.float32),
            CONTRACT_COLS,
            precision=PRECISE,
            preferred_element_type=jnp.float32,
        )

    @pl.when(phase == 2)
    def _():
        centered, before = residual()
        back = dot(pre_grads[place], head_ref[0], CONTRACT_COLS) + hidden_pre[0:1] / area
        upstream = back * silu_slope(before)
        up_ref[...] = upstream
        add_sums(sums, upstream, upstream * centered)

    @pl.when((image == last) & (step == 3 * chunks - 1))
    def _():
        grad_ref[...] = matrix[...].astype(grad_ref.dtype)
        wait_peers([("dp", members)])
        sum_over_owners(members, sums, total, *exchange[1:])


def head_call(y, x, totals, gains, head, out_rows, bias, info, weights, identity):
    images, height, width, channels = x.shape
    chunks = height // CHUNK
    rows = CHUNK * width
    members = lax.axis_size("dp")

    def again(b, c):
        return jnp.where(c // chunks == 1, chunks - 1, lax.rem(c, chunks))

    def constant(*shape):
        return pl.BlockSpec(shape, lambda b, c: (0,) * len(shape))

    stream = pl.BlockSpec((1, CHUNK, width, channels), lambda b, c: (b, again(b, c), 0, 0))
    return pl.pallas_call(
        functools.partial(head_kernel, members, chunks, images),
        grid=(images, 3 * chunks),
        in_specs=[
            stream,
            stream,
            constant(8, channels),
            constant(4, channels),
            constant(*head.shape),
            constant(*out_rows.shape),
            constant(1, BRANCH_WIDTH),
            pl.BlockSpec((1, 1, 8, rows), lambda b, c: (b, lax.rem(c, chunks), 0, 0)),
            pl.BlockSpec((1, 8, 128), lambda b, c: (b, 0, 0)),
        ],
        out_specs=(
            pl.BlockSpec(
                (rows, channels), lambda b, c: (b * chunks + jnp.maximum(c - 2 * chunks, 0), 0)
            ),
            constant(channels, 2 * BRANCH_WIDTH),
            constant(16, channels),
        ),
        out_shape=(
            jax.ShapeDtypeStruct((images * height * width, channels), jnp.float32),
            jax.ShapeDtypeStruct((channels, 2 * BRANCH_WIDTH), jnp.bfloat16),
            jax.ShapeDtypeStruct((16, channels), jnp.float32),
        ),
        scratch_shapes=[
            pltpu.VMEM((chunks * rows, channels), jnp.bfloat16),
            pltpu.VMEM((8, channels), jnp.float32),
            pltpu.VMEM((chunks * rows, BRANCH_WIDTH), jnp.bfloat16),
            pltpu.VMEM((8, channels), jnp.float32),
            pltpu.VMEM((8, BRANCH_WIDTH), jnp.float32),
            pltpu.VMEM((8, BRANCH_WIDTH), jnp.float32),
            pltpu.VMEM((channels, 2 * BRANCH_WIDTH), jnp.float32),
        ]
        + sum_scratch(members, 16, channels),
        compiler_params=summing(identity),
        name="heads",
    )(y.reshape(x.shape), x, totals, gains, head, out_rows, bias, info, weights)


def adamw_update(gradient, moment_one, moment_two, weight, rate):
    moment_one = 0.5 * moment_one + 0.5 * gradient
    moment_two = 0.5 * moment_two + 0.5 * gradient * gradient
    correction = 1.0 - 0.5**STEP
    weight = weight - rate * (
        moment_one / correction / (jnp.sqrt(moment_two / correction) + ADAM_EPS)
        + WEIGHT_DECAY * weight
    )
    return (moment_one, moment_two, weight)


def body(
    features,
    labels,
    depth_mask,
    depth_target,
    normal_target,
    scene_ids,
    task_weights,
    conflict,
    trunk_copy,
    trunk_master,
    trunk_left,
    trunk_right,
    left_root,
    right_root,
    head_copy,
    head_master,
    head_first,
    head_second,
    out_copy,
    out_master,
    out_first,
    out_second,
    trunk_gains,
    gains_first,
    gains_second,
    head_bias,
    bias_first,
    bias_second,
):
    images, feature_rows, feature_columns, channels = features.shape
    pixels = jnp.array(images * feature_rows * feature_columns * lax.axis_size("dp"), jnp.float32)
    task_index = lax.axis_index("task")
    owner_index = lax.axis_index("dp")
    local_valid = jnp.sum(depth_mask.astype(jnp.float32))
    first_note = jnp.where(jnp.arange(8)[:, None] == 3, local_valid, jnp.zeros((8, channels)))
    first_conv, first_totals, second_full, head_full = first_conv_call(
        features, trunk_copy, head_copy, first_note, 0
    )
    valid_count = first_totals[3, 0]
    second_conv, first_act, second_totals = second_conv_call(
        first_conv, first_totals, trunk_gains, second_full, features.shape, 1
    )
    selector = (jnp.arange(TASKS) == task_index).astype(jnp.float32)
    own_bias = jnp.sum(selector[:, None] * head_bias, axis=0, keepdims=True)
    choose = (scene_ids[:, None] == jnp.arange(task_weights.shape[0])[None, :]).astype(jnp.float32)
    image_weights = jnp.sum(choose[:, :, None] * task_weights[None], axis=1) * selector
    image_weights = jnp.broadcast_to(
        jnp.pad(image_weights, ((0, 0), (0, 8 - TASKS)))[:, :, None], (images, 8, 128)
    )
    out_rows = jnp.pad(out_copy.T, ((0, 32 - out_copy.shape[1]), (0, 0)))
    second_up, head_grad, second_back_sums = head_call(
        second_conv,
        features,
        second_totals,
        trunk_gains,
        head_full,
        out_rows,
        own_bias,
        pixel_rows(labels, depth_mask, depth_target, normal_target),
        image_weights,
        2,
    )
    keep_ahead, send_ahead, keep_rest, send_rest, second_edges, second_back = weight_grad_call(
        first_act,
        second_up,
        second_conv,
        second_totals,
        trunk_gains,
        second_back_sums,
        head_grad,
        6,
    )
    second_back, send_ahead = lax.optimization_barrier((second_back, send_ahead))
    members = lax.axis_size("dp")
    got_ahead = lax.ppermute(send_ahead, "dp", [(i, i ^ 1) for i in range(members)])
    first_up, first_back_sums = act_grad_call(
        second_back, first_conv, first_totals, trunk_gains, second_full, second_edges, 3
    )
    sums, first_edges = reduce_call(
        features,
        first_up,
        first_conv,
        first_totals,
        trunk_gains,
        first_back_sums,
        [keep_ahead, got_ahead],
        [keep_rest, send_rest],
        7,
    )
    edges = jnp.stack([first_edges, first_back_sums])
    means = jnp.stack([first_totals[2], second_totals[2]]) / pixels
    shard_rows = trunk_copy.shape[2]
    own_means = lax.dynamic_slice_in_dim(means, owner_index * shard_rows, shard_rows, 1)
    divisor = jnp.stack([pixels, valid_count, pixels, pixels])
    own_divisor = jnp.sum(divisor * selector)
    notes = pad_rows(
        [
            first_back_sums[1:2],
            first_back_sums[0:1],
            second_back_sums[1:2],
            second_back_sums[0:1],
            second_back_sums[2:12],
        ],
        16,
    )
    combined, pairs, notes = mix_call(
        sums,
        9,
        own_means[:, :, None],
        edges,
        jnp.full((8, channels), 1.0 / own_divisor),
        jnp.broadcast_to(
            conflict.astype(jnp.float32).reshape(TASKS * TASKS, 1), (TASKS * TASKS, 128)
        ),
        notes,
        6,
    )
    pair_products = pairs[:, 0].reshape(TASKS, TASKS)
    gains_total = jnp.sum(notes[:, 0:4] / divisor[:, None, None], axis=0)
    bias_total = notes[:, 4, :BRANCH_WIDTH] / divisor[:, None]
    loss_sum = jnp.sum(notes[:, 4, BRANCH_WIDTH : BRANCH_WIDTH + TASKS], axis=0)
    column_divisor = jnp.concatenate(
        [jnp.full((CLASSES,), divisor[0]), divisor[1:2], jnp.full((3,), divisor[2]), divisor[3:4]]
    )
    out_total = (
        jnp.concatenate(jnp.split(jnp.sum(notes[:, 5:14], axis=0), 2, axis=1)).T
        / column_divisor[None, :]
    )
    head_rows = jnp.stack(jnp.split(sums[18], 2, axis=1))[None]
    grad_rows, left_new, right_new, master_new, copy_new = update_call(
        owner_index, combined, trunk_left, trunk_right, trunk_master, left_root, right_root
    )
    head_one, head_two, head_new = adamw_update(
        head_rows / own_divisor, head_first, head_second, head_master, RATE_MATRIX
    )
    out_one, out_two, out_new = adamw_update(
        out_total, out_first, out_second, out_master, RATE_MATRIX
    )
    gain_one, gain_two, gain_new = adamw_update(
        gains_total, gains_first, gains_second, trunk_gains, RATE_VECTOR
    )
    bias_one, bias_two, bias_new = adamw_update(
        bias_total, bias_first, bias_second, head_bias, RATE_VECTOR
    )
    loss_terms = jnp.concatenate([loss_sum, valid_count[None]])
    return (
        grad_rows,
        left_new,
        right_new,
        master_new,
        copy_new,
        head_one,
        head_two,
        head_new,
        head_new.astype(jnp.bfloat16),
        out_one,
        out_two,
        out_new,
        out_new.astype(jnp.bfloat16),
        gain_one,
        gain_two,
        gain_new,
        bias_one,
        bias_two,
        bias_new,
        loss_terms,
        pair_products,
    )


def solution(mesh):
    rows = P(None, None, "dp", None)
    heads = P("task", None, "dp", None)
    images = P("dp")
    placed = (
        (images,) * 6
        + (P(), P())
        + (rows,) * 5
        + (P(),)
        + (heads,) * 4
        + (P(),) * 10
    )
    return jax.shard_map(
        body,
        mesh=mesh,
        in_specs=placed,
        out_specs=(rows,) * 5 + (heads,) * 4 + (P(),) * 12,
        check_vma=False,
    )
```

```python
import functools

import jax
import jax.numpy as jnp
from jax import lax
from jax.experimental import pallas as pl
from jax.experimental.pallas import tpu as pltpu
from jax.sharding import PartitionSpec as P

BRANCH_WIDTH = 256
CLASSES = 13
TASKS = 4
DILATION_STEP = 2
STEP = 5


PRECISE = lax.Precision.HIGHEST
NORM_EPS = 1e-05
RATE_TRUNK = 0.3
RATE_MATRIX = 0.05
RATE_VECTOR = 0.3
WEIGHT_DECAY = 0.01
ADAM_EPS = 1e-08
GRAM_EPS = 1e-12
PLAIN = (((1,), (0,)), ((), ()))
CONTRACT_ROWS = (((0,), (0,)), ((), ()))
CONTRACT_COLS = (((1,), (1,)), ((), ()))
CHUNK = 9
TILE = 12
VMEM_LIMIT = 58 * 1024 * 1024
PARAMS = pltpu.CompilerParams(vmem_limit_bytes=VMEM_LIMIT)


def summing(identity):
    return pltpu.CompilerParams(
        collective_id=identity, has_side_effects=True, vmem_limit_bytes=VMEM_LIMIT
    )


def silu_slope(tap_values):
    sigmoid = jax.nn.sigmoid(tap_values)
    return sigmoid * (1.0 + tap_values * (1.0 - sigmoid))


def dot(a, b, contract=PLAIN):
    return lax.dot_general(a, b, contract, preferred_element_type=jnp.float32)


def clear_edges(wide):
    rows = wide.shape[1]
    edge = jnp.zeros((wide.shape[0], DILATION_STEP) + wide.shape[2:], wide.dtype)
    wide[:, 0:DILATION_STEP] = edge
    wide[:, rows - DILATION_STEP : rows] = edge


def spread_columns(wide, image, row, values):
    width, channels = values.shape[1:]
    column = lax.broadcasted_iota(jnp.int32, (1, width, channels), 1)
    left = jnp.where(column >= DILATION_STEP, pltpu.roll(values, DILATION_STEP, 1), 0.0)
    right = jnp.where(
        column < width - DILATION_STEP, pltpu.roll(values, width - DILATION_STEP, 1), 0.0
    )
    place = pl.ds(DILATION_STEP + row, values.shape[0])
    for part, piece in enumerate((left, values, right)):
        wide[image, place, :, part * channels : (part + 1) * channels] = piece.astype(wide.dtype)


def window(wide, image, row, rows, kernel_row, part=None):
    channels = wide.shape[3] // 3
    place = pl.ds(row + DILATION_STEP * kernel_row, rows)
    if part is None:
        return wide[image, place].reshape(rows * wide.shape[2], 3 * channels)
    return wide[image, place, :, part * channels : (part + 1) * channels].reshape(
        rows * wide.shape[2], channels
    )


def conv_tile(wide, parts, image, row, rows):
    taps = jnp.concatenate([window(wide, image, row, rows, k) for k in range(3)], axis=1)
    parts = [part.reshape(-1, part.shape[-1]) for part in parts]
    return dot(taps, jnp.concatenate(parts, axis=1))


def conv_tile_back(wide, weights, image, row, rows):
    total = None
    for tap in range(9):
        kernel_row, kernel_column = divmod(tap, 3)
        part = dot(
            window(wide, image, row, rows, 2 - kernel_row, 2 - kernel_column),
            jnp.concatenate([weights[tap, part] for part in range(weights.shape[1])], axis=1),
            CONTRACT_COLS,
        )
        total = part if total is None else total + part
    return total


def peers(axis, members):
    me = lax.axis_index(axis)
    return [lax.rem(me + k, members) for k in range(1, members)]


def greet_peers(groups):
    signal_peers(groups)
    wait_peers(groups)


def share(axis, members, source, slots, send_sem, recv_sem):
    me = lax.axis_index(axis)
    copies = []
    for k, peer in enumerate(peers(axis, members)):
        copy = pltpu.make_async_remote_copy(
            src_ref=source(peer),
            dst_ref=slots.at[me],
            send_sem=send_sem.at[k],
            recv_sem=recv_sem.at[me],
            device_id={axis: peer},
            device_id_type=pl.DeviceIdType.MESH,
        )
        copy.start()
        copies.append(copy)
    return copies


def await_shares(axis, members, source, slots, send_sem, recv_sem):
    for k, peer in enumerate(peers(axis, members)):
        pltpu.make_async_remote_copy(
            src_ref=source(peer),
            dst_ref=slots.at[peer],
            send_sem=send_sem.at[k],
            recv_sem=recv_sem.at[peer],
            device_id={axis: peer},
            device_id_type=pl.DeviceIdType.MESH,
        ).wait_recv()


def await_sends(axis, members, source, slots, send_sem, recv_sem):
    for k, peer in enumerate(peers(axis, members)):
        pltpu.make_async_remote_copy(
            src_ref=source(peer),
            dst_ref=slots.at[peer],
            send_sem=send_sem.at[k],
            recv_sem=recv_sem.at[peer],
            device_id={axis: peer},
            device_id_type=pl.DeviceIdType.MESH,
        ).wait_send()


def slot_total(slots):
    total = slots[0]
    for k in range(1, slots.shape[0]):
        total = total + slots[k]
    return total


def signal_peers(groups):
    barrier = pltpu.get_barrier_semaphore()
    for axis, members in groups:
        for peer in peers(axis, members):
            pl.semaphore_signal(
                barrier, inc=1, device_id={axis: peer}, device_id_type=pl.DeviceIdType.MESH
            )


def wait_peers(groups):
    pl.semaphore_wait(pltpu.get_barrier_semaphore(), sum(members - 1 for _, members in groups))


def sum_over_owners(members, local, total, slots, send_sem, recv_sem):
    copies = share("dp", members, lambda peer: local, slots, send_sem, recv_sem)
    slots[lax.axis_index("dp")] = local[...]
    await_shares("dp", members, lambda peer: local, slots, send_sem, recv_sem)
    total[...] = slot_total(slots)
    for copy in copies:
        copy.wait_send()


def sum_scratch(members, rows, channels):
    return [
        pltpu.VMEM((rows, channels), jnp.float32),
        pltpu.VMEM((members, rows, channels), jnp.float32),
        pltpu.SemaphoreType.DMA((members,)),
        pltpu.SemaphoreType.DMA((members,)),
    ]


def pixel_count(wide, members):
    images, padded, width, _ = wide.shape
    return float(images * (padded - 2 * DILATION_STEP) * width * members)


def norm_rows(sums_ref, gain_ref, layer, pixels):
    center = sums_ref[0:1] / pixels
    inverse = lax.rsqrt(sums_ref[1:2] / pixels - center * center + NORM_EPS)
    return center, inverse, gain_ref[2 * layer : 2 * layer + 1], gain_ref[2 * layer + 1 : 2 * layer + 2]


def add_sums(sums, first, second):
    sums[0:1] += jnp.sum(first, axis=0, keepdims=True)
    sums[1:2] += jnp.sum(second, axis=0, keepdims=True)


FAR = ("task", 2)
CORE = ("task", 1)


def owner_bits(members):
    bits = []
    bit = members // 2
    while bit:
        bits.append(("dp", bit))
        bit //= 2
    return bits


def partner(dim):
    axis, bit = dim
    me = lax.axis_index(axis)
    mine = lax.rem(me // bit, 2)
    return mine, {axis: me + bit * (1 - 2 * mine)}


class Gather:
    def __init__(self, plans, dims, split, ins, outs, local_sem, send_sem, recv_sem):
        self.dims, self.split, self.ins, self.outs = dims, split, ins, outs
        self.local_sem, self.send_sem, self.recv_sem = local_sem, send_sem, recv_sem
        self.entries = [
            (array, start, rows, order)
            for array, (plan, _) in enumerate(plans)
            for start, rows, order in plan
        ]
        self.group_of, groups = [], 0
        for array, (plan, width) in enumerate(plans):
            late = groups + (4 if array == 1 else 0)
            self.group_of += [late + i // width for i in range(len(plan))]
            groups = self.group_of[-1] + 1
        self.depth = max(len(entry[3]) for entry in self.entries)
        self.steps = groups + self.depth

    def held(self, array, start, rows, free):
        return (pl.ds(start, rows),) + tuple(
            slice(None) if dim in free else partner(dim)[0] for dim in self.dims[array]
        )

    def placements(self, index):
        array, start, rows, order = self.entries[index]
        target = self.held(array, start, rows, ())
        source = self.ins[array]
        task = lax.axis_index("task")
        if not self.split[array]:
            pairs = [(source.at[pl.ds(start, rows)], target)]
        else:
            halves_of = [None] if FAR in order else [0, 1]
            pairs = []
            for half in halves_of:
                column = task if half is None else lax.rem(task, 2) + 2 * half
                column = pl.multiple_of(column * 128, 128)
                place = target if half is None else (target[0], half) + target[2:]
                pairs.append((source.at[pl.ds(start, rows), :, pl.ds(column, 128)], place))
        return [
            pltpu.make_async_copy(source, self.outs[array].at[place], self.local_sem.at[index, i])
            for i, (source, place) in enumerate(pairs)
        ]

    def copy_of(self, index, stage):
        array, start, rows, order = self.entries[index]
        free = set(order[:stage]) | {d for d in self.dims[array] if d not in order}
        where = self.held(array, start, rows, free)
        return pltpu.make_async_remote_copy(
            src_ref=self.outs[array].at[where],
            dst_ref=self.outs[array].at[where],
            send_sem=self.send_sem.at[index, stage],
            recv_sem=self.recv_sem.at[index, stage],
            device_id=partner(order[stage])[1],
            device_id_type=pl.DeviceIdType.MESH,
        )

    def place(self):
        for index in range(len(self.entries)):
            for copy in self.placements(index):
                copy.start()

    def step(self, step):
        for stage in range(self.depth, -1, -1):
            for index, (array, start, rows, order) in enumerate(self.entries):
                if self.group_of[index] != step - stage or stage > len(order):
                    continue
                if stage == 0:
                    for copy in self.placements(index):
                        copy.wait()
                else:
                    self.copy_of(index, stage - 1).wait_recv()
                if stage < len(order):
                    self.copy_of(index, stage).start()

    def finish(self):
        for index, entry in enumerate(self.entries):
            for stage in range(len(entry[3])):
                self.copy_of(index, stage).wait_send()

    def run(self):
        self.place()
        for step in range(self.steps):
            self.step(step)
        self.finish()


def spread(orders, taps, width):
    rows = taps // len(orders)
    return [(i * rows, rows, order) for i, order in enumerate(orders)], width


def weight_plans(members, taps):
    bits = owner_bits(members)
    quarters = tuple(bits) + (FAR, CORE)
    halves_only = tuple(bits) + (CORE,)
    trunk_plan = spread([quarters, halves_only, quarters] * 3, taps, 3)
    head_plan = spread([tuple(bits)], 2, 1)
    digits = [FAR, CORE] + bits
    return [trunk_plan, trunk_plan, head_plan], [digits, digits, bits], [True, True, False]


def first_kernel(
    members, steps, tiles, layout, x_ref, trunk_ref, head_ref, note_ref, conv_ref, total, full_ref,
    heads_ref, wide, weights, local_sem, send_sem, recv_sem, *exchange,
):
    g = pl.program_id(0)
    sums = exchange[0]
    moving = Gather(
        *layout,
        [trunk_ref.at[0], trunk_ref.at[1], head_ref],
        [weights, full_ref, heads_ref],
        local_sem,
        send_sem,
        recv_sem,
    )

    @pl.when(g == 0)
    def _():
        greet_peers([("dp", members), ("task", TASKS)])
        moving.place()
        clear_edges(wide)
        sums[...] = note_ref[...]

    spread_over = steps + tiles - 1
    ready = 3 + moving.depth
    for step in range(moving.steps):
        if step < ready:
            at = step * steps // ready
        else:
            at = steps + min(step - ready, tiles - 1)

        @pl.when(g == at)
        def _():
            moving.step(step)

    @pl.when(g < steps)
    def _():
        per = steps // wide.shape[0]

        def one(i, carry):
            spread_columns(
                wide,
                g // per,
                lax.rem(g, per) * CHUNK + 3 * i,
                x_ref[0, pl.ds(3 * i, 3)].astype(jnp.float32),
            )
            return carry

        lax.fori_loop(0, CHUNK // 3, one, 0)
        sums[2:3] += jnp.sum(x_ref[0].astype(jnp.float32), axis=(0, 1))[None]

    @pl.when(g >= steps)
    def _():
        per = tiles // wide.shape[0]
        t = g - steps
        parts = [weights[:, i, j] for i in range(2) for j in range(2)]
        conv = conv_tile(wide, parts, t // per, lax.rem(t, per) * TILE, TILE)
        conv_ref[...] = conv
        add_sums(sums, conv, conv * conv)

    @pl.when(g == spread_over)
    def _():
        moving.finish()
        sum_over_owners(members, sums, total, *exchange[1:])


def second_kernel(
    members, steps, tiles, y_ref, t_ref, n_ref, w_ref, conv_ref, act_ref, total, wide, *exchange
):
    g = pl.program_id(0)
    sums = exchange[0]

    @pl.when(g == 0)
    def _():
        signal_peers([("dp", members)])
        clear_edges(wide)
        sums[...] = jnp.zeros_like(sums)

    @pl.when(g < steps)
    def _():
        per = steps // wide.shape[0]
        center, inverse, gain, shift = norm_rows(t_ref, n_ref, 0, pixel_count(wide, members))

        def one(i, carry):
            values = y_ref[0, pl.ds(3 * i, 3)]
            normed = gain * ((values - center) * inverse) + shift
            act = jax.nn.silu(normed).astype(jnp.bfloat16)
            act_ref[0, pl.ds(3 * i, 3)] = act
            act = act.astype(jnp.float32)
            spread_columns(wide, g // per, lax.rem(g, per) * CHUNK + 3 * i, act)
            sums[2:3] += jnp.sum(act, axis=(0, 1))[None]
            return carry

        lax.fori_loop(0, CHUNK // 3, one, 0)

    @pl.when(g >= steps)
    def _():
        per = tiles // wide.shape[0]
        t = g - steps
        parts = [w_ref[:, part] for part in range(w_ref.shape[1])]
        conv = conv_tile(wide, parts, t // per, lax.rem(t, per) * TILE, TILE)
        conv_ref[...] = conv
        add_sums(sums, conv, conv * conv)

    @pl.when(g == steps + tiles - 1)
    def _():
        wait_peers([("dp", members)])
        sum_over_owners(members, sums, total, *exchange[1:])


def map_specs(images, height, width, channels):
    per = height // CHUNK
    steps = images * per
    stream = pl.BlockSpec(
        (1, CHUNK, width, channels),
        lambda g: (jnp.minimum(g, steps - 1) // per, lax.rem(jnp.minimum(g, steps - 1), per), 0, 0),
    )
    rows = pl.BlockSpec((TILE * width, channels), lambda g: (jnp.maximum(g - steps, 0), 0))
    return steps, images * (height // TILE), stream, rows


def fixed(*shape):
    return pl.BlockSpec(shape, lambda g: (0,) * len(shape))


def first_conv_call(x, trunk, head, note, identity):
    images, height, width, channels = x.shape
    steps, tiles, stream, rows = map_specs(*x.shape)
    pixels = images * height * width
    members = lax.axis_size("dp")
    layers, taps, shard_rows, _ = trunk.shape
    layout = weight_plans(members, taps)
    plans, dims, _ = layout
    entries = sum(len(plan) for plan, _ in plans)
    depth = max(len(digits) for digits in dims)
    matrix = (taps,) + (2,) * len(dims[0]) + (shard_rows, 128)
    branch = head.shape[3]
    anywhere = pl.BlockSpec(memory_space=pl.ANY)
    conv, total, full, heads = pl.pallas_call(
        functools.partial(first_kernel, members, steps, tiles, layout),
        grid=(steps + tiles,),
        in_specs=[stream, anywhere, anywhere, fixed(*note.shape)],
        out_specs=(rows, fixed(*note.shape), anywhere, anywhere),
        out_shape=(
            jax.ShapeDtypeStruct((pixels, channels), jnp.float32),
            jax.ShapeDtypeStruct(note.shape, jnp.float32),
            jax.ShapeDtypeStruct(matrix, trunk.dtype),
            jax.ShapeDtypeStruct((2,) + (2,) * len(dims[2]) + (shard_rows, branch), head.dtype),
        ),
        scratch_shapes=[
            pltpu.VMEM((images, height + 2 * DILATION_STEP, width, 3 * channels), jnp.bfloat16),
            pltpu.VMEM(matrix, trunk.dtype),
            pltpu.SemaphoreType.DMA((entries, 2)),
            pltpu.SemaphoreType.DMA((entries, depth)),
            pltpu.SemaphoreType.DMA((entries, depth)),
        ]
        + sum_scratch(members, note.shape[0], channels),
        compiler_params=summing(identity),
        name="first_conv",
    )(x, trunk, head[0], note)
    full = full.reshape(taps, TASKS, channels, 128)
    return conv, total, full, heads.reshape(2, channels, branch)


def second_conv_call(y, totals, gains, weights, shape, identity):
    images, height, width, channels = shape
    steps, tiles, stream, rows = map_specs(*shape)
    pixels = images * height * width
    members = lax.axis_size("dp")
    return pl.pallas_call(
        functools.partial(second_kernel, members, steps, tiles),
        grid=(steps + tiles,),
        in_specs=[stream, fixed(8, channels), fixed(4, channels), fixed(*weights.shape)],
        out_specs=(rows, stream, fixed(8, channels)),
        out_shape=(
            jax.ShapeDtypeStruct((pixels, channels), jnp.float32),
            jax.ShapeDtypeStruct(shape, jnp.bfloat16),
            jax.ShapeDtypeStruct((8, channels), jnp.float32),
        ),
        scratch_shapes=[
            pltpu.VMEM((images, height + 2 * DILATION_STEP, width, 3 * channels), jnp.bfloat16)
        ]
        + sum_scratch(members, 8, channels),
        compiler_params=summing(identity),
        name="second_conv",
    )(y.reshape(shape), totals, gains, weights)


def deltas(
    g, steps, members, layer, x_ref, up_ref, y_ref, t_ref, n_ref, b_ref, edge_ref, back_ref, wide, back
):
    images, padded, width, channels = wide.shape
    channels = channels // 3
    height = padded - 2 * DILATION_STEP

    @pl.when(g == 0)
    def _():
        clear_edges(wide)
        edge_ref[...] = jnp.zeros_like(edge_ref)

    @pl.when(g < steps)
    def _():
        per = steps // images
        column = lax.broadcasted_iota(jnp.int32, (1, 8, channels), 1)
        pixels = pixel_count(wide, members)
        center, inverse, gain, _ = norm_rows(t_ref, n_ref, layer, pixels)
        lean, slant = b_ref[0:1] / pixels, b_ref[1:2] / pixels

        def one(i, carry):
            place = pl.ds(3 * i, 3)
            row = lax.rem(g, per) * CHUNK + 3 * i
            spread_columns(wide, g // per, row, x_ref[0, place].astype(jnp.float32))
            centered = (y_ref[0, place] - center) * inverse
            values = gain * inverse * (up_ref[0, place] - lean - centered * slant)
            values = values.astype(jnp.bfloat16)
            if back_ref is not None:
                back_ref[0, place] = values
            back[g // per, pl.ds(row, 3)] = values
            values = values.astype(jnp.float32)
            whole = jnp.sum(values, axis=1)
            first = jnp.sum(jnp.where(column < DILATION_STEP, values[:, :8], 0.0), axis=1)
            last = jnp.sum(
                jnp.where(column >= 8 - DILATION_STEP, values[:, width - 8 :], 0.0), axis=1
            )
            for kernel_column, line in enumerate((whole - first, whole, whole - last)):
                for kernel_row in range(3):
                    at = row + DILATION_STEP * (kernel_row - 1)
                    part = [
                        jnp.where((at + r >= 0) & (at + r < height), line[r : r + 1], 0.0)
                        for r in range(3)
                    ]
                    tap = 3 * kernel_row + kernel_column
                    edge_ref[tap + 2 : tap + 3] += part[0] + part[1] + part[2]
            return carry

        lax.fori_loop(0, CHUNK // 3, one, 0)


def tap_gradient(wide, back, members, tap_row, column, t_ref, line):
    images, height, width, channels = back.shape
    total = None
    for image in range(images):
        part = dot(
            window(wide, image, 0, height, tap_row, column),
            back[image].reshape(height * width, channels),
            CONTRACT_ROWS,
        )
        total = part if total is None else total + part
    mean = jnp.swapaxes(t_ref[...], 0, 1)[:, 2:3] / pixel_count(wide, members)
    return total - mean * line


def weight_kernel(
    steps, members, cut, x_ref, up_ref, y_ref, t_ref, n_ref, b_ref, extra_ref, keep_ref, send_ref,
    keep_rest, send_rest, edge_ref, back_ref, wide, back, whole,
):
    g = pl.program_id(0)
    mine = lax.rem(lax.axis_index("dp"), 2)
    deltas(
        g, steps, members, 1, x_ref, up_ref, y_ref, t_ref, n_ref, b_ref, edge_ref, back_ref, wide, back
    )
    for column in range(3):

        @pl.when((g >= steps) & (lax.rem(g - steps, 3) == column))
        def _():
            line = edge_ref[pl.ds(g - steps + 2, 1)]
            grad = tap_gradient(wide, back, members, (g - steps) // 3, column, t_ref, line)
            whole[...] = grad.reshape(whole.shape)

    @pl.when((g >= steps) & (g < steps + cut))
    def _():
        keep_ref[0] = whole[:, mine].astype(keep_ref.dtype)
        send_ref[0] = whole[:, 1 - mine].astype(send_ref.dtype)

    @pl.when(g == steps + cut)
    def _():
        keep_ref[0] = extra_ref[:, mine]
        send_ref[0] = extra_ref[:, 1 - mine]

    @pl.when(g >= steps + cut)
    def _():
        keep_rest[0] = whole[:, mine].astype(keep_rest.dtype)
        send_rest[0] = whole[:, 1 - mine].astype(send_rest.dtype)


def weight_grad_call(x, upstream, y, totals, gains, backs, extra, cut):
    images, height, width, channels = x.shape
    steps, tiles, stream, rows = map_specs(*x.shape)
    members = lax.axis_size("dp")
    shape = (members // 2, channels // members, channels)

    def part(first, count):
        return pl.BlockSpec(
            (1,) + shape, lambda g: (jnp.clip(g - steps - first, 0, count - 1), 0, 0, 0)
        )

    ahead, rest = part(0, cut + 1), part(cut, 9 - cut)
    ahead_shape = jax.ShapeDtypeStruct((cut + 1,) + shape, jnp.bfloat16)
    rest_shape = jax.ShapeDtypeStruct((9 - cut,) + shape, jnp.bfloat16)
    extra = extra.reshape(shape[:1] + (2,) + shape[1:])
    return pl.pallas_call(
        functools.partial(weight_kernel, steps, members, cut),
        grid=(steps + 9,),
        in_specs=[
            stream,
            stream,
            stream,
            fixed(8, channels),
            fixed(4, channels),
            fixed(16, channels),
            fixed(*extra.shape),
        ],
        out_specs=(ahead, ahead, rest, rest, fixed(16, channels), stream),
        out_shape=(
            ahead_shape,
            ahead_shape,
            rest_shape,
            rest_shape,
            jax.ShapeDtypeStruct((16, channels), jnp.float32),
            jax.ShapeDtypeStruct(x.shape, jnp.bfloat16),
        ),
        scratch_shapes=[
            pltpu.VMEM((images, height + 2 * DILATION_STEP, width, 3 * channels), jnp.bfloat16),
            pltpu.VMEM((images, height, width, channels), jnp.bfloat16),
            pltpu.VMEM(shape[:1] + (2,) + shape[1:], jnp.float32),
        ],
        compiler_params=PARAMS,
        name="weight_grad",
    )(x, upstream.reshape(x.shape), y.reshape(x.shape), totals, gains, backs, extra)


def act_grad_kernel(
    members, steps, tiles, back_ref, y_ref, t_ref, n_ref, w_ref, note_ref, up_ref, total, wide, *exchange
):
    g = pl.program_id(0)
    sums = exchange[0]

    @pl.when(g == 0)
    def _():
        signal_peers([("dp", members)])
        clear_edges(wide)
        sums[...] = note_ref[...]

    @pl.when(g < steps)
    def _():
        per = steps // wide.shape[0]

        def one(i, carry):
            spread_columns(
                wide,
                g // per,
                lax.rem(g, per) * CHUNK + 3 * i,
                back_ref[0, pl.ds(3 * i, 3)].astype(jnp.float32),
            )
            return carry

        lax.fori_loop(0, CHUNK // 3, one, 0)

    @pl.when(g >= steps)
    def _():
        per = tiles // wide.shape[0]
        t = g - steps
        grad = conv_tile_back(wide, w_ref, t // per, lax.rem(t, per) * TILE, TILE)
        center, inverse, gain, shift = norm_rows(t_ref, n_ref, 0, pixel_count(wide, members))
        centered = (y_ref[...] - center) * inverse
        upstream = grad * silu_slope(gain * centered + shift)
        up_ref[...] = upstream
        add_sums(sums, upstream, upstream * centered)

    @pl.when(g == steps + tiles - 1)
    def _():
        wait_peers([("dp", members)])
        sum_over_owners(members, sums, total, *exchange[1:])


def act_grad_call(back, y, totals, gains, weights, note, identity):
    images, height, width, channels = back.shape
    steps, tiles, stream, rows = map_specs(*back.shape)
    pixels = images * height * width
    members = lax.axis_size("dp")
    return pl.pallas_call(
        functools.partial(act_grad_kernel, members, steps, tiles),
        grid=(steps + tiles,),
        in_specs=[
            stream,
            rows,
            fixed(8, channels),
            fixed(4, channels),
            fixed(*weights.shape),
            fixed(*note.shape),
        ],
        out_specs=(rows, fixed(16, channels)),
        out_shape=(
            jax.ShapeDtypeStruct((pixels, channels), jnp.float32),
            jax.ShapeDtypeStruct((16, channels), jnp.float32),
        ),
        scratch_shapes=[
            pltpu.VMEM((images, height + 2 * DILATION_STEP, width, 3 * channels), jnp.bfloat16)
        ]
        + sum_scratch(members, 16, channels),
        compiler_params=summing(identity),
        name="act_grad",
    )(back, y, totals, gains, weights, note)


def update_kernel(
    place_ref, g_ref, rows_ref, cols_ref, left_ref, right_ref, master_ref, lroot_ref, rroot_ref,
    grad_out, left_out, right_out, master_out, copy_out, gram,
):
    parts = g_ref.shape[1]
    shard_rows = left_ref.shape[1]
    for item in range(g_ref.shape[0]):
        full = jnp.concatenate([g_ref[item, part] for part in range(parts)], axis=1)
        rows = jnp.concatenate([rows_ref[item, part] for part in range(parts)], axis=1)
        grad_out[item] = rows.astype(jnp.float32)
        left_out[item] = 0.5 * left_ref[item] + 0.5 * dot(rows, full, CONTRACT_COLS)
        gram[item] = dot(cols_ref[item, 0], full, CONTRACT_ROWS)
        right_out[item] = 0.5 * right_ref[item] + 0.5 * gram[
            item, pl.ds(pl.multiple_of(place_ref[2], 8), shard_rows)
        ]
        turned = dot(lroot_ref[item].astype(jnp.bfloat16), full).astype(jnp.bfloat16)
        step = dot(turned, rroot_ref[item].astype(jnp.bfloat16))
        master = master_ref[item]
        master = master - RATE_TRUNK * (step + WEIGHT_DECAY * master)
        master_out[item] = master
        copy_out[item] = master.astype(jnp.bfloat16)


def update_call(owner, combined, left, right, master, lroot, rroot):
    layers, taps, shard_rows, channels = left.shape
    count, parts, _, width = combined.shape
    one = pl.BlockSpec((3, shard_rows, channels), lambda g, place: (g, 0, 0))
    whole = pl.BlockSpec((3, channels, channels), lambda g, place: (g, 0, 0))
    flat = (count, shard_rows, channels)
    start = owner * shard_rows
    place = jnp.stack([owner, start // width, lax.rem(start, width)]).astype(jnp.int32)
    outs = pl.pallas_call(
        update_kernel,
        grid_spec=pltpu.PrefetchScalarGridSpec(
            num_scalar_prefetch=1,
            grid=(count // 3,),
            in_specs=[
                pl.BlockSpec((3, parts, channels, width), lambda g, place: (g, 0, 0, 0)),
                pl.BlockSpec((3, parts, shard_rows, width), lambda g, place: (g, 0, place[0], 0)),
                pl.BlockSpec((3, 1, channels, width), lambda g, place: (g, place[1], 0, 0)),
                one,
                one,
                one,
                one,
                whole,
            ],
            out_specs=(one,) * 5,
            scratch_shapes=[pltpu.VMEM((3, width, channels), jnp.float32)],
        ),
        out_shape=tuple(
            jax.ShapeDtypeStruct(flat, kind)
            for kind in (jnp.float32, jnp.float32, jnp.float32, jnp.float32, jnp.bfloat16)
        ),
        compiler_params=PARAMS,
        name="update",
    )(
        place,
        combined,
        combined,
        combined,
        left.reshape(flat),
        right.reshape(flat),
        master.reshape(flat),
        lroot.reshape(flat),
        rroot.reshape(count, channels, channels),
    )
    return [out.reshape(left.shape) for out in outs]


def combined_plan(members, taps):
    bits = owner_bits(members)
    last = bits[-1:]
    plain = tuple(bits) + (FAR, CORE)
    other = tuple(bits[:-1]) + (FAR,) + tuple(last) + (CORE,)
    early = tuple(last) + (FAR,) + tuple(bits[:-1]) + (CORE,)
    first = (FAR,) + tuple(last) + tuple(bits[:-1]) + (CORE,)
    return [spread([plain, other, plain, other, early, first] * 3, taps, 6)], [[FAR, CORE] + bits]


MIX_SEMS = 14
PAIRS = [(i, j) for i in range(TASKS) for j in range(i, TASKS)]


def send_layer(grads, first, edges, mean, scale, outbox, inbox, send_sem, recv_sem):
    taps = outbox.shape[1]

    def one(tap, carry):
        grad = (grads[first + tap] + mean * edges[pl.ds(tap + 2, 1)]) * scale
        grad = grad.astype(jnp.bfloat16)
        for part in range(TASKS):
            outbox[part, tap] = grad[:, part * 128 : (part + 1) * 128]
        return carry

    lax.fori_loop(0, taps, one, 0)
    return share("task", TASKS, lambda peer: outbox.at[peer], inbox, send_sem, recv_sem)


def mix_layers(
    members, plans, dims, boxes, conflict_ref, full_ref, pair_ref, products, dp_slots, partial,
    task_slots, mixed, own_sem, dp_send, dp_recv, task_send, task_recv, local_sem, send_sem, recv_sem,
):
    task = lax.axis_index("task")
    owner = lax.axis_index("dp")
    for layer, (outbox, inbox, block_send, block_recv) in enumerate(boxes):
        local = pltpu.make_async_copy(outbox.at[task], inbox.at[task], own_sem.at[layer])
        local.start()
        local.wait()
        await_shares(
            "task", TASKS, lambda peer: outbox.at[peer], inbox, block_send, block_recv
        )
    width = mixed.shape[2]
    taps = mixed.shape[0] // 2
    sums = tuple(jnp.zeros((8, width), jnp.float32) for _ in PAIRS)
    for _, inbox, _, _ in boxes:

        def multiply(tap, sums):
            values = [inbox[t, tap].astype(jnp.float32) for t in range(TASKS)]
            return tuple(
                total + jnp.sum((values[i] * values[j]).reshape(-1, 8, width), axis=0)
                for total, (i, j) in zip(sums, PAIRS)
            )

        sums = lax.fori_loop(0, taps, multiply, sums)
    for row, total in enumerate(sums):
        products[row : row + 1] = jnp.sum(total, axis=0, keepdims=True)
    products[len(PAIRS) : 16] = jnp.zeros((16 - len(PAIRS), width), jnp.float32)
    copies = share("dp", members, lambda peer: products, dp_slots, dp_send, dp_recv)
    dp_slots[owner] = products[...]
    await_shares("dp", members, lambda peer: products, dp_slots, dp_send, dp_recv)
    partial[...] = slot_total(dp_slots)
    copies += share("task", TASKS, lambda peer: partial, task_slots, task_send, task_recv)
    task_slots[task] = partial[...]
    await_shares("task", TASKS, lambda peer: partial, task_slots, task_send, task_recv)
    total = jnp.broadcast_to(
        jnp.sum(slot_total(task_slots), axis=1, keepdims=True), products.shape
    )
    rows = {pair: total[row : row + 1] for row, pair in enumerate(PAIRS)}
    weights = []
    for j in range(TASKS):
        weight = jnp.ones((1, width), jnp.float32)
        for i in range(TASKS):
            pair = rows[min(i, j), max(i, j)]
            at = TASKS * i + j
            pair_ref[at : at + 1] = pair
            if i != j:
                weight = weight - conflict_ref[at : at + 1] * pair / (rows[j, j] + GRAM_EPS)
        weights.append(weight)
    for layer, (_, inbox, _, _) in enumerate(boxes):

        def blend(tap, carry):
            value = weights[0] * inbox[0, tap].astype(jnp.float32)
            for t in range(1, TASKS):
                value = value + weights[t] * inbox[t, tap].astype(jnp.float32)
            mixed[layer * taps + tap] = value.astype(jnp.bfloat16)
            return carry

        lax.fori_loop(0, taps, blend, 0)
    Gather(plans, dims, [False], [mixed], [full_ref], local_sem, send_sem, recv_sem).run()
    for copy in copies:
        copy.wait_send()


def reduce_kernel(
    members, stages, cut, steps, layout, x_ref, up_ref, y_ref, t_ref, n_ref, b_ref, later_ref,
    head_ref, conflict_ref, keep_ahead, got_ahead, keep_rest, send_rest, full_ref,
    pair_ref, notes_out, head_out, *refs
):
    sum_ref, edge_out, wide, back, edge_ref, part_ref = refs[:6]
    outboxes, inboxes, mixing = refs[6:8], refs[8:10], refs[10:-MIX_SEMS - 5]
    mixing, notes_in, notes_ref, turned, buffers = mixing[:5], mixing[5], mixing[6], mixing[7], mixing[8:]
    mix_sems = refs[-MIX_SEMS - 5 : -5]
    slots, send_sem, recv_sem, slot_send, slot_recv = refs[-5:]
    block_sems, note_sems, mix_sems = mix_sems[:4], mix_sems[4:6], mix_sems[6:]
    g = pl.program_id(0)
    got = buffers[:stages]
    sent = (None,) + tuple(buffers[stages : 2 * stages - 1])
    kept = (None,) + tuple(buffers[2 * stages - 1 :])
    taps = part_ref.shape[0]
    dims = [("dp", 1 << stage) for stage in range(stages)]
    own, ahead, rest = "own", "ahead", "rest"
    starts = [(own, tap) for tap in range(taps)]
    starts += [(ahead, tap) for tap in range(cut)]
    starts += [(rest, tap) for tap in range(taps - cut)]
    starts += [(ahead, cut)]
    whole = [entry for entry, (kind, _) in enumerate(starts) if kind != ahead]

    def landed(stage, entry):
        return got[stage].at[entry if stage else whole.index(entry)]

    def copy_of(stage, entry):
        kind, tap = starts[entry]
        mine, device = partner(dims[stage])
        if stage:
            source = sent[stage].at[entry]
        elif kind == own:
            source = part_ref.at[tap, :, 1 - mine]
        else:
            source = send_rest.at[tap]
        return pltpu.make_async_remote_copy(
            src_ref=source,
            dst_ref=landed(stage, entry),
            send_sem=send_sem.at[stage, entry],
            recv_sem=recv_sem.at[stage, entry],
            device_id=device,
            device_id_type=pl.DeviceIdType.MESH,
        )

    def total_of(stage, entry, at):
        kind, tap = starts[entry]
        if stage:
            value = kept[stage][entry, at]
        elif kind == own:
            value = part_ref[tap, at, partner(dims[0])[0]]
        elif kind == rest:
            value = keep_rest[tap, at]
        else:
            value = keep_ahead[tap, at]
        if stage == 0 and kind == ahead:
            other = got_ahead[tap, at]
        else:
            other = landed(stage, entry)[at]
        return value.astype(jnp.float32) + other.astype(jnp.float32)

    finished = set()

    def advance(stage, entry):
        if stage or entry in whole:
            copy_of(stage, entry).wait_recv()
        if stage == stages - 1:
            sum_ref[entry] = total_of(stage, entry, 0)
            finished.add(entry)
            return
        following = partner(dims[stage + 1])[0]
        for block in range((members >> (stage + 1)) // 2):
            for half in range(2):
                at = 2 * block + (following if half else 1 - following)
                value = total_of(stage, entry, at)
                if half:
                    kept[stage + 1][entry, block] = value
                else:
                    sent[stage + 1][entry, block] = value.astype(jnp.bfloat16)
        copy_of(stage + 1, entry).start()

    @pl.when(g == 0)
    def _():
        greet_peers([("dp", members), ("task", TASKS)])
        for entry, (kind, _) in enumerate(starts):
            if kind == rest:
                copy_of(0, entry).start()
        for entry, (kind, _) in enumerate(starts):
            if kind == ahead:
                advance(0, entry)

    deltas(g, steps, members, 0, x_ref, up_ref, y_ref, t_ref, n_ref, b_ref, edge_ref, None, wide, back)

    @pl.when(g == steps)
    def _():
        share("dp", members, lambda peer: edge_ref, slots, slot_send, slot_recv)
        slots[lax.axis_index("dp")] = edge_ref[...]

    waiting = [[] for _ in range(stages)]
    waiting[0] += [entry for entry, (kind, _) in enumerate(starts) if kind == rest]
    waiting[1] += [entry for entry, (kind, _) in enumerate(starts) if kind == ahead]

    def turn():
        moved = []
        for stage in range(stages - 1, -1, -1):
            if waiting[stage]:
                entry = waiting[stage].pop(0)
                advance(stage, entry)
                if stage + 1 < stages:
                    moved.append((stage + 1, entry))
        for stage, entry in moved:
            waiting[stage].append(entry)

    for tap in range(taps):

        @pl.when(g == steps + tap)
        def _():
            grad = tap_gradient(
                wide, back, members, tap // 3, tap % 3, t_ref, edge_ref[tap + 2 : tap + 3]
            )
            part_ref[tap] = grad.reshape(part_ref.shape[1:]).astype(part_ref.dtype)
            copy_of(0, tap).start()
            if tap >= 4:
                turn()

    @pl.when(g == steps + taps - 1)
    def _():
        task = lax.axis_index("task")
        for row, (source, at) in enumerate(((b_ref, 1), (b_ref, 0), (head_ref, 1), (head_ref, 0))):
            notes_ref[row : row + 1] = source[at : at + 1]
        notes_ref[4:14] = head_ref[2:12]
        notes_ref[14:16] = jnp.zeros_like(notes_ref[14:16])
        copies = share("task", TASKS, lambda peer: notes_ref, notes_in, *note_sems)
        pixels = pixel_count(wide, members)
        shard_rows = sum_ref.shape[1]
        place = pl.ds(pl.multiple_of(lax.axis_index("dp") * shard_rows, 8), shard_rows)
        means = []
        for layer, totals_ref in enumerate((t_ref, later_ref)):
            turned[layer] = jnp.swapaxes(totals_ref[...], 0, 1)
            means.append(turned[layer, place][:, 2:3] / pixels)
        scale = 1.0 / jnp.where(task == 1, t_ref[3:4], jnp.full_like(t_ref[3:4], pixels))
        notes_in[task] = notes_ref[...]
        waiting[0].extend(range(taps))
        second_sent = False
        while any(waiting):
            turn()
            if not second_sent and finished.issuperset(range(taps, 2 * taps)):
                second_sent = True
                copies += send_layer(
                    sum_ref, taps, b_ref, means[1], scale, outboxes[1], inboxes[1],
                    *block_sems[2:],
                )
        await_shares("dp", members, lambda peer: edge_ref, slots, slot_send, slot_recv)
        edge_out[...] = slot_total(slots)
        copies += send_layer(
            sum_ref, 0, edge_out, means[0], scale, outboxes[0], inboxes[0], *block_sems[:2]
        )
        head_out[...] = sum_ref[2 * taps]
        plans, dims = layout
        boxes = [
            (outboxes[0], inboxes[0]) + tuple(block_sems[:2]),
            (outboxes[1], inboxes[1]) + tuple(block_sems[2:]),
        ]
        mix_layers(
            members, plans, dims, boxes, conflict_ref, full_ref, pair_ref, *mixing, *mix_sems
        )
        await_shares("task", TASKS, lambda peer: notes_ref, notes_in, *note_sems)
        notes_out[...] = notes_in[...]
        for entry in range(len(starts)):
            for stage in range(0 if entry in whole else 1, stages):
                copy_of(stage, entry).wait_send()
        await_sends("dp", members, lambda peer: edge_ref, slots, slot_send, slot_recv)
        for copy in copies:
            copy.wait_send()


def reduce_call(
    x, upstream, y, totals, gains, backs, later, heads, conflict, ahead, rest, identity
):
    images, height, columns, channels = x.shape
    steps, _, stream, _ = map_specs(*x.shape)
    members = lax.axis_size("dp")
    stages = members.bit_length() - 1
    taps, width = 9, channels
    shard_rows = channels // members
    cut = ahead[0].shape[0] - 1
    entries, whole = 2 * taps + 1, 2 * taps - cut
    layout = combined_plan(members, 2 * taps)
    plans, dims = layout
    moves, quarter = len(plans[0][0]), channels // TASKS
    vmem = pl.BlockSpec(memory_space=pltpu.VMEM)
    dma = pltpu.SemaphoreType.DMA

    def blocks(stage, kind):
        held = entries if stage else whole
        return pltpu.VMEM((held, members >> (stage + 1), shard_rows, width), kind)

    box = pltpu.VMEM((TASKS, taps, shard_rows, quarter), jnp.bfloat16)
    full, pairs, notes, head = pl.pallas_call(
        functools.partial(reduce_kernel, members, stages, cut, steps, layout),
        grid=(steps + taps,),
        out_shape=(
            jax.ShapeDtypeStruct(
                (2 * taps,) + (2,) * len(dims[0]) + (shard_rows, quarter), jnp.bfloat16
            ),
            jax.ShapeDtypeStruct((16, quarter), jnp.float32),
            jax.ShapeDtypeStruct((TASKS, 16, channels), jnp.float32),
            jax.ShapeDtypeStruct((shard_rows, width), jnp.float32),
        ),
        in_specs=[stream, stream, stream, fixed(8, channels), fixed(4, channels), fixed(16, channels)]
        + [vmem] * 7,
        out_specs=(pl.BlockSpec(memory_space=pl.ANY), vmem, vmem, vmem),
        scratch_shapes=[
            pltpu.VMEM((entries, shard_rows, width), jnp.float32),
            pltpu.VMEM((16, channels), jnp.float32),
            pltpu.VMEM((images, height + 2 * DILATION_STEP, columns, 3 * channels), jnp.bfloat16),
            pltpu.VMEM((images, height, columns, channels), jnp.bfloat16),
            pltpu.VMEM((16, channels), jnp.float32),
            pltpu.VMEM((taps, members // 2, 2, shard_rows, width), jnp.bfloat16),
            box,
            box,
            box,
            box,
            pltpu.VMEM((16, quarter), jnp.float32),
            pltpu.VMEM((members, 16, quarter), jnp.float32),
            pltpu.VMEM((16, quarter), jnp.float32),
            pltpu.VMEM((TASKS, 16, quarter), jnp.float32),
            pltpu.VMEM((2 * taps, shard_rows, quarter), jnp.bfloat16),
            pltpu.VMEM((TASKS, 16, channels), jnp.float32),
            pltpu.VMEM((16, channels), jnp.float32),
            pltpu.VMEM((2, channels, 8), jnp.float32),
        ]
        + [blocks(stage, jnp.bfloat16) for stage in range(stages)]
        + [blocks(stage, jnp.bfloat16) for stage in range(1, stages)]
        + [blocks(stage, jnp.float32) for stage in range(1, stages)]
        + [dma((TASKS,))] * 6
        + [
            dma((2,)),
            dma((members,)),
            dma((members,)),
            dma((TASKS,)),
            dma((TASKS,)),
            dma((moves, 2)),
            dma((moves, len(dims[0]))),
            dma((moves, len(dims[0]))),
        ]
        + [
            pltpu.VMEM((members, 16, channels), jnp.float32),
            dma((stages, entries)),
            dma((stages, entries)),
            dma((members,)),
            dma((members,)),
        ],
        compiler_params=summing(identity),
        name="reduce",
    )(
        x,
        upstream.reshape(x.shape),
        y.reshape(x.shape),
        totals,
        gains,
        backs,
        later,
        heads,
        conflict,
        *ahead,
        *rest,
    )
    return full.reshape(2 * taps, TASKS, channels, quarter), pairs, notes, head


def boundary(labels):
    across = jnp.pad(
        (labels[:, :, 1:] != labels[:, :, :-1]).astype(jnp.float32), ((0, 0), (0, 0), (0, 1))
    )
    downward = jnp.pad(
        (labels[:, 1:, :] != labels[:, :-1, :]).astype(jnp.float32), ((0, 0), (0, 1), (0, 0))
    )
    return jnp.maximum(across, downward)


def pixel_rows(labels, depth_mask, depth_target, normal_target):
    images, height, width = labels.shape
    rows = jnp.stack(
        [
            labels.astype(jnp.float32),
            depth_mask.astype(jnp.float32),
            boundary(labels),
            depth_target,
        ],
        axis=1,
    )
    rows = jnp.concatenate([rows, normal_target, jnp.zeros_like(rows[:, :1])], axis=1)
    rows = rows.reshape(images, 8, height // CHUNK, CHUNK * width)
    return jnp.swapaxes(rows, 1, 2)


def head_kernel(
    members, chunks, images, y_ref, x_ref, t_ref, n_ref, head_ref, out_ref, bias_ref, info_ref, weight_ref,
    up_ref, grad_ref, total, trunk, hidden_pre, pre_grads, pooled, base, per_image, matrix, *exchange,
):
    image, step = pl.program_id(0), pl.program_id(1)
    last = images - 1
    sums = exchange[0]
    rows = CHUNK * y_ref.shape[2]
    channels = y_ref.shape[3]
    area = float(chunks * rows)
    pixels = area * images * members
    phase = step // chunks
    place = pl.ds(lax.rem(step, chunks) * rows, rows)

    @pl.when((image == 0) & (step == 0))
    def _():
        signal_peers([("dp", members)])
        sums[...] = jnp.zeros_like(sums)
        matrix[...] = jnp.zeros_like(matrix)

    @pl.when(step == 0)
    def _():
        pooled[...] = jnp.zeros_like(pooled)
        per_image[...] = jnp.zeros_like(per_image)

    def residual():
        center, inverse, gain, shift = norm_rows(t_ref, n_ref, 1, pixels)
        centered = (y_ref[0].reshape(rows, channels) - center) * inverse
        inputs = x_ref[0].reshape(rows, channels).astype(jnp.float32)
        return centered, gain * centered + shift + inputs

    @pl.when(phase == 0)
    def _():
        _, before = residual()
        act = jax.nn.silu(before).astype(jnp.bfloat16)
        trunk[place] = act
        pooled[0:1] += jnp.sum(act.astype(jnp.float32), axis=0, keepdims=True)

    @pl.when(step == chunks)
    def _():
        mean = jnp.broadcast_to((pooled[0:1] / area).astype(jnp.bfloat16), (16, channels))
        base[...] = dot(mean, head_ref[1])[0:8] + bias_ref[...]

    @pl.when(phase == 1)
    def _():
        act = trunk[place]
        before = dot(act, head_ref[0]) + base[0:1]
        sigmoid = jax.nn.sigmoid(before)
        hidden = (before * sigmoid).astype(jnp.bfloat16)
        logits = dot(out_ref[...], hidden, CONTRACT_COLS)
        info = info_ref[0, 0]
        weight = [weight_ref[0, t : t + 1, 0:1] for t in range(TASKS)]
        classes = logits[:CLASSES]
        largest = jnp.max(classes, axis=0, keepdims=True)
        powers = jnp.exp(classes - largest)
        power = jnp.sum(powers, axis=0, keepdims=True)
        index = lax.broadcasted_iota(jnp.int32, classes.shape, 0).astype(jnp.float32)
        chosen = index == info[0:1]
        picked = jnp.sum(jnp.where(chosen, classes, 0.0), axis=0, keepdims=True)
        segment = jnp.log(power) + largest - picked
        class_grad = weight[0] * (powers / power - jnp.where(chosen, 1.0, 0.0))
        offset = logits[CLASSES : CLASSES + 1] - info[3:4]
        length = jnp.sqrt(offset * offset + 1.0)
        depth_grad = weight[1] * info[1:2] * (offset / length)
        predicted = logits[CLASSES + 1 : CLASSES + 4]
        normal = info[4:7]
        product = jnp.sum(predicted * normal, axis=0, keepdims=True)
        square = jnp.sum(predicted * predicted, axis=0, keepdims=True) + 1.0
        scale = lax.rsqrt(square * (jnp.sum(normal * normal, axis=0, keepdims=True) + 1.0))
        cosine = product * scale
        normal_grad = -weight[2] * (normal * scale - cosine * predicted / square)
        edge = logits[CLASSES + 4 : CLASSES + 5]
        softplus = jnp.maximum(edge, 0.0) + jnp.log1p(jnp.exp(-jnp.abs(edge)))
        edge_grad = weight[3] * (jax.nn.sigmoid(edge) - info[2:3])
        losses = (
            weight[0] * segment,
            weight[1] * info[1:2] * (length - 1.0),
            weight[2] * (1.0 - cosine),
            weight[3] * (softplus - info[2:3] * edge),
        )
        lane = lax.broadcasted_iota(jnp.int32, (1, channels), 1)
        for t, loss in enumerate(losses):
            value = jnp.sum(loss, axis=1, keepdims=True)
            sums[2:3] += jnp.where(lane == BRANCH_WIDTH + t, value, 0.0)
        rest = jnp.zeros((out_ref.shape[0] - CLASSES - 5, rows), jnp.float32)
        grads = jnp.concatenate([class_grad, depth_grad, normal_grad, edge_grad, rest], axis=0)
        grads = grads.astype(jnp.bfloat16)
        out_grad = dot(grads, hidden)
        sums[3:12, :BRANCH_WIDTH] += out_grad[0:9]
        sums[3:12, BRANCH_WIDTH:] += out_grad[9:18]
        back = dot(grads, out_ref[...], CONTRACT_ROWS)
        back = (back * (sigmoid * (1.0 + before * (1.0 - sigmoid)))).astype(jnp.bfloat16)
        pre_grads[place] = back
        matrix[:, :BRANCH_WIDTH] += dot(act, back, CONTRACT_ROWS)
        per_image[0:1] += jnp.sum(back.astype(jnp.float32), axis=0, keepdims=True)

    @pl.when(step == 2 * chunks)
    def _():
        line = per_image[...]
        mean = pooled[...] / area
        mean = mean.astype(jnp.bfloat16).astype(jnp.float32)
        matrix[:, BRANCH_WIDTH:] += lax.dot_general(
            mean, line, CONTRACT_ROWS, precision=PRECISE, preferred_element_type=jnp.float32
        )
        sums[2:3, :BRANCH_WIDTH] += line[0:1]
        hidden_pre[...] = lax.dot_general(
            line,
            head_ref[1].astype(jnp.float32),
            CONTRACT_COLS,
            precision=PRECISE,
            preferred_element_type=jnp.float32,
        )

    @pl.when(phase == 2)
    def _():
        centered, before = residual()
        back = dot(pre_grads[place], head_ref[0], CONTRACT_COLS) + hidden_pre[0:1] / area
        upstream = back * silu_slope(before)
        up_ref[...] = upstream
        add_sums(sums, upstream, upstream * centered)

    @pl.when((image == last) & (step == 3 * chunks - 1))
    def _():
        grad_ref[...] = matrix[...].astype(grad_ref.dtype)
        wait_peers([("dp", members)])
        sum_over_owners(members, sums, total, *exchange[1:])


def head_call(y, x, totals, gains, head, out_rows, bias, info, weights, identity):
    images, height, width, channels = x.shape
    chunks = height // CHUNK
    rows = CHUNK * width
    members = lax.axis_size("dp")

    def again(b, c):
        return jnp.where(c // chunks == 1, chunks - 1, lax.rem(c, chunks))

    def constant(*shape):
        return pl.BlockSpec(shape, lambda b, c: (0,) * len(shape))

    stream = pl.BlockSpec((1, CHUNK, width, channels), lambda b, c: (b, again(b, c), 0, 0))
    return pl.pallas_call(
        functools.partial(head_kernel, members, chunks, images),
        grid=(images, 3 * chunks),
        in_specs=[
            stream,
            stream,
            constant(8, channels),
            constant(4, channels),
            constant(*head.shape),
            constant(*out_rows.shape),
            constant(1, BRANCH_WIDTH),
            pl.BlockSpec((1, 1, 8, rows), lambda b, c: (b, lax.rem(c, chunks), 0, 0)),
            pl.BlockSpec((1, 8, 128), lambda b, c: (b, 0, 0)),
        ],
        out_specs=(
            pl.BlockSpec(
                (rows, channels), lambda b, c: (b * chunks + jnp.maximum(c - 2 * chunks, 0), 0)
            ),
            constant(channels, 2 * BRANCH_WIDTH),
            constant(16, channels),
        ),
        out_shape=(
            jax.ShapeDtypeStruct((images * height * width, channels), jnp.float32),
            jax.ShapeDtypeStruct((channels, 2 * BRANCH_WIDTH), jnp.bfloat16),
            jax.ShapeDtypeStruct((16, channels), jnp.float32),
        ),
        scratch_shapes=[
            pltpu.VMEM((chunks * rows, channels), jnp.bfloat16),
            pltpu.VMEM((8, channels), jnp.float32),
            pltpu.VMEM((chunks * rows, BRANCH_WIDTH), jnp.bfloat16),
            pltpu.VMEM((8, channels), jnp.float32),
            pltpu.VMEM((8, BRANCH_WIDTH), jnp.float32),
            pltpu.VMEM((8, BRANCH_WIDTH), jnp.float32),
            pltpu.VMEM((channels, 2 * BRANCH_WIDTH), jnp.float32),
        ]
        + sum_scratch(members, 16, channels),
        compiler_params=summing(identity),
        name="heads",
    )(y.reshape(x.shape), x, totals, gains, head, out_rows, bias, info, weights)


def adamw_update(gradient, moment_one, moment_two, weight, rate):
    moment_one = 0.5 * moment_one + 0.5 * gradient
    moment_two = 0.5 * moment_two + 0.5 * gradient * gradient
    correction = 1.0 - 0.5**STEP
    weight = weight - rate * (
        moment_one / correction / (jnp.sqrt(moment_two / correction) + ADAM_EPS)
        + WEIGHT_DECAY * weight
    )
    return (moment_one, moment_two, weight)


def body(
    features,
    labels,
    depth_mask,
    depth_target,
    normal_target,
    scene_ids,
    task_weights,
    conflict,
    trunk_copy,
    trunk_master,
    trunk_left,
    trunk_right,
    left_root,
    right_root,
    head_copy,
    head_master,
    head_first,
    head_second,
    out_copy,
    out_master,
    out_first,
    out_second,
    trunk_gains,
    gains_first,
    gains_second,
    head_bias,
    bias_first,
    bias_second,
):
    images, feature_rows, feature_columns, channels = features.shape
    pixels = jnp.array(images * feature_rows * feature_columns * lax.axis_size("dp"), jnp.float32)
    task_index = lax.axis_index("task")
    owner_index = lax.axis_index("dp")
    local_valid = jnp.sum(depth_mask.astype(jnp.float32))
    first_note = jnp.where(jnp.arange(8)[:, None] == 3, local_valid, jnp.zeros((8, channels)))
    first_conv, first_totals, second_full, head_full = first_conv_call(
        features, trunk_copy, head_copy, first_note, 0
    )
    valid_count = first_totals[3, 0]
    second_conv, first_act, second_totals = second_conv_call(
        first_conv, first_totals, trunk_gains, second_full, features.shape, 1
    )
    selector = (jnp.arange(TASKS) == task_index).astype(jnp.float32)
    own_bias = jnp.sum(selector[:, None] * head_bias, axis=0, keepdims=True)
    choose = (scene_ids[:, None] == jnp.arange(task_weights.shape[0])[None, :]).astype(jnp.float32)
    image_weights = jnp.sum(choose[:, :, None] * task_weights[None], axis=1) * selector
    image_weights = jnp.broadcast_to(
        jnp.pad(image_weights, ((0, 0), (0, 8 - TASKS)))[:, :, None], (images, 8, 128)
    )
    out_rows = jnp.pad(out_copy.T, ((0, 32 - out_copy.shape[1]), (0, 0)))
    second_up, head_grad, second_back_sums = head_call(
        second_conv,
        features,
        second_totals,
        trunk_gains,
        head_full,
        out_rows,
        own_bias,
        pixel_rows(labels, depth_mask, depth_target, normal_target),
        image_weights,
        2,
    )
    keep_ahead, send_ahead, keep_rest, send_rest, second_edges, second_back = weight_grad_call(
        first_act,
        second_up,
        second_conv,
        second_totals,
        trunk_gains,
        second_back_sums,
        head_grad,
        6,
    )
    second_back, send_ahead = lax.optimization_barrier((second_back, send_ahead))
    members = lax.axis_size("dp")
    got_ahead = lax.ppermute(send_ahead, "dp", [(i, i ^ 1) for i in range(members)])
    first_up, first_back_sums = act_grad_call(
        second_back, first_conv, first_totals, trunk_gains, second_full, second_edges, 3
    )
    divisor = jnp.stack([pixels, valid_count, pixels, pixels])
    own_divisor = jnp.sum(divisor * selector)
    combined, pairs, notes, head_total = reduce_call(
        features,
        first_up,
        first_conv,
        first_totals,
        trunk_gains,
        first_back_sums,
        second_totals,
        second_back_sums,
        jnp.broadcast_to(
            conflict.astype(jnp.float32).reshape(TASKS * TASKS, 1), (TASKS * TASKS, 128)
        ),
        [keep_ahead, got_ahead],
        [keep_rest, send_rest],
        7,
    )
    pair_products = pairs[:, 0].reshape(TASKS, TASKS)
    gains_total = jnp.sum(notes[:, 0:4] / divisor[:, None, None], axis=0)
    bias_total = notes[:, 4, :BRANCH_WIDTH] / divisor[:, None]
    loss_sum = jnp.sum(notes[:, 4, BRANCH_WIDTH : BRANCH_WIDTH + TASKS], axis=0)
    column_divisor = jnp.concatenate(
        [jnp.full((CLASSES,), divisor[0]), divisor[1:2], jnp.full((3,), divisor[2]), divisor[3:4]]
    )
    out_total = (
        jnp.concatenate(jnp.split(jnp.sum(notes[:, 5:14], axis=0), 2, axis=1)).T
        / column_divisor[None, :]
    )
    head_rows = jnp.stack(jnp.split(head_total, 2, axis=1))[None]
    grad_rows, left_new, right_new, master_new, copy_new = update_call(
        owner_index, combined, trunk_left, trunk_right, trunk_master, left_root, right_root
    )
    head_one, head_two, head_new = adamw_update(
        head_rows / own_divisor, head_first, head_second, head_master, RATE_MATRIX
    )
    out_one, out_two, out_new = adamw_update(
        out_total, out_first, out_second, out_master, RATE_MATRIX
    )
    gain_one, gain_two, gain_new = adamw_update(
        gains_total, gains_first, gains_second, trunk_gains, RATE_VECTOR
    )
    bias_one, bias_two, bias_new = adamw_update(
        bias_total, bias_first, bias_second, head_bias, RATE_VECTOR
    )
    loss_terms = jnp.concatenate([loss_sum, valid_count[None]])
    return (
        grad_rows,
        left_new,
        right_new,
        master_new,
        copy_new,
        head_one,
        head_two,
        head_new,
        head_new.astype(jnp.bfloat16),
        out_one,
        out_two,
        out_new,
        out_new.astype(jnp.bfloat16),
        gain_one,
        gain_two,
        gain_new,
        bias_one,
        bias_two,
        bias_new,
        loss_terms,
        pair_products,
    )


def solution(mesh):
    rows = P(None, None, "dp", None)
    heads = P("task", None, "dp", None)
    images = P("dp")
    placed = (
        (images,) * 6
        + (P(), P())
        + (rows,) * 5
        + (P(),)
        + (heads,) * 4
        + (P(),) * 10
    )
    return jax.shard_map(
        body,
        mesh=mesh,
        in_specs=placed,
        out_specs=(rows,) * 5 + (heads,) * 4 + (P(),) * 12,
        check_vma=False,
    )
```
